128 devices in a mesh: ctx: 8 (over z_lo, x), exp: 16 (over z_hi, y, core).
Axes of the slice: x: 4, y: 4, z: 4 (z_hi: 2, z_lo: 2; z = z_hi * 2 + z_lo), core: 2. Of those that a mesh axis runs over, the one named last changes fastest.
Arguments:
- tokens: bfloat16 [16, 1024, 1024], P('exp', 'ctx'), may hold values from -6 to 6
- cotangent: bfloat16 [16, 1024, 1024], P('exp', 'ctx'), may hold values from -6 to 6
- span_order: int32 [16], replicated, may hold values from 0 to 15, each once
- expert_choice: int32 [16, 1024, 8], P('exp', 'ctx'), may hold values from 0 to 31, all different within a row; in each aligned block of 128 rows (0 to 127, 128 to 255, ..., all dimensions but the last counted through in order) at most 48 rows name the same one
- norm_attn: bfloat16 [1024], P('exp'), may hold values from 0.5 to 1.5
- w_query: bfloat16 [1024, 1024], P('exp'), may hold values from -0.1875 to 0.1875
- key_matrix: bfloat16 [1024, 512], P('exp'), may hold values from -0.1875 to 0.1875
- value_matrix: bfloat16 [1024, 512], P('exp'), may hold values from -0.1875 to 0.1875
- w_out: bfloat16 [1024, 1024], P('exp'), may hold values from -1.5 to 1.5
- norm_moe: bfloat16 [1024], P('exp'), may hold values from 0.5 to 1.5
- w_router: bfloat16 [1024, 32], P('exp'), may hold values from -0.09375 to 0.09375
- w_gate: bfloat16 [32, 1024, 512], P('exp', 'ctx'), may hold values from -0.1875 to 0.1875
- w_up: bfloat16 [32, 1024, 512], P('exp', 'ctx'), may hold values from -0.1875 to 0.1875
- w_down: bfloat16 [32, 512, 1024], P('exp', 'ctx'), may hold values from -1 to 1
Outputs:
- out: bfloat16 [16, 1024, 1024], P('exp', 'ctx')
- grad_tokens: float32 [16, 1024, 1024], P('exp', 'ctx')
- grad_norm_attn: float32 [1024], P('exp')
- grad_w_query: float32 [1024, 1024], P('exp')
- grad_w_key: float32 [1024, 512], P('exp')
- grad_w_value: float32 [1024, 512], P('exp')
- grad_w_out: float32 [1024, 1024], P('exp')
- grad_norm_moe: float32 [1024], P('exp')
- grad_w_router: float32 [1024, 32], P('exp')
- grad_w_gate: float32 [32, 1024, 512], P('exp', 'ctx')
- grad_w_up: float32 [32, 1024, 512], P('exp', 'ctx')
- grad_w_down: float32 [32, 512, 1024], P('exp', 'ctx')
The draws below stay inside these ranges and needn't reach their ends.
Inputs may be any that keep to these rules, and one draw needn't show every extreme that they name: Index i of ctx holds spans span_order[2 i] and span_order[2 i + 1] of each sequence, in this order; each span number appears once. `expert_choice`: A token's 8 experts differ. Among the choices of the 128 tokens of one device no expert appears more than 48 times, and in every draw some expert appears exactly 48 times among the tokens of some device.
All inputs are finite; a program needn't handle non-finite values.
Results may differ from the reference program's by a relative error of at most 0.025.
Values may be sent and summed in bfloat16 or wider, within the bound.
A program may use at most 128 MiB of HBM per device.

```python
import math
import jax
import jax.numpy as jnp
import numpy as np
from jax import lax

MODEL_WIDTH = 1024
QUERY_HEADS = 16
KEY_VALUE_HEADS = 8
HEAD_SIZE = 64
F = 512
TOP = 8
SEQUENCE_TOKENS = 1024
SEQS = 16
TOK_DEV = 128
SPAN = 64
EXPERTS = 32
CAP = 48
N_CTX = 8


def steps_of(key, shape, split, least, high):
    loudness = 1.0
    for position, blocks in split:
        draws = jax.random.uniform(jax.random.fold_in(jax.random.fold_in(key, 6), position), (blocks,), jnp.float32, least / len(split), high / len(split))
        loudness = loudness * jnp.repeat(jnp.exp(draws), shape[position] // blocks).reshape((-1,) + (1,) * (len(shape) - 1 - position))
    return loudness


def routed_block(key, own, number, rows, count, top, bound, slope):
    order = jax.random.permutation(key, count)
    crowded, common = portions_of(count, rows * top, bound, slope, True), portions_of(count, rows * top, bound, slope, False)
    places = jnp.arange(count)

    def named(lengths, turn):
        used = int((lengths > 0).sum())
        fixed = max(1, used // 4)
        moved = fixed + (places - fixed + turn * (used - fixed)) % max(1, count - fixed)
        return jnp.zeros((count,), jnp.int32).at[order[jnp.where(places < fixed, places, moved)]].set(jnp.asarray(lengths, jnp.int32))

    lengths = jnp.where(number % 4 == 0, named(crowded, number // 4), named(common, number - number // 4 - 1))
    mixed = jax.random.permutation(jax.random.fold_in(own, 3), count)
    source_of, sink = mixed[0:count // 2 * 2:2], mixed[1:count // 2 * 2:2]
    slack = jnp.minimum(lengths[source_of] - 1, bound - lengths[sink]) // 2
    slack = jnp.where((source_of == order[0]) | (sink == order[0]) | (lengths[sink] == 0), 0, jnp.maximum(slack, 0))
    moved = jax.random.randint(jax.random.fold_in(own, 4), (count // 2,), 0, 1 << 20) % (slack + 1)
    lengths = lengths.at[source_of].add(-moved).at[sink].add(moved)
    members = jnp.searchsorted(jnp.cumsum(lengths), jnp.arange(rows * top), side="right").astype(jnp.int32)
    table = members.reshape(top, rows).T
    table = table[jax.random.permutation(jax.random.fold_in(own, 1), rows)]
    turn = jax.random.randint(jax.random.fold_in(own, 2), (rows, 1), 0, top)
    return jnp.take_along_axis(table, (jnp.arange(top)[None, :] + turn) % top, axis=1)


def portions_of(number_of, total, bound, slope, full):
    portions = [(1 << 20) // math.isqrt(standing ** slope) + 1 for standing in range(1, number_of + 1)]
    largest = bound if full else min(bound, max(-(-total // number_of), total * portions[0] // sum(portions)))
    least = 1 if total - largest >= number_of - 1 else 0
    counts, rest = [largest] + [least] * (number_of - 1), total - largest - least * (number_of - 1)
    while rest > 0:
        free = [i for i in range(1, number_of) if counts[i] < largest] or [i for i in range(1, number_of) if counts[i] < bound]
        whole, budget = sum([portions[i] for i in free]), rest
        for i in free:
            addition = min(bound - counts[i], max(1, budget * portions[i] // whole), rest)
            counts[i] = counts[i] + addition
            rest = rest - addition
    return np.array(counts)


def scatter_about(stream_key, dims, width, limit, shards=(), kind=jnp.bfloat16):
    array = width * jax.random.normal(stream_key, dims, jnp.float32)
    if shards:
        array = array * steps_of(stream_key, dims, shards, -0.22, 0.18)
    return jnp.clip(array, -limit, limit).astype(kind)


def setup_inputs(seed: int = 0) -> dict:
    splits = jax.random.split(jax.random.key(seed), 15)
    tokens = scatter_about(splits[0], (SEQS, SEQUENCE_TOKENS, MODEL_WIDTH), 1.0, 6.0, ((0, 16), (1, 8)))
    cotangent = scatter_about(splits[1], (SEQS, SEQUENCE_TOKENS, MODEL_WIDTH), 1.0, 6.0, ((0, 16), (1, 8)))
    span_order = jax.random.permutation(splits[2], 2 * N_CTX).astype(jnp.int32)
    expert_choice_keys = jax.random.split(jax.random.fold_in(splits[3], 1), SEQS * SEQUENCE_TOKENS // TOK_DEV)
    expert_choice_turns = jax.random.permutation(jax.random.fold_in(splits[3], 3), SEQS * SEQUENCE_TOKENS // TOK_DEV)
    expert_choice = jax.vmap(lambda own, number: routed_block(jax.random.fold_in(splits[3], 2), own, number, TOK_DEV, EXPERTS, TOP, CAP, 1))(expert_choice_keys, expert_choice_turns).reshape((SEQS, SEQUENCE_TOKENS, TOP))
    norm_attn = jnp.clip(1.0 + 0.1 * jax.random.normal(splits[4], (MODEL_WIDTH,), jnp.float32), 0.5, 1.5).astype(jnp.bfloat16)
    w_query = scatter_about(splits[5], (MODEL_WIDTH, QUERY_HEADS * HEAD_SIZE), MODEL_WIDTH ** -0.5, 0.1875, ((0, 16),))
    key_matrix = scatter_about(splits[6], (MODEL_WIDTH, KEY_VALUE_HEADS * HEAD_SIZE), MODEL_WIDTH ** -0.5, 0.1875, ((0, 16),))
    value_matrix = scatter_about(splits[7], (MODEL_WIDTH, KEY_VALUE_HEADS * HEAD_SIZE), MODEL_WIDTH ** -0.5, 0.1875, ((0, 16),))
    w_out = scatter_about(splits[8], (QUERY_HEADS * HEAD_SIZE, MODEL_WIDTH), (QUERY_HEADS * HEAD_SIZE // 64) ** -0.5, 1.5, ((0, 16),))
    norm_moe = jnp.clip(1.0 + 0.1 * jax.random.normal(splits[9], (MODEL_WIDTH,), jnp.float32), 0.5, 1.5).astype(jnp.bfloat16)
    w_router = scatter_about(splits[10], (MODEL_WIDTH, EXPERTS), (4 * MODEL_WIDTH) ** -0.5, 0.09375, ((0, 16),))
    w_gate = scatter_about(splits[11], (EXPERTS, MODEL_WIDTH, F), MODEL_WIDTH ** -0.5, 0.1875, ((0, 16), (1, 8)))
    w_up = scatter_about(splits[12], (EXPERTS, MODEL_WIDTH, F), MODEL_WIDTH ** -0.5, 0.1875, ((0, 16), (1, 8)))
    w_down = scatter_about(splits[13], (EXPERTS, F, MODEL_WIDTH), (F // 16) ** -0.5, 1.0, ((0, 16), (1, 8)))
    return dict(tokens=tokens, cotangent=cotangent, span_order=span_order, expert_choice=expert_choice, norm_attn=norm_attn, w_query=w_query, key_matrix=key_matrix, value_matrix=value_matrix, w_out=w_out, norm_moe=norm_moe, w_router=w_router, w_gate=w_gate, w_up=w_up, w_down=w_down)


@jax.custom_vjp
def reduced_precision(v):
    return lax.optimization_barrier(v.astype(jnp.bfloat16)).astype(jnp.float32)

@jax.custom_vjp
def low_back(v):
    return v

def low_keep(v):
    return (reduced_precision(v), None)

def low_pass(kept, grad):
    return (grad,)

def back_keep(v):
    return (v, None)

def back_low(kept, grad):
    return (reduced_precision(grad),)
reduced_precision.defvjp(low_keep, low_pass)
low_back.defvjp(back_keep, back_low)
eps_norm = 1e-06
rope_base = 10000.0
neg_big = -1e+30
precise = lax.Precision.HIGHEST

def normalize(values, gain):
    factor = lax.rsqrt(lax.optimization_barrier(jnp.mean(values * values, axis=-1, keepdims=True)) + eps_norm)
    return values * factor * gain

def softmax_rows(values):
    largest = lax.optimization_barrier(jnp.max(values, axis=-1, keepdims=True))
    shifted = jnp.exp(values - largest)
    return shifted / lax.optimization_barrier(jnp.sum(shifted, axis=-1, keepdims=True))

def angles(places):
    freqs = rope_base ** (-(jnp.arange(HEAD_SIZE // 2, dtype=jnp.float32) * 2.0 / HEAD_SIZE))
    turned = places.astype(jnp.float32)[:, None] * freqs[None, :]
    return (jnp.cos(turned)[:, None, :], jnp.sin(turned)[:, None, :])

def apply_rotary(values, cosine_table, sine_table, heads, direction):
    count_of_rows = values.shape[0]
    by_head = values.reshape(count_of_rows, heads, HEAD_SIZE)
    leading = by_head[:, :, :HEAD_SIZE // 2]
    trailing = by_head[:, :, HEAD_SIZE // 2:]
    turned = jnp.concatenate([leading * cosine_table - direction * trailing * sine_table, trailing * cosine_table + direction * leading * sine_table], axis=2)
    return turned.reshape(count_of_rows, heads * HEAD_SIZE)

def attention(rotated_queries, rotated_keys, value_reduced, places):
    rows_per_block = min(SEQUENCE_TOKENS, 512)
    heads_of_keys = rotated_keys.reshape(SEQUENCE_TOKENS, KEY_VALUE_HEADS, HEAD_SIZE)
    heads_of_values = value_reduced.reshape(SEQUENCE_TOKENS, KEY_VALUE_HEADS, HEAD_SIZE)

    def per_block(element):
        block_of_queries, place_block = element
        query_rows = block_of_queries.reshape(rows_per_block, KEY_VALUE_HEADS, QUERY_HEADS // KEY_VALUE_HEADS, HEAD_SIZE)
        raw_scores = jnp.einsum('bkgh,jkh->kgbj', query_rows, heads_of_keys, precision=precise)
        scaled = low_back(raw_scores * HEAD_SIZE ** (-0.5))
        visible = places[None, :] <= place_block[:, None]
        probs = softmax_rows(jnp.where(visible, scaled, neg_big))
        mixed = jnp.einsum('kgbj,jkh->bkgh', reduced_precision(probs), heads_of_values, precision=precise)
        return mixed.reshape(rows_per_block, QUERY_HEADS * HEAD_SIZE)
    results = lax.map(jax.checkpoint(per_block), (rotated_queries.reshape(SEQUENCE_TOKENS // rows_per_block, rows_per_block, QUERY_HEADS * HEAD_SIZE), places.reshape(SEQUENCE_TOKENS // rows_per_block, rows_per_block)))
    return results.reshape(SEQUENCE_TOKENS, QUERY_HEADS * HEAD_SIZE)

def experts(expanded, flat_choice, w_gate, w_up, w_down):
    row_ids = jnp.arange(SEQUENCE_TOKENS * TOP, dtype=jnp.int32)
    most_rows = N_CTX * CAP

    def per_expert(element):
        number, gate_weight, up_weight, down_weight = element
        sort_keys = jnp.where(flat_choice == number, 0, 1).astype(jnp.int32) * (SEQUENCE_TOKENS * TOP) + row_ids
        picked = jnp.argsort(sort_keys)[:most_rows].astype(jnp.int32)
        valid = (flat_choice[picked] == number).astype(jnp.float32)[:, None]
        inputs = expanded[picked] * valid
        gate_h = low_back(jnp.dot(inputs, gate_weight, precision=precise))
        up_h = low_back(jnp.dot(inputs, up_weight, precision=precise))
        hidden = reduced_precision(jax.nn.silu(gate_h) * up_h)
        produced = low_back(reduced_precision(jnp.dot(hidden, down_weight, precision=precise)))
        return (produced * valid, picked)
    produced, picked = lax.map(per_expert, (jnp.arange(EXPERTS, dtype=jnp.int32), w_gate, w_up, w_down))
    return jnp.zeros((SEQUENCE_TOKENS * TOP, MODEL_WIDTH), jnp.float32).at[picked.reshape(-1)].add(produced.reshape(-1, MODEL_WIDTH))

def layer(inputs, choice_rows, places, weights):
    norm_attn, w_query, key_matrix, value_matrix, w_out, norm_moe, w_router, w_gate, w_up, w_down = weights
    h_one = reduced_precision(normalize(inputs, norm_attn))
    query = low_back(jnp.dot(h_one, w_query, precision=precise))
    key_unrotated = low_back(jnp.dot(h_one, key_matrix, precision=precise))
    value_pre = low_back(jnp.dot(h_one, value_matrix, precision=precise))
    cosine_table, sine_table = angles(places)
    rotated_queries = reduced_precision(apply_rotary(query, cosine_table, sine_table, QUERY_HEADS, 1.0))
    rotated_keys = reduced_precision(apply_rotary(key_unrotated, cosine_table, sine_table, KEY_VALUE_HEADS, 1.0))
    value_reduced = reduced_precision(value_pre)
    attn_low = low_back(reduced_precision(attention(rotated_queries, rotated_keys, value_reduced, places)))
    x_mid = inputs + low_back(jnp.dot(attn_low, w_out, precision=precise))
    routed_in = reduced_precision(normalize(x_mid, norm_moe))
    logits = low_back(jnp.dot(routed_in, w_router, precision=precise))
    onehot = (choice_rows[:, :, None] == jnp.arange(EXPERTS, dtype=jnp.int32)[None, None, :]).astype(jnp.float32)
    chosen = lax.optimization_barrier(jnp.sum(onehot * logits[:, None, :], axis=-1))
    gates = softmax_rows(chosen)
    expanded = low_back(jnp.broadcast_to(routed_in[:, None, :], (SEQUENCE_TOKENS, TOP, MODEL_WIDTH))).reshape(SEQUENCE_TOKENS * TOP, MODEL_WIDTH)
    produced = experts(expanded, choice_rows.reshape(-1), w_gate, w_up, w_down).reshape(SEQUENCE_TOKENS, TOP, MODEL_WIDTH)
    return x_mid + lax.optimization_barrier(jnp.sum(gates[:, :, None] * produced, axis=1))

def reference(tokens, cotangent, span_order, expert_choice, norm_attn, w_query, key_matrix, value_matrix, w_out, norm_moe, w_router, w_gate, w_up, w_down):
    row_ids = jnp.arange(SEQUENCE_TOKENS, dtype=jnp.int32)
    places = (span_order[row_ids // SPAN] * SPAN + row_ids % SPAN).astype(jnp.int32)
    weights = tuple((w.astype(jnp.float32) for w in (norm_attn, w_query, key_matrix, value_matrix, w_out, norm_moe, w_router, w_gate, w_up, w_down)))

    def forward(inputs, params):

        def advance(carried, element):
            return (carried, jax.checkpoint(layer)(element[0], element[1], places, params))
        return lax.scan(advance, jnp.zeros((), jnp.float32), (inputs, expert_choice))[1]
    outputs, pullback = jax.vjp(forward, tokens.astype(jnp.float32), weights)
    grad_inputs, grad_weights = pullback(cotangent.astype(jnp.float32))
    return (outputs.astype(jnp.bfloat16), grad_inputs, grad_weights[0], grad_weights[1], grad_weights[2], grad_weights[3], grad_weights[4], grad_weights[5], grad_weights[6], grad_weights[7], grad_weights[8], grad_weights[9])
```

```python
import jax
import jax.numpy as jnp
from jax import lax
from jax.experimental import pallas as pl
from jax.experimental.pallas import tpu as pltpu
from jax.sharding import PartitionSpec as P

HEAD_SIZE = 64
HALF = 32
N_CTX = 8
N_EXP = 16
eps_norm = 1e-06
rope_base = 10000.0
neg_big = -1e30
f32, bf16 = jnp.float32, jnp.bfloat16

MESH = pl.DeviceIdType.MESH
ANY = pl.BlockSpec(memory_space=pl.ANY)
VMEM = pl.BlockSpec(memory_space=pltpu.VMEM)
DMA = pltpu.SemaphoreType.DMA
NEAR_LAST = (6, 2, 4, 5, 3, 1, 7)
NEAR_FIRST = (1, 7, 3, 5, 4, 2, 6)
CTX_ORDER = (2, 6, 4, 1, 3, 5, 7)


def remote(src, dst, send, recv, where):
    return pltpu.make_async_remote_copy(
        src_ref=src, dst_ref=dst, send_sem=send, recv_sem=recv, device_id=where, device_id_type=MESH
    )


def greet(places, amount=None):
    barrier = pltpu.get_barrier_semaphore()
    for where in places:
        pl.semaphore_signal(barrier, inc=1, device_id=where, device_id_type=MESH)
    pl.semaphore_wait(barrier, len(places) if amount is None else amount)


class Here:
    def __init__(self):
        self.c = lax.axis_index("ctx")
        self.e = lax.axis_index("exp")
        self.core = lax.rem(self.e, 2)
        self.chip = self.e // 2
        self.partner = {"exp": self.e + 1 - 2 * self.core}

    def ctx(self, k):
        return lax.rem(self.c + k, N_CTX)

    def chip_at(self, k):
        return lax.rem(self.chip + k, 8)

    def ctx_peers(self):
        return [{"ctx": self.ctx(k)} for k in range(1, N_CTX)]

    def same_core(self, k):
        return {"exp": 2 * self.chip_at(k) + self.core}

    def exp_peers(self):
        return [self.partner] + [self.same_core(k) for k in range(1, 8)]

    def other_core_peers(self):
        return [{"exp": 2 * self.chip_at(k) + 1 - self.core} for k in range(1, 8)]


class Gather:
    sems = (8, 8)

    def __init__(self, here, x, out, send, recv):
        self.copies = [pltpu.make_async_copy(x, out.at[here.c], send.at[0])]
        for k in CTX_ORDER:
            self.copies.append(remote(x, out.at[here.c], send.at[k], recv.at[k], {"ctx": here.ctx(k)}))

    def start(self):
        for c in self.copies:
            c.start()

    def wait(self):
        for c in self.copies:
            c.wait()


class Turn:
    sems = (8, 8)

    def __init__(self, here, x, out, send, recv):
        rows, cols = out.shape[0], x.shape[1]
        into = out.at[:, pl.ds(pl.multiple_of(here.c * cols, cols), cols)]

        def part(j):
            return x.at[pl.ds(pl.multiple_of(j * rows, rows), rows)]

        self.copies = [pltpu.make_async_copy(part(here.c), into, send.at[0])]
        for k in CTX_ORDER:
            j = here.ctx(k)
            self.copies.append(remote(part(j), into, send.at[k], recv.at[k], {"ctx": j}))

    start = Gather.start
    wait = Gather.wait


class PairGather:
    sems = (8, 8, 8, 8)

    def __init__(self, here, x, out, send, recv, fsend, frecv):
        e = here.e
        self.own = pltpu.make_async_copy(x, out.at[e], fsend.at[0])
        self.first = remote(x, out.at[e], send.at[0], recv.at[0], here.partner)
        self.far, self.forward = {}, {}
        for k in NEAR_LAST:
            self.far[k] = remote(x, out.at[e], send.at[k], recv.at[k], here.same_core(k))
            slot = 2 * here.chip_at(8 - k) + here.core
            self.forward[k] = remote(out.at[slot], out.at[slot], fsend.at[k], frecv.at[k], here.partner)

    def start(self):
        for k in NEAR_LAST:
            self.far[k].start()
        self.first.start()
        self.own.start()

    def pass_on(self):
        for k in NEAR_FIRST:
            self.far[k].wait_recv()
            self.forward[k].start()

    def wait(self):
        self.own.wait()
        self.first.wait()
        for k in NEAR_FIRST:
            self.far[k].wait_send()
            self.forward[k].wait()


class PairScatter:
    sems = (8, 8, 8, 8, 8)

    @staticmethod
    def scratch(x):
        return [pltpu.VMEM((8,) + x.shape[1:], x.dtype)] * 4

    def __init__(self, here, x, total, mine, near, summed, far, load, nsend, nrecv, fsend, frecv):
        self.total, self.mine, self.near, self.summed, self.far = total, mine, near, summed, far
        self.loads, self.nears, self.fars = {}, {}, {}
        self.order = NEAR_LAST + (0,)
        for k in self.order:
            there = here.chip_at(k)
            self.nears[k] = remote(x.at[2 * there + 1 - here.core], near.at[k], nsend.at[k], nrecv.at[k], here.partner)
            self.loads[k] = pltpu.make_async_copy(x.at[2 * there + here.core], mine.at[k], load.at[k])
            if k:
                self.fars[k] = remote(summed.at[k], far.at[k], fsend.at[k], frecv.at[k], here.same_core(k))

    def start(self):
        for k in self.order:
            self.nears[k].start()
            self.loads[k].start()

    def pass_on(self):
        for k in self.order:
            self.loads[k].wait()
            self.nears[k].wait_recv()
            both = self.mine[k].astype(f32) + self.near[k].astype(f32)
            if k:
                self.summed[k] = both.astype(self.summed.dtype)
                self.fars[k].start()
            else:
                self.total[...] = both

    def wait(self):
        for k in NEAR_FIRST:
            self.fars[k].wait_recv()
            self.total[...] += self.far[k].astype(f32)
        for k in self.order:
            self.nears[k].wait_send()
            if k:
                self.fars[k].wait_send()


class Spread:
    sems = (16, 16)

    def __init__(self, here, x, out, send, recv):
        self.copies = [pltpu.make_async_copy(x.at[here.e], out.at[here.e], send.at[0])]
        for k in range(1, N_EXP):
            j = lax.rem(here.e + k, N_EXP)
            self.copies.append(remote(x.at[j], out.at[here.e], send.at[k], recv.at[k], {"exp": j}))

    start = Gather.start
    wait = Gather.wait


def sem_shapes(*kinds):
    return [DMA((n,)) for kind in kinds for n in kind.sems]


def params(cid):
    return pltpu.CompilerParams(collective_id=cid, has_side_effects=True, vmem_limit_bytes=40 * 2**20)


def call(kernel, outs, scratch, cid, *args, out_specs=None):
    return pl.pallas_call(
        kernel,
        out_shape=outs,
        in_specs=[ANY] * len(args),
        out_specs=out_specs or [ANY] * len(outs),
        scratch_shapes=scratch,
        compiler_params=params(cid),
    )(*args)


def shape(s, t):
    return jax.ShapeDtypeStruct(s, t)


def start_exchange(tokens, pack, wo, cot):
    def kernel(x, p, w, u, xs, ps, ws, us, *sems):
        here = Here()
        greet(here.ctx_peers() + here.exp_peers())
        a = Gather(here, x, xs, *sems[0:2])
        g = [PairGather(here, i, o, *sems[2 + 4 * n : 6 + 4 * n]) for n, (i, o) in enumerate(((p, ps), (w, ws), (u, us)))]
        a.start()
        for i in g:
            i.start()
        for i in g:
            i.pass_on()
        a.wait()
        for i in g:
            i.wait()

    return call(
        kernel,
        [shape((8,) + tokens.shape, bf16)] + [shape((16,) + a.shape, bf16) for a in (pack, wo, cot)],
        sem_shapes(Gather, PairGather, PairGather, PairGather),
        1,
        tokens,
        pack,
        wo,
        cot,
    )


def turn_exchange(attn):
    def kernel(x, out, *sems):
        here = Here()
        greet(here.ctx_peers())
        t = Turn(here, x, out, *sems)
        t.start()
        t.wait()

    return call(kernel, [shape((attn.shape[0] // 8, attn.shape[1] * 8), attn.dtype)], sem_shapes(Turn), 2, attn)[0]


def routed_exchange(routed, gates):
    def kernel(x, g, xs, gs, *sems):
        here = Here()
        greet(here.exp_peers())
        items = [PairGather(here, g, gs, *sems[4:8]), PairGather(here, x, xs, *sems[0:4])]
        for i in items:
            i.start()
        for i in items:
            i.pass_on()
        for i in items:
            i.wait()

    return call(
        kernel,
        [shape((16,) + a.shape, a.dtype) for a in (routed, gates)],
        sem_shapes(PairGather, PairGather),
        3,
        routed,
        gates,
    )


def grad_exchange(parts, gate_parts):
    def kernel(x, g, total, gs, *rest):
        here = Here()
        greet(here.exp_peers() + here.other_core_peers())
        sems = rest[4:]
        small = Spread(here, g, gs, *sems[5:7])
        s = PairScatter(here, x, total, *rest[:4], *sems[0:5])
        s.start()
        small.start()
        s.pass_on()
        s.wait()
        small.wait()

    return call(
        kernel,
        [shape(parts.shape[1:], f32), shape(gate_parts.shape, f32)],
        PairScatter.scratch(parts) + sem_shapes(PairScatter, Spread),
        4,
        parts,
        gate_parts,
        out_specs=[VMEM, ANY],
    )


def branch_exchange(branch, out_parts):
    def kernel(b, x, bs, total, *rest):
        here = Here()
        greet(here.ctx_peers() + here.exp_peers())
        sems = rest[4:]
        a = Gather(here, b, bs, *sems[5:7])
        s = PairScatter(here, x, total, *rest[:4], *sems[0:5])
        a.start()
        s.start()
        s.pass_on()
        s.wait()
        a.wait()

    return call(
        kernel,
        [shape((8,) + branch.shape, bf16), shape(out_parts.shape[1:], f32)],
        PairScatter.scratch(out_parts) + sem_shapes(PairScatter, Gather),
        5,
        branch,
        out_parts,
        out_specs=[ANY, VMEM],
    )


def last_exchange(grads, shares):
    def kernel(g, x, back, alls, wos, total, low, *rest):
        here = Here()
        greet(here.ctx_peers() + here.exp_peers())
        sems = rest[4:]
        turn = Turn(here, g, back, *sems[5:7])
        s = PairScatter(here, x, total, *rest[:4], *sems[0:5])
        spread = Gather(here, low, alls, *sems[7:9])
        wsend, wrecv = sems[9:11]
        chunk = pl.ds(256, 128)
        moves = [pltpu.make_async_copy(alls.at[here.chip, :, chunk], wos.at[here.chip], wsend.at[0])]
        for k in NEAR_LAST:
            moves.append(
                remote(alls.at[here.chip_at(k), :, chunk], wos.at[here.chip], wsend.at[k], wrecv.at[k], here.same_core(k))
            )
        s.start()
        turn.start()
        s.pass_on()
        s.wait()
        low[...] = total[...].astype(bf16)
        spread.start()
        spread.wait()
        for m in moves:
            m.start()
        for m in moves:
            m.wait()
        turn.wait()

    rows, cols = shares.shape[1:]
    return call(
        kernel,
        [
            shape((grads.shape[0] // 8, grads.shape[1] * 8), bf16),
            shape((8, rows, cols), bf16),
            shape((8, rows, 128), bf16),
        ],
        [pltpu.VMEM((rows, cols), f32), pltpu.VMEM((rows, cols), bf16)]
        + PairScatter.scratch(shares)
        + sem_shapes(PairScatter, Turn, Gather, Gather),
        6,
        grads,
        shares,
    )


def dot(a, b, dims=((1,), (0,))):
    return lax.dot_general(a, b, (dims, ((), ())), preferred_element_type=f32)


NT = ((1,), (1,))
TN = ((0,), (0,))


def swap_halves(x):
    parts = []
    for i in range(0, x.shape[1], HEAD_SIZE):
        parts += [-x[:, i + HALF : i + HEAD_SIZE], x[:, i : i + HALF]]
    return jnp.concatenate(parts, axis=1)


def unswap_halves(x):
    return -swap_halves(x)


def factor_of(values):
    return lax.rsqrt(jnp.mean(values * values, axis=-1, keepdims=True) + eps_norm)


def normalize_back(values, factor, gain, upstream):
    scaled = upstream * gain
    inner = jnp.mean(scaled * values, axis=-1, keepdims=True)
    return factor * scaled - values * factor * factor * factor * inner


def body(
    tokens, cotangent, span_order, expert_choice, norm_attn, w_query, key_matrix, value_matrix,
    w_out, norm_moe, w_router, w_gate, w_up, w_down,
):
    c = lax.axis_index("ctx")
    tokens, cotangent, choice = tokens[0], cotangent[0], expert_choice[0]
    rows, width = tokens.shape
    own_rows = w_query.shape[0]
    wgu_own = jnp.concatenate([w_gate[0], w_gate[1], w_up[0], w_up[1]], axis=1)
    wgu = lax.all_gather(wgu_own, "ctx", axis=0, tiled=True)
    wd_own = jnp.concatenate([w_down[0], w_down[1]], axis=1)
    wd_wide = lax.all_gather(wd_own, "ctx", axis=0, tiled=True)
    wd = jnp.concatenate([wd_wide[:, :width], wd_wide[:, width:]], axis=0)
    wqkv_own = jnp.concatenate(
        [
            w_query.reshape(own_rows, N_CTX, 128),
            key_matrix.reshape(own_rows, N_CTX, 64),
            value_matrix.reshape(own_rows, N_CTX, 64),
        ],
        axis=2,
    ).reshape(own_rows, N_CTX * 256)
    wqkv = lax.all_gather(wqkv_own, "exp", axis=0, tiled=True)
    own_cols = lax.dynamic_slice_in_dim(wqkv_own, c * 256, 256, axis=1)
    pack = jnp.concatenate(
        [
            own_cols,
            swap_halves(own_cols[:, :192]),
            w_router,
            norm_attn[:, None],
            norm_moe[:, None],
            jnp.zeros((own_rows, 512 - 448 - 34), bf16),
        ],
        axis=1,
    )
    x_all, pack_all, wo, up_all = start_exchange(tokens, pack, w_out, cotangent)
    pack_all = pack_all.reshape(width, 512)
    wo = wo.reshape(width, width)
    up_all = up_all.reshape(N_EXP * rows, width)
    gain_a = pack_all[:, 480].astype(f32)[None, :]
    gain_m = pack_all[:, 481].astype(f32)[None, :]
    wr = pack_all[:, 448:480]
    count = N_CTX * rows
    span_len = rows // 2
    ids = jnp.arange(count, dtype=jnp.int32)
    table = ids[:, None] // span_len == jnp.arange(2 * N_CTX, dtype=jnp.int32)[None, :]
    places = jnp.sum(jnp.where(table, span_order[None, :], 0), axis=1) * span_len + ids % span_len
    freqs = rope_base ** (-(jnp.arange(HALF, dtype=f32) * 2.0 / HEAD_SIZE))
    turned = places.astype(f32)[:, None] * freqs[None, :]
    cosine = jnp.tile(jnp.cos(turned), (1, 6))
    sine = jnp.tile(jnp.sin(turned), (1, 6))
    x_seq = x_all.reshape(count, width).astype(f32)
    h_all = (x_seq * factor_of(x_seq) * gain_a).astype(bf16)
    projected = dot(h_all, pack_all[:, :448])
    qk = (projected[:, :192] * cosine + projected[:, 256:448] * sine).astype(bf16)
    v = projected[:, 192:256].astype(bf16)
    q = qk[:, :128].reshape(count, 2, HEAD_SIZE)
    k = qk[:, 128:]
    visible = places[None, :] <= places[:, None]
    scores = jnp.einsum("qhd,kd->hqk", q, k, preferred_element_type=f32) * HEAD_SIZE ** (-0.5)
    scores = jnp.where(visible[None], scores, neg_big)
    largest = jnp.max(scores, axis=-1, keepdims=True)
    shifted = jnp.exp(scores - largest)
    probs = shifted / jnp.sum(shifted, axis=-1, keepdims=True)
    probs_low = probs.astype(bf16)
    attn = jnp.einsum("hqk,kd->qhd", probs_low, v, preferred_element_type=f32)
    attn = attn.reshape(count, 128).astype(bf16)
    attn_low = turn_exchange(attn)
    inputs = tokens.astype(f32)
    upstream = cotangent.astype(f32)
    x_mid = inputs + dot(attn_low, wo)
    factor_two = factor_of(x_mid)
    routed_in = (x_mid * factor_two * gain_m).astype(bf16)
    logits = dot(routed_in, wr)
    expert_ids = jnp.arange(32, dtype=jnp.int32)
    chosen = jnp.any(choice[:, :, None] == expert_ids[None, None, :], axis=1)
    masked = jnp.where(chosen, logits, neg_big)
    lifted = jnp.where(chosen, jnp.exp(masked - jnp.max(masked, axis=-1, keepdims=True)), 0.0)
    gates = lifted / jnp.sum(lifted, axis=-1, keepdims=True)
    routed_all, gates_all = routed_exchange(routed_in, gates.T)
    e = lax.axis_index("exp")
    routed_all = routed_all.reshape(N_EXP * rows, width)
    own_gates = lax.dynamic_slice_in_dim(gates_all, e * 2, 2, axis=1)
    own_gates = own_gates.transpose(0, 2, 1).reshape(N_EXP * rows, 2)
    f = wd.shape[0] // 2
    gate_col = jnp.concatenate(
        [jnp.broadcast_to(own_gates[:, i : i + 1], (N_EXP * rows, f)) for i in range(2)], axis=1
    )
    lifted_h = dot(routed_all, wgu)
    gate_h, up_h = lifted_h[:, : 2 * f], lifted_h[:, 2 * f :]
    sig = jax.nn.sigmoid(gate_h)
    silu = gate_h * sig
    hidden = silu * up_h
    hidden_gated = (hidden * gate_col).astype(bf16)
    out_part = dot(hidden_gated, wd).astype(bf16)
    back = dot(up_all, wd, NT)
    gate_parts = jnp.sum((hidden * back).reshape(N_EXP * rows, 2, f), axis=2)
    grad_hidden = back * gate_col
    grad_lifted = jnp.concatenate(
        [
            (grad_hidden * up_h * (sig * (1.0 + gate_h * (1.0 - sig)))).astype(bf16),
            (grad_hidden * silu).astype(bf16),
        ],
        axis=1,
    )
    in_part = dot(grad_lifted, wgu, NT).astype(bf16)
    grad_wgu = dot(routed_all, grad_lifted, TN).astype(bf16)
    grad_wd = jnp.concatenate(
        [dot(hidden_gated[:, i * f : (i + 1) * f], up_all, TN) for i in range(2)], axis=1
    ).astype(bf16)
    gate_parts = jnp.pad(gate_parts.reshape(N_EXP, rows, 2).transpose(0, 2, 1), ((0, 0), (0, 6), (0, 0)))
    grad_routed, gate_back = grad_exchange(in_part.reshape(N_EXP, rows, width), gate_parts)
    wgu_share = lax.psum_scatter(grad_wgu, "ctx", scatter_dimension=0, tiled=True).astype(f32)
    wd_share = lax.psum_scatter(grad_wd, "ctx", scatter_dimension=0, tiled=True).astype(f32)
    grad_gates = gate_back[:, :2].reshape(32, rows).T
    weighted = gates * grad_gates
    grad_logits = (weighted - gates * jnp.sum(weighted, axis=-1, keepdims=True)).astype(bf16)
    grad_wr = dot(routed_in, grad_logits, TN)
    grad_routed = grad_routed + dot(grad_logits, wr, NT)
    grad_gain_m = jnp.sum(grad_routed * x_mid * factor_two, axis=0)
    grad_mid = upstream + normalize_back(x_mid, factor_two, gain_m, grad_routed)
    branch_all, moe_out = branch_exchange(grad_mid.astype(bf16), out_part.reshape(N_EXP, rows, width))
    result = (x_mid + moe_out).astype(bf16)
    branch_all = branch_all.reshape(count, width)
    wo_rows = lax.dynamic_slice_in_dim(wo, c * 128, 128, axis=0)
    grad_attn = dot(branch_all, wo_rows, NT).astype(bf16)
    grad_wo = dot(attn, branch_all, TN)
    heads_grad = grad_attn.reshape(count, 2, HEAD_SIZE)
    grad_probs = jnp.einsum("qhd,kd->hqk", heads_grad, v, preferred_element_type=f32)
    grad_scores = probs * (grad_probs - jnp.sum(probs * grad_probs, axis=-1, keepdims=True))
    grad_scores = grad_scores.astype(bf16)
    scale = HEAD_SIZE ** (-0.5)
    grad_q = jnp.einsum("hqk,kd->qhd", grad_scores, k, preferred_element_type=f32).reshape(count, 128) * scale
    grad_k = jnp.einsum("hqk,qhd->kd", grad_scores, q, preferred_element_type=f32) * scale
    grad_v = jnp.einsum("hqk,qhd->kd", probs_low, heads_grad, preferred_element_type=f32)
    grad_qk = jnp.concatenate([grad_q, grad_k], axis=1)
    grad_qk = grad_qk * cosine + unswap_halves(grad_qk * sine)
    grad_qkv = jnp.concatenate([grad_qk, grad_v], axis=1).astype(bf16)
    grad_w = dot(h_all, grad_qkv, TN).astype(bf16).reshape(N_EXP, own_rows, 256)
    wo_chunks = grad_wo.astype(bf16).reshape(2, 8, 8, width).transpose(1, 0, 2, 3).reshape(N_EXP, own_rows, 128)
    small = jnp.concatenate(
        [grad_wr, grad_gain_m[:, None], jnp.zeros((width, 128 - 33), f32)], axis=1
    ).astype(bf16)
    shares = jnp.concatenate([grad_w, wo_chunks, small.reshape(N_EXP, own_rows, 128)], axis=2)
    grad_tokens_qkv, owned, wo_owned = last_exchange(grad_qkv, shares)
    grad_h_one = dot(grad_tokens_qkv, wqkv, NT)
    grad_tokens = grad_mid + normalize_back(inputs, factor_of(inputs), gain_a, grad_h_one)
    owned = owned.astype(f32)
    by_head = owned.transpose(1, 0, 2)
    out_wq = by_head[:, :, :128].reshape(own_rows, width)
    out_wk = by_head[:, :, 128:192].reshape(own_rows, width // 2)
    out_wv = by_head[:, :, 192:256].reshape(own_rows, width // 2)
    out_wo = wo_owned.astype(f32).reshape(own_rows, width)
    tail = jnp.sum(owned[:, :, 384:], axis=0)
    out_gain_a = (
        jnp.sum(w_query.astype(f32) * out_wq, axis=1)
        + jnp.sum(key_matrix.astype(f32) * out_wk, axis=1)
        + jnp.sum(value_matrix.astype(f32) * out_wv, axis=1)
    ) / norm_attn.astype(f32)
    f_own = wgu_share.shape[1] // 4
    return (
        result[None],
        grad_tokens[None],
        out_gain_a,
        out_wq,
        out_wk,
        out_wv,
        out_wo,
        tail[:, 32],
        tail[:, :32],
        jnp.stack([wgu_share[:, :f_own], wgu_share[:, f_own : 2 * f_own]]),
        jnp.stack([wgu_share[:, 2 * f_own : 3 * f_own], wgu_share[:, 3 * f_own :]]),
        jnp.stack([wd_share[:, :width], wd_share[:, width:]]),
    )


def solution(mesh):
    return jax.shard_map(
        body,
        mesh=mesh,
        in_specs=(
            P("exp", "ctx", None),
            P("exp", "ctx", None),
            P(),
            P("exp", "ctx", None),
            P("exp"),
            P("exp", None),
            P("exp", None),
            P("exp", None),
            P("exp", None),
            P("exp"),
            P("exp", None),
            P("exp", "ctx", None),
            P("exp", "ctx", None),
            P("exp", "ctx", None),
        ),
        out_specs=(
            P("exp", "ctx", None),
            P("exp", "ctx", None),
            P("exp"),
            P("exp", None),
            P("exp", None),
            P("exp", None),
            P("exp", None),
            P("exp"),
            P("exp", None),
            P("exp", "ctx", None),
            P("exp", "ctx", None),
            P("exp", "ctx", None),
        ),
        check_vma=False,
    )
```

```python
import jax
import jax.numpy as jnp
from jax import lax
from jax.experimental import pallas as pl
from jax.experimental.pallas import tpu as pltpu
from jax.sharding import PartitionSpec as P

HEAD_SIZE = 64
HALF = 32
N_CTX = 8
N_EXP = 16
eps_norm = 1e-06
rope_base = 10000.0
neg_big = -1e30
f32, bf16 = jnp.float32, jnp.bfloat16

MESH = pl.DeviceIdType.MESH
ANY = pl.BlockSpec(memory_space=pl.ANY)
VMEM = pl.BlockSpec(memory_space=pltpu.VMEM)
DMA = pltpu.SemaphoreType.DMA
NEAR_LAST = (6, 5, 7, 2, 4, 1, 3)
NEAR_FIRST = (1, 3, 2, 4, 5, 7, 6)
CTX_ORDER = (2, 6, 4, 1, 3, 5, 7)


def remote(src, dst, send, recv, where):
    return pltpu.make_async_remote_copy(
        src_ref=src, dst_ref=dst, send_sem=send, recv_sem=recv, device_id=where, device_id_type=MESH
    )


def greet(places, amount=None):
    barrier = pltpu.get_barrier_semaphore()
    for where in places:
        pl.semaphore_signal(barrier, inc=1, device_id=where, device_id_type=MESH)
    pl.semaphore_wait(barrier, len(places) if amount is None else amount)


class Here:
    def __init__(self):
        self.c = lax.axis_index("ctx")
        self.e = lax.axis_index("exp")
        self.core = lax.rem(self.e, 2)
        self.chip = self.e // 2
        self.partner = {"exp": self.e + 1 - 2 * self.core}

    def ctx(self, k):
        return lax.rem(self.c + k, N_CTX)

    def chip_at(self, k):
        return 4 * lax.rem(self.chip // 4 + k // 4, 2) + lax.rem(lax.rem(self.chip, 4) + lax.rem(k, 4), 4)

    def chip_from(self, k):
        return 4 * lax.rem(self.chip // 4 + k // 4, 2) + lax.rem(lax.rem(self.chip, 4) + 4 - lax.rem(k, 4), 4)

    def ctx_peers(self):
        return [{"ctx": self.ctx(k)} for k in range(1, N_CTX)]

    def same_core(self, k):
        return {"exp": 2 * self.chip_at(k) + self.core}

    def exp_peers(self):
        return [self.partner] + [self.same_core(k) for k in range(1, 8)]

    def other_core_peers(self):
        return [{"exp": 2 * self.chip_at(k) + 1 - self.core} for k in range(1, 8)]


class Gather:
    sems = (8, 8)

    def __init__(self, here, x, out, send, recv):
        self.copies = [pltpu.make_async_copy(x, out.at[here.c], send.at[0])]
        for k in CTX_ORDER:
            self.copies.append(remote(x, out.at[here.c], send.at[k], recv.at[k], {"ctx": here.ctx(k)}))

    def start(self):
        for c in self.copies:
            c.start()

    def wait(self):
        for c in self.copies:
            c.wait()


class Turn:
    sems = (8, 8)

    def __init__(self, here, x, out, send, recv):
        rows, cols = out.shape[0], x.shape[1]
        into = out.at[:, pl.ds(pl.multiple_of(here.c * cols, cols), cols)]

        def part(j):
            return x.at[pl.ds(pl.multiple_of(j * rows, rows), rows)]

        self.copies = [pltpu.make_async_copy(part(here.c), into, send.at[0])]
        for k in CTX_ORDER:
            j = here.ctx(k)
            self.copies.append(remote(part(j), into, send.at[k], recv.at[k], {"ctx": j}))

    start = Gather.start
    wait = Gather.wait


class PairGather:
    sems = (8, 8, 8, 8)

    def __init__(self, here, x, out, send, recv, fsend, frecv):
        e = here.e
        self.own = pltpu.make_async_copy(x, out.at[e], fsend.at[0])
        self.first = remote(x, out.at[e], send.at[0], recv.at[0], here.partner)
        self.far, self.forward = {}, {}
        for k in NEAR_LAST:
            self.far[k] = remote(x, out.at[e], send.at[k], recv.at[k], here.same_core(k))
            slot = 2 * here.chip_from(k) + here.core
            self.forward[k] = remote(out.at[slot], out.at[slot], fsend.at[k], frecv.at[k], here.partner)

    def start(self):
        for k in NEAR_LAST:
            self.far[k].start()
        self.first.start()
        self.own.start()

    def pass_on(self):
        for k in NEAR_FIRST:
            self.far[k].wait_recv()
            self.forward[k].start()

    def wait(self):
        self.own.wait()
        self.first.wait()
        for k in NEAR_FIRST:
            self.far[k].wait_send()
            self.forward[k].wait()


class PairScatter:
    sems = (8, 8, 8, 8, 8)

    @staticmethod
    def scratch(x):
        return [pltpu.VMEM((8,) + x.shape[1:], x.dtype)] * 4

    def __init__(self, here, x, total, mine, near, summed, far, load, nsend, nrecv, fsend, frecv):
        self.total, self.mine, self.near, self.summed, self.far = total, mine, near, summed, far
        self.loads, self.nears, self.fars = {}, {}, {}
        self.order = NEAR_LAST + (0,)
        for k in self.order:
            there = here.chip_at(k)
            self.nears[k] = remote(x.at[2 * there + 1 - here.core], near.at[k], nsend.at[k], nrecv.at[k], here.partner)
            self.loads[k] = pltpu.make_async_copy(x.at[2 * there + here.core], mine.at[k], load.at[k])
            if k:
                self.fars[k] = remote(summed.at[k], far.at[k], fsend.at[k], frecv.at[k], here.same_core(k))

    def start(self):
        for k in self.order:
            self.nears[k].start()
            self.loads[k].start()

    def pass_on(self):
        for k in self.order:
            self.loads[k].wait()
            self.nears[k].wait_recv()
            both = self.mine[k].astype(f32) + self.near[k].astype(f32)
            if k:
                self.summed[k] = both.astype(self.summed.dtype)
                self.fars[k].start()
            else:
                self.total[...] = both

    def wait(self):
        for k in NEAR_FIRST:
            self.fars[k].wait_recv()
            self.total[...] += self.far[k].astype(f32)
        for k in self.order:
            self.nears[k].wait_send()
            if k:
                self.fars[k].wait_send()


class Spread:
    sems = (16, 16)

    def __init__(self, here, x, out, send, recv):
        self.copies = [pltpu.make_async_copy(x.at[here.e], out.at[here.e], send.at[0])]
        for k in range(1, N_EXP):
            j = lax.rem(here.e + k, N_EXP)
            self.copies.append(remote(x.at[j], out.at[here.e], send.at[k], recv.at[k], {"exp": j}))

    start = Gather.start
    wait = Gather.wait


def sem_shapes(*kinds):
    return [DMA((n,)) for kind in kinds for n in kind.sems]


def params(cid):
    return pltpu.CompilerParams(collective_id=cid, has_side_effects=True, vmem_limit_bytes=40 * 2**20)


def call(kernel, outs, scratch, cid, *args, out_specs=None):
    return pl.pallas_call(
        kernel,
        out_shape=outs,
        in_specs=[ANY] * len(args),
        out_specs=out_specs or [ANY] * len(outs),
        scratch_shapes=scratch,
        compiler_params=params(cid),
    )(*args)


def shape(s, t):
    return jax.ShapeDtypeStruct(s, t)


def start_exchange(tokens, pack, wo, cot):
    def kernel(x, p, w, u, xs, ps, ws, us, *sems):
        here = Here()
        greet(here.ctx_peers() + here.exp_peers())
        a = Gather(here, x, xs, *sems[0:2])
        g = [PairGather(here, i, o, *sems[2 + 4 * n : 6 + 4 * n]) for n, (i, o) in enumerate(((p, ps), (w, ws), (u, us)))]
        a.start()
        for i in g:
            i.start()
        for i in g:
            i.pass_on()
        a.wait()
        for i in g:
            i.wait()

    return call(
        kernel,
        [shape((8,) + tokens.shape, bf16)] + [shape((16,) + a.shape, bf16) for a in (pack, wo, cot)],
        sem_shapes(Gather, PairGather, PairGather, PairGather),
        1,
        tokens,
        pack,
        wo,
        cot,
    )


def turn_exchange(attn):
    def kernel(x, out, *sems):
        here = Here()
        greet(here.ctx_peers())
        t = Turn(here, x, out, *sems)
        t.start()
        t.wait()

    return call(kernel, [shape((attn.shape[0] // 8, attn.shape[1] * 8), attn.dtype)], sem_shapes(Turn), 2, attn)[0]


def experts(routed, gates, up_all, wgu, wd):
    rows, width = routed.shape
    both = 2 * rows
    hid = wd.shape[0]
    f = hid // 2
    chunk = 256

    def kernel(
        x, g, up, wgu, wd, out_part, total, gback, dwgu, dwd,
        xs, gs, parts, near, summed, far, hg, dgu, gparts,
        xsend, xrecv, xfsend, xfrecv, gsend, grecv, gfsend, gfrecv,
        nsend, nrecv, rsend, rrecv, psend, precv,
    ):
        here = Here()
        core, e = here.core, here.e
        greet(here.exp_peers() + here.other_core_peers())
        own = [pltpu.make_async_copy(g, gs.at[e], gfsend.at[0]), pltpu.make_async_copy(x, xs.at[e], xfsend.at[0])]
        first = [
            remote(g, gs.at[e], gsend.at[0], grecv.at[0], here.partner),
            remote(x, xs.at[e], xsend.at[0], xrecv.at[0], here.partner),
        ]
        for copy in own + first:
            copy.start()

        def away(k):
            return [
                remote(g, gs.at[e], gsend.at[k], grecv.at[k], here.same_core(k)),
                remote(x, xs.at[e], xsend.at[k], xrecv.at[k], here.same_core(k)),
            ]

        def pass_on(k):
            slot = 2 * here.chip_from(k) + core
            return [
                remote(gs.at[slot], gs.at[slot], gfsend.at[k], gfrecv.at[k], here.partner),
                remote(xs.at[slot], xs.at[slot], xfsend.at[k], xfrecv.at[k], here.partner),
            ]

        def to_partner(k):
            return remote(parts.at[k, 1 - core], near.at[k], nsend.at[k], nrecv.at[k], here.partner)

        def to_chip(k):
            where = {"exp": 2 * here.chip_from(k) + core}
            return remote(summed.at[k], far.at[k], rsend.at[k], rrecv.at[k], where)

        def gate_part(j):
            return remote(gparts.at[j], gback.at[e], psend.at[j], precv.at[e], {"exp": j})

        for k in range(1, 8):
            for copy in away(k):
                copy.start()

        picks = lax.broadcasted_iota(jnp.int32, (32, 2 * 128), 0) == 2 * e + (
            lax.broadcasted_iota(jnp.int32, (32, 2 * 128), 1) // 128
        )
        picks = picks.astype(f32)

        def finish(k):
            to_partner(k).wait_recv()
            both_cores = parts[k, core].astype(f32) + near[k].astype(f32)

            @pl.when(k == 0)
            def _():
                total[...] = both_cores

            @pl.when(k > 0)
            def _():
                summed[k] = both_cores.astype(bf16)
                to_chip(k).start()

        def step(k, carry):
            @pl.when(k < 7)
            def _():
                for copy in away(k + 1):
                    copy.wait_recv()
                for copy in pass_on(k + 1):
                    copy.start()

            @pl.when(k == 0)
            def _():
                for copy in own:
                    copy.wait()
                for copy in first:
                    copy.wait_recv()

            @pl.when(k > 0)
            def _():
                for copy in pass_on(k):
                    copy.wait_recv()

            chip = here.chip_from(k)
            at = pl.ds(pl.multiple_of(chip * both, both), both)
            xb = xs[pl.ds(2 * chip, 2)].reshape(both, width)
            ub = up[at]
            gate_cols = jnp.concatenate(
                [
                    lax.dot_general(
                        gs[2 * chip + i], picks, (TN, ((), ())), precision=lax.Precision.HIGHEST,
                        preferred_element_type=f32,
                    )
                    for i in range(2)
                ],
                axis=0,
            )
            gate_sums = jnp.zeros((8, both), f32)
            for i in range(2):
                gate = jnp.concatenate([gate_cols[:, 128 * i : 128 * (i + 1)]] * (chunk // 128), axis=1)
                to_row = (lax.broadcasted_iota(jnp.int32, (8, chunk), 0) == i).astype(bf16)
                for j in range(i * f, (i + 1) * f, chunk):
                    cols, up_cols = pl.ds(j, chunk), pl.ds(hid + j, chunk)
                    gate_h = dot(xb, wgu[:, cols])
                    up_h = dot(xb, wgu[:, up_cols])
                    back = dot(ub, wd[cols], NT)
                    sig = 1.0 / (1.0 + jnp.exp(-gate_h))
                    silu = gate_h * sig
                    hidden = silu * up_h
                    hg[at, cols] = (hidden * gate).astype(bf16)
                    gate_sums += dot(to_row, (hidden * back).astype(bf16), NT)
                    grad_hidden = back * gate
                    dgu[at, cols] = (grad_hidden * up_h * (sig * (1.0 + gate_h * (1.0 - sig)))).astype(bf16)
                    dgu[at, up_cols] = (grad_hidden * silu).astype(bf16)
            for i in range(2):
                gparts[2 * chip + i] = gate_sums[:, rows * i : rows * (i + 1)]
            parts[k] = dot(dgu[at], wgu[...], NT).astype(bf16).reshape(2, rows, width)
            to_partner(k).start()
            gate_part(2 * chip + 1 - core).start()

            @pl.when(k > 0)
            def _():
                gate_part(2 * chip + core).start()

            out_part[pl.ds(2 * chip, 2)] = dot(hg[at], wd[...]).astype(bf16).reshape(2, rows, width)

            @pl.when(k > 0)
            def _():
                finish(k - 1)

            return carry

        lax.fori_loop(0, 8, step, 0)
        mine = pltpu.make_async_copy(gparts.at[e], gback.at[e], psend.at[e])
        mine.start()
        finish(jnp.int32(7))

        def weight_rows(i, carry):
            at = pl.ds(pl.multiple_of(i * 256, 256), 256)
            columns = xs[:, :, at].reshape(16 * rows, 256)
            dwgu[at] = dot(columns, dgu[...], TN).astype(bf16)
            return carry

        lax.fori_loop(0, width // 256, weight_rows, 0)

        def down_rows(i, carry):
            at = pl.ds(pl.multiple_of(i * 256, 256), 256)
            grads = dot(hg[:, at], up[...], TN).astype(bf16)
            down = pl.ds(pl.multiple_of(lax.rem(i, 2) * 256, 256), 256)
            dwd[down, pl.ds(pl.multiple_of((i // 2) * width, width), width)] = grads
            return carry

        lax.fori_loop(0, hid // 256, down_rows, 0)

        def collect(k, carry):
            to_chip(k).wait_recv()
            total[...] += far[k].astype(f32)
            return carry

        lax.fori_loop(1, 8, collect, 0)
        for copy in first:
            copy.wait_send()
        mine.wait()

        def drain(k, carry):
            for copy in away(k) + pass_on(k) + [to_partner(k), to_chip(k)]:
                copy.wait_send()
            return carry

        lax.fori_loop(1, 8, drain, 0)
        to_partner(0).wait_send()

        def drain_gates(k, carry):
            j = lax.rem(e + k, N_EXP)
            gate_part(j).wait_send()
            remote(gparts.at[j], gback.at[j], psend.at[j], precv.at[j], {"exp": j}).wait_recv()
            return carry

        lax.fori_loop(1, N_EXP, drain_gates, 0)

    block = (8, rows, width)
    return pl.pallas_call(
        kernel,
        out_shape=[
            shape((16, rows, width), bf16),
            shape((rows, width), f32),
            shape((16, 8, rows), f32),
            shape(wgu.shape, bf16),
            shape((f, 2 * width), bf16),
        ],
        in_specs=[ANY, ANY, VMEM, VMEM, VMEM],
        out_specs=[VMEM, VMEM, ANY, VMEM, VMEM],
        scratch_shapes=[
            pltpu.VMEM((16, rows, width), bf16),
            pltpu.VMEM((16, 32, rows), f32),
            pltpu.VMEM((8, 2, rows, width), bf16),
            pltpu.VMEM(block, bf16),
            pltpu.VMEM(block, bf16),
            pltpu.VMEM(block, bf16),
            pltpu.VMEM((16 * rows, hid), bf16),
            pltpu.VMEM((16 * rows, 2 * hid), bf16),
            pltpu.VMEM((16, 8, rows), f32),
        ]
        + [DMA((8,))] * 12
        + [DMA((16,))] * 2,
        compiler_params=pltpu.CompilerParams(collective_id=3, has_side_effects=True, vmem_limit_bytes=60 * 2**20),
    )(routed, gates, up_all, wgu, wd)


def branch_exchange(branch, out_parts):
    def kernel(b, x, bs, total, *rest):
        here = Here()
        greet(here.ctx_peers() + here.exp_peers())
        sems = rest[4:]
        a = Gather(here, b, bs, *sems[5:7])
        s = PairScatter(here, x, total, *rest[:4], *sems[0:5])
        a.start()
        s.start()
        s.pass_on()
        s.wait()
        a.wait()

    return call(
        kernel,
        [shape((8,) + branch.shape, bf16), shape(out_parts.shape[1:], f32)],
        PairScatter.scratch(out_parts) + sem_shapes(PairScatter, Gather),
        5,
        branch,
        out_parts,
        out_specs=[ANY, VMEM],
    )


def last_exchange(grads, shares):
    def kernel(g, x, back, alls, wos, total, low, *rest):
        here = Here()
        greet(here.ctx_peers() + here.exp_peers())
        sems = rest[4:]
        turn = Turn(here, g, back, *sems[5:7])
        s = PairScatter(here, x, total, *rest[:4], *sems[0:5])
        spread = Gather(here, low, alls, *sems[7:9])
        wsend, wrecv = sems[9:11]
        chunk = pl.ds(256, 128)
        moves = [pltpu.make_async_copy(alls.at[here.chip, :, chunk], wos.at[here.chip], wsend.at[0])]
        for k in NEAR_LAST:
            moves.append(
                remote(alls.at[here.chip_at(k), :, chunk], wos.at[here.chip], wsend.at[k], wrecv.at[k], here.same_core(k))
            )
        s.start()
        turn.start()
        s.pass_on()
        s.wait()
        low[...] = total[...].astype(bf16)
        spread.start()
        spread.wait()
        for m in moves:
            m.start()
        for m in moves:
            m.wait()
        turn.wait()

    rows, cols = shares.shape[1:]
    return call(
        kernel,
        [
            shape((grads.shape[0] // 8, grads.shape[1] * 8), bf16),
            shape((8, rows, cols), bf16),
            shape((8, rows, 128), bf16),
        ],
        [pltpu.VMEM((rows, cols), f32), pltpu.VMEM((rows, cols), bf16)]
        + PairScatter.scratch(shares)
        + sem_shapes(PairScatter, Turn, Gather, Gather),
        6,
        grads,
        shares,
    )


def dot(a, b, dims=((1,), (0,))):
    return lax.dot_general(a, b, (dims, ((), ())), preferred_element_type=f32)


NT = ((1,), (1,))
TN = ((0,), (0,))


def swap_halves(x):
    parts = []
    for i in range(0, x.shape[1], HEAD_SIZE):
        parts += [-x[:, i + HALF : i + HEAD_SIZE], x[:, i : i + HALF]]
    return jnp.concatenate(parts, axis=1)


def unswap_halves(x):
    return -swap_halves(x)


def factor_of(values):
    return lax.rsqrt(jnp.mean(values * values, axis=-1, keepdims=True) + eps_norm)


def normalize_back(values, factor, gain, upstream):
    scaled = upstream * gain
    inner = jnp.mean(scaled * values, axis=-1, keepdims=True)
    return factor * scaled - values * factor * factor * factor * inner


def body(
    tokens, cotangent, span_order, expert_choice, norm_attn, w_query, key_matrix, value_matrix,
    w_out, norm_moe, w_router, w_gate, w_up, w_down,
):
    c = lax.axis_index("ctx")
    tokens, cotangent, choice = tokens[0], cotangent[0], expert_choice[0]
    rows, width = tokens.shape
    own_rows = w_query.shape[0]
    wgu_own = jnp.concatenate([w_gate[0], w_gate[1], w_up[0], w_up[1]], axis=1)
    wgu = lax.all_gather(wgu_own, "ctx", axis=0, tiled=True)
    wd_own = jnp.concatenate([w_down[0], w_down[1]], axis=1)
    wd_wide = lax.all_gather(wd_own, "ctx", axis=0, tiled=True)
    wd = jnp.concatenate([wd_wide[:, :width], wd_wide[:, width:]], axis=0)
    wqkv_own = jnp.concatenate(
        [
            w_query.reshape(own_rows, N_CTX, 128),
            key_matrix.reshape(own_rows, N_CTX, 64),
            value_matrix.reshape(own_rows, N_CTX, 64),
        ],
        axis=2,
    ).reshape(own_rows, N_CTX * 256)
    wqkv = lax.all_gather(wqkv_own, "exp", axis=0, tiled=True)
    own_cols = lax.dynamic_slice_in_dim(wqkv_own, c * 256, 256, axis=1)
    pack = jnp.concatenate(
        [
            own_cols,
            swap_halves(own_cols[:, :192]),
            w_router,
            norm_attn[:, None],
            norm_moe[:, None],
            jnp.zeros((own_rows, 512 - 448 - 34), bf16),
        ],
        axis=1,
    )
    x_all, pack_all, wo, up_all = start_exchange(tokens, pack, w_out, cotangent)
    pack_all = pack_all.reshape(width, 512)
    wo = wo.reshape(width, width)
    up_all = up_all.reshape(N_EXP * rows, width)
    gain_a = pack_all[:, 480].astype(f32)[None, :]
    gain_m = pack_all[:, 481].astype(f32)[None, :]
    wr = pack_all[:, 448:480]
    count = N_CTX * rows
    span_len = rows // 2
    ids = jnp.arange(count, dtype=jnp.int32)
    table = ids[:, None] // span_len == jnp.arange(2 * N_CTX, dtype=jnp.int32)[None, :]
    places = jnp.sum(jnp.where(table, span_order[None, :], 0), axis=1) * span_len + ids % span_len
    freqs = rope_base ** (-(jnp.arange(HALF, dtype=f32) * 2.0 / HEAD_SIZE))
    turned = places.astype(f32)[:, None] * freqs[None, :]
    cosine = jnp.tile(jnp.cos(turned), (1, 6))
    sine = jnp.tile(jnp.sin(turned), (1, 6))
    x_seq = x_all.reshape(count, width).astype(f32)
    h_all = (x_seq * factor_of(x_seq) * gain_a).astype(bf16)
    projected = dot(h_all, pack_all[:, :448])
    qk = (projected[:, :192] * cosine + projected[:, 256:448] * sine).astype(bf16)
    v = projected[:, 192:256].astype(bf16)
    q = qk[:, :128].reshape(count, 2, HEAD_SIZE)
    k = qk[:, 128:]
    visible = places[None, :] <= places[:, None]
    scores = jnp.einsum("qhd,kd->hqk", q, k, preferred_element_type=f32) * HEAD_SIZE ** (-0.5)
    scores = jnp.where(visible[None], scores, neg_big)
    largest = jnp.max(scores, axis=-1, keepdims=True)
    shifted = jnp.exp(scores - largest)
    probs = shifted / jnp.sum(shifted, axis=-1, keepdims=True)
    probs_low = probs.astype(bf16)
    attn = jnp.einsum("hqk,kd->qhd", probs_low, v, preferred_element_type=f32)
    attn = attn.reshape(count, 128).astype(bf16)
    attn_low = turn_exchange(attn)
    inputs = tokens.astype(f32)
    upstream = cotangent.astype(f32)
    x_mid = inputs + dot(attn_low, wo)
    factor_two = factor_of(x_mid)
    routed_in = (x_mid * factor_two * gain_m).astype(bf16)
    logits = dot(routed_in, wr)
    expert_ids = jnp.arange(32, dtype=jnp.int32)
    chosen = jnp.any(choice[:, :, None] == expert_ids[None, None, :], axis=1)
    masked = jnp.where(chosen, logits, neg_big)
    lifted = jnp.where(chosen, jnp.exp(masked - jnp.max(masked, axis=-1, keepdims=True)), 0.0)
    gates = lifted / jnp.sum(lifted, axis=-1, keepdims=True)
    out_part, grad_routed, gate_back, grad_wgu, grad_wd = experts(routed_in, gates.T, up_all, wgu, wd)
    wgu_share = lax.psum_scatter(grad_wgu, "ctx", scatter_dimension=0, tiled=True).astype(f32)
    wd_share = lax.psum_scatter(grad_wd, "ctx", scatter_dimension=0, tiled=True).astype(f32)
    grad_gates = gate_back[:, :2].reshape(32, rows).T
    weighted = gates * grad_gates
    grad_logits = (weighted - gates * jnp.sum(weighted, axis=-1, keepdims=True)).astype(bf16)
    grad_wr = dot(routed_in, grad_logits, TN)
    grad_routed = grad_routed + dot(grad_logits, wr, NT)
    grad_gain_m = jnp.sum(grad_routed * x_mid * factor_two, axis=0)
    grad_mid = upstream + normalize_back(x_mid, factor_two, gain_m, grad_routed)
    branch_all, moe_out = branch_exchange(grad_mid.astype(bf16), out_part)
    result = (x_mid + moe_out).astype(bf16)
    branch_all = branch_all.reshape(count, width)
    wo_rows = lax.dynamic_slice_in_dim(wo, c * 128, 128, axis=0)
    grad_attn = dot(branch_all, wo_rows, NT).astype(bf16)
    grad_wo = dot(attn, branch_all, TN)
    heads_grad = grad_attn.reshape(count, 2, HEAD_SIZE)
    grad_probs = jnp.einsum("qhd,kd->hqk", heads_grad, v, preferred_element_type=f32)
    grad_scores = probs * (grad_probs - jnp.sum(probs * grad_probs, axis=-1, keepdims=True))
    grad_scores = grad_scores.astype(bf16)
    scale = HEAD_SIZE ** (-0.5)
    grad_q = jnp.einsum("hqk,kd->qhd", grad_scores, k, preferred_element_type=f32).reshape(count, 128) * scale
    grad_k = jnp.einsum("hqk,qhd->kd", grad_scores, q, preferred_element_type=f32) * scale
    grad_v = jnp.einsum("hqk,qhd->kd", probs_low, heads_grad, preferred_element_type=f32)
    grad_qk = jnp.concatenate([grad_q, grad_k], axis=1)
    grad_qk = grad_qk * cosine + unswap_halves(grad_qk * sine)
    grad_qkv = jnp.concatenate([grad_qk, grad_v], axis=1).astype(bf16)
    grad_w = dot(h_all, grad_qkv, TN).astype(bf16).reshape(N_EXP, own_rows, 256)
    wo_chunks = grad_wo.astype(bf16).reshape(2, 8, 8, width).transpose(1, 0, 2, 3).reshape(N_EXP, own_rows, 128)
    small = jnp.concatenate(
        [grad_wr, grad_gain_m[:, None], jnp.zeros((width, 128 - 33), f32)], axis=1
    ).astype(bf16)
    shares = jnp.concatenate([grad_w, wo_chunks, small.reshape(N_EXP, own_rows, 128)], axis=2)
    grad_tokens_qkv, owned, wo_owned = last_exchange(grad_qkv, shares)
    grad_h_one = dot(grad_tokens_qkv, wqkv, NT)
    grad_tokens = grad_mid + normalize_back(inputs, factor_of(inputs), gain_a, grad_h_one)
    owned = owned.astype(f32)
    by_head = owned.transpose(1, 0, 2)
    out_wq = by_head[:, :, :128].reshape(own_rows, width)
    out_wk = by_head[:, :, 128:192].reshape(own_rows, width // 2)
    out_wv = by_head[:, :, 192:256].reshape(own_rows, width // 2)
    out_wo = wo_owned.astype(f32).reshape(own_rows, width)
    tail = jnp.sum(owned[:, :, 384:], axis=0)
    out_gain_a = (
        jnp.sum(w_query.astype(f32) * out_wq, axis=1)
        + jnp.sum(key_matrix.astype(f32) * out_wk, axis=1)
        + jnp.sum(value_matrix.astype(f32) * out_wv, axis=1)
    ) / norm_attn.astype(f32)
    f_own = wgu_share.shape[1] // 4
    return (
        result[None],
        grad_tokens[None],
        out_gain_a,
        out_wq,
        out_wk,
        out_wv,
        out_wo,
        tail[:, 32],
        tail[:, :32],
        jnp.stack([wgu_share[:, :f_own], wgu_share[:, f_own : 2 * f_own]]),
        jnp.stack([wgu_share[:, 2 * f_own : 3 * f_own], wgu_share[:, 3 * f_own :]]),
        jnp.stack([wd_share[:, :width], wd_share[:, width:]]),
    )


def solution(mesh):
    return jax.shard_map(
        body,
        mesh=mesh,
        in_specs=(
            P("exp", "ctx", None),
            P("exp", "ctx", None),
            P(),
            P("exp", "ctx", None),
            P("exp"),
            P("exp", None),
            P("exp", None),
            P("exp", None),
            P("exp", None),
            P("exp"),
            P("exp", None),
            P("exp", "ctx", None),
            P("exp", "ctx", None),
            P("exp", "ctx", None),
        ),
        out_specs=(
            P("exp", "ctx", None),
            P("exp", "ctx", None),
            P("exp"),
            P("exp", None),
            P("exp", None),
            P("exp", None),
            P("exp", None),
            P("exp"),
            P("exp", None),
            P("exp", "ctx", None),
            P("exp", "ctx", None),
            P("exp", "ctx", None),
        ),
        check_vma=False,
    )
```

```python
import functools

import jax
import jax.numpy as jnp
from jax import lax
from jax.experimental import pallas as pl
from jax.experimental.pallas import tpu as pltpu
from jax.sharding import PartitionSpec as P

HEAD_SIZE = 64
HALF = 32
N_CTX = 8
N_EXP = 16
eps_norm = 1e-06
rope_base = 10000.0
neg_big = -1e30
f32, bf16 = jnp.float32, jnp.bfloat16

MESH = pl.DeviceIdType.MESH
ANY = pl.BlockSpec(memory_space=pl.ANY)
VMEM = pl.BlockSpec(memory_space=pltpu.VMEM)
DMA = pltpu.SemaphoreType.DMA
NEAR_LAST = (6, 5, 7, 2, 4, 1, 3)
NEAR_FIRST = (1, 3, 2, 4, 5, 7, 6)
CTX_ORDER = (2, 6, 4, 1, 3, 5, 7)


def remote(src, dst, send, recv, where):
    return pltpu.make_async_remote_copy(
        src_ref=src, dst_ref=dst, send_sem=send, recv_sem=recv, device_id=where, device_id_type=MESH
    )


def greet(places, amount=None):
    barrier = pltpu.get_barrier_semaphore()
    for where in places:
        pl.semaphore_signal(barrier, inc=1, device_id=where, device_id_type=MESH)
    pl.semaphore_wait(barrier, len(places) if amount is None else amount)


class Here:
    def __init__(self):
        self.c = lax.axis_index("ctx")
        self.e = lax.axis_index("exp")
        self.core = lax.rem(self.e, 2)
        self.chip = self.e // 2
        self.partner = {"exp": self.e + 1 - 2 * self.core}

    def ctx(self, k):
        return lax.rem(self.c + k, N_CTX)

    def chip_at(self, k):
        return 4 * lax.rem(self.chip // 4 + k // 4, 2) + lax.rem(lax.rem(self.chip, 4) + lax.rem(k, 4), 4)

    def chip_from(self, k):
        return 4 * lax.rem(self.chip // 4 + k // 4, 2) + lax.rem(lax.rem(self.chip, 4) + 4 - lax.rem(k, 4), 4)

    def ctx_peers(self):
        return [{"ctx": self.ctx(k)} for k in range(1, N_CTX)]

    def same_core(self, k):
        return {"exp": 2 * self.chip_at(k) + self.core}

    def exp_peers(self):
        return [self.partner] + [self.same_core(k) for k in range(1, 8)]

    def other_core_peers(self):
        return [{"exp": 2 * self.chip_at(k) + 1 - self.core} for k in range(1, 8)]


class Gather:
    sems = (8, 8)

    def __init__(self, here, x, out, send, recv):
        self.copies = [pltpu.make_async_copy(x, out.at[here.c], send.at[0])]
        for k in CTX_ORDER:
            self.copies.append(remote(x, out.at[here.c], send.at[k], recv.at[k], {"ctx": here.ctx(k)}))

    def start(self):
        for c in self.copies:
            c.start()

    def wait(self):
        for c in self.copies:
            c.wait()


class AxisGather:
    sems = (8, 8)

    def __init__(self, here, x, out, send, recv):
        c = here.c
        self.own = pltpu.make_async_copy(x, out.at[c], send.at[0])
        across = lax.rem(c + 4, 8)
        self.across = remote(x, out.at[c], send.at[4], recv.at[4], {"ctx": across})
        self.near, self.rest = [], []
        for k in (2, 1, 3):
            peer = {"ctx": c // 4 * 4 + lax.rem(lax.rem(c, 4) + k, 4)}
            self.near.append(remote(x, out.at[c], send.at[k], recv.at[k], peer))
            self.rest.append(remote(out.at[across], out.at[across], send.at[4 + k], recv.at[4 + k], peer))

    def start(self):
        self.across.start()
        for copy in self.near:
            copy.start()
        self.own.start()

    def cross(self):
        self.across.wait_recv()
        for copy in self.rest:
            copy.start()

    def wait(self):
        self.own.wait()
        self.across.wait_send()
        for copy in self.near + self.rest:
            copy.wait()


class Turn:
    sems = (8, 8)

    def __init__(self, here, x, out, send, recv):
        rows, cols = out.shape[0], x.shape[1]
        into = out.at[:, pl.ds(pl.multiple_of(here.c * cols, cols), cols)]

        def part(j):
            return x.at[pl.ds(pl.multiple_of(j * rows, rows), rows)]

        self.copies = [pltpu.make_async_copy(part(here.c), into, send.at[0])]
        for k in CTX_ORDER:
            j = here.ctx(k)
            self.copies.append(remote(part(j), into, send.at[k], recv.at[k], {"ctx": j}))

    start = Gather.start
    wait = Gather.wait


class Columns:
    sems = (8, 8)

    def __init__(self, here, x, out, send, recv):
        rows, cols = x.shape[0], out.shape[1]
        into = out.at[pl.ds(pl.multiple_of(here.c * rows, rows), rows)]

        def part(j):
            return x.at[:, pl.ds(pl.multiple_of(j * cols, cols), cols)]

        self.copies = [pltpu.make_async_copy(part(here.c), into, send.at[0])]
        for k in CTX_ORDER:
            j = here.ctx(k)
            self.copies.append(remote(part(j), into, send.at[k], recv.at[k], {"ctx": j}))

    start = Gather.start
    wait = Gather.wait


class PairGather:
    sems = (8, 8, 8, 8)

    def __init__(self, here, x, out, send, recv, fsend, frecv):
        e = here.e
        self.own = pltpu.make_async_copy(x, out.at[e], fsend.at[0])
        self.first = remote(x, out.at[e], send.at[0], recv.at[0], here.partner)
        self.far, self.forward = {}, {}
        across = out.at[2 * here.chip_at(4) + here.core]
        for k in range(1, 8):
            if k <= 4:
                self.far[k] = remote(x, out.at[e], send.at[k], recv.at[k], here.same_core(k))
            else:
                self.far[k] = remote(across, across, send.at[k], recv.at[k], here.same_core(k - 4))
            slot = 2 * here.chip_from(k) + here.core
            self.forward[k] = remote(out.at[slot], out.at[slot], fsend.at[k], frecv.at[k], here.partner)

    def start(self):
        for k in (4, 2, 1, 3):
            self.far[k].start()
        self.first.start()
        self.own.start()

    def cross(self):
        self.far[4].wait_recv()
        for k in (6, 5, 7):
            self.far[k].start()
        self.forward[4].start()

    def pass_on(self):
        for k in (1, 3, 2, 5, 7, 6):
            self.far[k].wait_recv()
            self.forward[k].start()

    def wait(self):
        self.own.wait()
        self.first.wait()
        for k in range(1, 8):
            self.far[k].wait_send()
            self.forward[k].wait()


class PairScatter:
    sems = (8, 8, 8, 8, 8)

    @staticmethod
    def scratch(x):
        return [pltpu.VMEM((8,) + x.shape[1:], x.dtype)] * 4

    def __init__(self, here, x, total, mine, near, summed, far, load, nsend, nrecv, fsend, frecv):
        self.total, self.mine, self.near, self.summed, self.far = total, mine, near, summed, far
        self.loads, self.nears, self.fars = {}, {}, {}
        self.order = (6, 2, 5, 1, 7, 3, 4, 0)
        for k in self.order:
            there = here.chip_at(k)
            self.nears[k] = remote(x.at[2 * there + 1 - here.core], near.at[k], nsend.at[k], nrecv.at[k], here.partner)
            self.loads[k] = pltpu.make_async_copy(x.at[2 * there + here.core], mine.at[k], load.at[k])
            if k:
                where = here.same_core(k if k <= 4 else k - 4)
                self.fars[k] = remote(summed.at[k], far.at[k], fsend.at[k], frecv.at[k], where)

    def start(self):
        for k in self.order:
            self.nears[k].start()
            self.loads[k].start()

    def pass_on(self):
        for k in self.order:
            self.loads[k].wait()
            self.nears[k].wait_recv()
            both = self.mine[k].astype(f32) + self.near[k].astype(f32)
            if k == 0:
                self.total[...] = both
            else:
                self.summed[k] = both.astype(self.summed.dtype)
                if k != 4:
                    self.fars[k].start()

    def cross(self):
        for k in (5, 7, 6):
            self.fars[k].wait_recv()
        both = self.summed[4].astype(f32) + self.far[5].astype(f32)
        both += self.far[6].astype(f32) + self.far[7].astype(f32)
        self.summed[4] = both.astype(self.summed.dtype)
        self.fars[4].start()

    def wait(self):
        for k in (1, 3, 2, 4):
            self.fars[k].wait_recv()
            self.total[...] += self.far[k].astype(f32)
        for k in self.order:
            self.nears[k].wait_send()
            if k:
                self.fars[k].wait_send()


class Spread:
    sems = (16, 16)

    def __init__(self, here, x, out, send, recv):
        self.copies = [pltpu.make_async_copy(x.at[here.e], out.at[here.e], send.at[0])]
        for k in range(1, N_EXP):
            j = lax.rem(here.e + k, N_EXP)
            self.copies.append(remote(x.at[j], out.at[here.e], send.at[k], recv.at[k], {"exp": j}))

    start = Gather.start
    wait = Gather.wait


def sem_shapes(*kinds):
    return [DMA((n,)) for kind in kinds for n in kind.sems]


def params(cid):
    return pltpu.CompilerParams(collective_id=cid, has_side_effects=True, vmem_limit_bytes=40 * 2**20)


def call(kernel, outs, scratch, cid, *args, out_specs=None):
    return pl.pallas_call(
        kernel,
        out_shape=outs,
        in_specs=[ANY] * len(args),
        out_specs=out_specs or [ANY] * len(outs),
        scratch_shapes=scratch,
        compiler_params=params(cid),
    )(*args)


def shape(s, t):
    return jax.ShapeDtypeStruct(s, t)


def start_exchange(over_ctx, *shards):
    n = len(shards)

    def kernel(*refs):
        here = Here()
        greet(here.exp_peers() + here.ctx_peers())
        ins, outs, sems = refs[: n + 1], refs[n + 1 : 2 * n + 2], refs[2 * n + 2 :]
        items = [PairGather(here, ins[i + 1], outs[i + 1], *sems[4 * i + 2 : 4 * i + 6]) for i in range(n)]
        rows = AxisGather(here, ins[0], outs[0], *sems[0:2])
        for i in items:
            i.start()
        rows.start()
        for i in items:
            i.cross()
        rows.cross()
        for i in items:
            i.pass_on()
        for i in items:
            i.wait()
        rows.wait()

    return call(
        kernel,
        [shape((8,) + over_ctx.shape, over_ctx.dtype)] + [shape((16,) + a.shape, a.dtype) for a in shards],
        sem_shapes(AxisGather, *[PairGather] * n),
        1,
        over_ctx,
        *shards,
    )


def dot(a, b, dims=((1,), (0,))):
    return lax.dot_general(a, b, (dims, ((), ())), preferred_element_type=f32)


NT = ((1,), (1,))
TN = ((0,), (0,))


def factor_of(values):
    return lax.rsqrt(jnp.mean(values * values, axis=-1, keepdims=True) + eps_norm)


def normalize_back(values, factor, gain, upstream):
    scaled = upstream * gain
    inner = jnp.mean(scaled * values, axis=-1, keepdims=True)
    return factor * scaled - values * factor * factor * factor * inner


def experts(routed, gates, up_all, wgu_all, wd_all):
    rows, width = routed.shape
    both = 2 * rows
    f = wd_all.shape[2] // 2 * 8 * wd_all.shape[1] // width
    hid = 2 * f
    wrows = rows + rows // 2
    chunk = 256

    def kernel(
        x, g, u, wg, wdown, out_part, total, gback, dwall,
        xs, gs, up, wgu, wd, usem, wsem, parts, near, summed, far, hg, dgu, gparts,
        xsend, xrecv, xfsend, xfrecv, gsend, grecv, gfsend, gfrecv,
        nsend, nrecv, rsend, rrecv, psend, precv,
    ):
        here = Here()
        core, e = here.core, here.e
        greet(here.exp_peers() + here.other_core_peers())
        own = [
            pltpu.make_async_copy(g, gs.at[e], gfsend.at[0]),
            pltpu.make_async_copy(x, xs.at[e], xfsend.at[0]),
            pltpu.make_async_copy(u, up, usem),
        ]
        own.append(pltpu.make_async_copy(wg, wgu, wsem.at[16]))
        for j in range(8):
            for i in range(2):
                own.append(
                    pltpu.make_async_copy(
                        wdown.at[j, :, pl.ds(width * i, width)],
                        wd.at[pl.ds(f * i + rows // 2 * j, rows // 2)],
                        wsem.at[2 * j + i],
                    )
                )
        first = [
            remote(g, gs.at[e], gsend.at[0], grecv.at[0], here.partner),
            remote(x, xs.at[e], xsend.at[0], xrecv.at[0], here.partner),
        ]
        for copy in own + first:
            copy.start()

        def away(k):
            return [
                remote(g, gs.at[e], gsend.at[k], grecv.at[k], here.same_core(k)),
                remote(x, xs.at[e], xsend.at[k], xrecv.at[k], here.same_core(k)),
            ]

        def pass_on(k):
            slot = 2 * here.chip_from(k) + core
            return [
                remote(gs.at[slot], gs.at[slot], gfsend.at[k], gfrecv.at[k], here.partner),
                remote(xs.at[slot], xs.at[slot], xfsend.at[k], xfrecv.at[k], here.partner),
            ]

        def to_partner(k):
            return remote(parts.at[k, 1 - core], near.at[k], nsend.at[k], nrecv.at[k], here.partner)

        def to_chip(k):
            where = {"exp": 2 * here.chip_from(k) + core}
            return remote(summed.at[k], far.at[k], rsend.at[k], rrecv.at[k], where)

        def gate_part(j):
            return remote(gparts.at[j], gback.at[e], psend.at[j], precv.at[e], {"exp": j})

        for k in range(1, 8):
            for copy in away(k):
                copy.start()

        picks = lax.broadcasted_iota(jnp.int32, (32, 2 * 128), 0) == 2 * e + (
            lax.broadcasted_iota(jnp.int32, (32, 2 * 128), 1) // 128
        )
        picks = picks.astype(f32)

        def finish(k):
            to_partner(k).wait_recv()
            both_cores = parts[k, core].astype(f32) + near[k].astype(f32)

            @pl.when(k == 0)
            def _():
                total[...] = both_cores

            @pl.when(k > 0)
            def _():
                summed[k] = both_cores.astype(bf16)
                to_chip(k).start()

        def step(k, carry):
            @pl.when(k < 7)
            def _():
                for copy in away(k + 1):
                    copy.wait_recv()
                for copy in pass_on(k + 1):
                    copy.start()

            @pl.when(k == 0)
            def _():
                for copy in own:
                    copy.wait()
                for copy in first:
                    copy.wait_recv()

            @pl.when(k > 0)
            def _():
                for copy in pass_on(k):
                    copy.wait_recv()

            chip = here.chip_from(k)
            at = pl.ds(pl.multiple_of(chip * both, both), both)
            xb = xs[pl.ds(2 * chip, 2)].reshape(both, width)
            ub = up[pl.ds(2 * chip, 2)].reshape(both, width)
            gate_cols = jnp.concatenate(
                [
                    lax.dot_general(
                        gs[2 * chip + i], picks, (TN, ((), ())), precision=lax.Precision.HIGHEST,
                        preferred_element_type=f32,
                    )
                    for i in range(2)
                ],
                axis=0,
            )
            gate_sums = jnp.zeros((8, both), f32)
            for i in range(2):
                gate = jnp.concatenate([gate_cols[:, 128 * i : 128 * (i + 1)]] * (chunk // 128), axis=1)
                to_row = (lax.broadcasted_iota(jnp.int32, (8, chunk), 0) == i).astype(bf16)
                for j in range(i * f, (i + 1) * f, chunk):
                    cols, up_cols = pl.ds(j, chunk), pl.ds(hid + j, chunk)
                    gate_h = dot(xb, wgu[:, cols])
                    up_h = dot(xb, wgu[:, up_cols])
                    back = dot(ub, wd[cols], NT)
                    sig = 1.0 / (1.0 + jnp.exp(-gate_h))
                    silu = gate_h * sig
                    hidden = silu * up_h
                    hg[at, cols] = (hidden * gate).astype(bf16)
                    gate_sums += dot(to_row, (hidden * back).astype(bf16), NT)
                    grad_hidden = back * gate
                    dgu[at, cols] = (grad_hidden * up_h * (sig * (1.0 + gate_h * (1.0 - sig)))).astype(bf16)
                    dgu[at, up_cols] = (grad_hidden * silu).astype(bf16)
            for i in range(2):
                gparts[2 * chip + i] = gate_sums[:, rows * i : rows * (i + 1)]
            parts[k] = dot(dgu[at], wgu[...], NT).astype(bf16).reshape(2, rows, width)
            to_partner(k).start()
            gate_part(2 * chip + 1 - core).start()

            @pl.when(k > 0)
            def _():
                gate_part(2 * chip + core).start()

            out_part[pl.ds(2 * chip, 2)] = dot(hg[at], wd[...]).astype(bf16).reshape(2, rows, width)

            @pl.when(k > 0)
            def _():
                finish(k - 1)

            return carry

        lax.fori_loop(0, 8, step, 0)
        mine = pltpu.make_async_copy(gparts.at[e], gback.at[e], psend.at[e])
        mine.start()
        finish(jnp.int32(7))

        def weight_rows(i, carry):
            at = pl.ds(pl.multiple_of(i * 256, 256), 256)
            columns = xs[:, :, at].reshape(16 * rows, 256)
            grads = dot(columns, dgu[...], TN).astype(bf16)
            dwall[pl.ds(2 * i, 2), pl.ds(0, rows)] = grads.reshape(2, rows, 2 * hid)
            return carry

        lax.fori_loop(0, width // 256, weight_rows, 0)

        def down_rows(i, carry):
            at = pl.ds(pl.multiple_of(i * 256, 256), 256)
            grads = dot(hg[:, at], up[...].reshape(16 * rows, width), TN).astype(bf16)
            cols = pl.ds(pl.multiple_of((i // 2) * width, width), width)
            dwall[pl.ds(4 * lax.rem(i, 2), 4), pl.ds(rows, rows // 2), cols] = grads.reshape(4, rows // 2, width)
            return carry

        lax.fori_loop(0, hid // 256, down_rows, 0)

        def collect(k, carry):
            to_chip(k).wait_recv()
            total[...] += far[k].astype(f32)
            return carry

        lax.fori_loop(1, 8, collect, 0)
        for copy in first:
            copy.wait_send()
        mine.wait()

        def drain(k, carry):
            for copy in away(k) + pass_on(k) + [to_partner(k), to_chip(k)]:
                copy.wait_send()
            return carry

        lax.fori_loop(1, 8, drain, 0)
        to_partner(0).wait_send()

        def drain_gates(k, carry):
            j = lax.rem(e + k, N_EXP)
            gate_part(j).wait_send()
            remote(gparts.at[j], gback.at[j], psend.at[j], precv.at[j], {"exp": j}).wait_recv()
            return carry

        lax.fori_loop(1, N_EXP, drain_gates, 0)

    block = (8, rows, width)
    return pl.pallas_call(
        kernel,
        out_shape=[
            shape((16, rows, width), bf16),
            shape((rows, width), f32),
            shape((16, 8, rows), f32),
            shape((8, wrows, 2 * hid), bf16),
        ],
        in_specs=[ANY] * 5,
        out_specs=[VMEM, VMEM, ANY, VMEM],
        scratch_shapes=[
            pltpu.VMEM((16, rows, width), bf16),
            pltpu.VMEM((16, 32, rows), f32),
            pltpu.VMEM((16, rows, width), bf16),
            pltpu.VMEM((width, 2 * hid), bf16),
            pltpu.VMEM((hid, width), bf16),
            DMA,
            DMA((17,)),
            pltpu.VMEM((8, 2, rows, width), bf16),
            pltpu.VMEM(block, bf16),
            pltpu.VMEM(block, bf16),
            pltpu.VMEM(block, bf16),
            pltpu.VMEM((16 * rows, hid), bf16),
            pltpu.VMEM((16 * rows, 2 * hid), bf16),
            pltpu.VMEM((16, 8, rows), f32),
        ]
        + [DMA((8,))] * 12
        + [DMA((16,))] * 2,
        compiler_params=pltpu.CompilerParams(collective_id=3, has_side_effects=True, vmem_limit_bytes=60 * 2**20),
    )(routed, gates, up_all, wgu_all, wd_all)


SCALE = HEAD_SIZE ** (-0.5)
QROWS = 256
SPAN = 64
SMEM = pl.BlockSpec(memory_space=pltpu.SMEM)


def left_lanes(shape_):
    return lax.broadcasted_iota(jnp.int32, shape_, 1) % 128 < HEAD_SIZE


def split_heads(kv):
    wide = kv.astype(f32)
    turned = pltpu.roll(wide, HEAD_SIZE, 1)
    left = left_lanes(kv.shape)
    return [
        jnp.where(left, wide, 0.0).astype(bf16),
        jnp.where(left, 0.0, turned).astype(bf16),
        jnp.where(left, turned, 0.0).astype(bf16),
        jnp.where(left, 0.0, wide).astype(bf16),
    ]


def place_column(spans, first, count):
    row = lax.broadcasted_iota(jnp.int32, (count, 1), 0)
    base = jnp.zeros((count, 1), jnp.int32)
    for i in range(count // SPAN):
        base = jnp.where(row // SPAN == i, spans[first + i], base)
    return base * SPAN + row % SPAN


def place_row(spans):
    lane = lax.broadcasted_iota(jnp.int32, (1, 16 * SPAN), 1)
    base = jnp.zeros((1, 16 * SPAN), jnp.int32)
    for i in range(16):
        base = jnp.where(lane // SPAN == i, spans[i], base)
    return base * SPAN + lane % SPAN


def tables(places, freqs):
    turned = places.astype(f32) * freqs
    return jnp.cos(turned), jnp.sin(turned)


def probs_of(q, k, visible):
    scores = jnp.where(visible, dot(q, k, NT) * SCALE, neg_big)
    shifted = jnp.exp(scores - jnp.max(scores, axis=-1, keepdims=True))
    return shifted * (1.0 / jnp.sum(shifted, axis=-1, keepdims=True))


def swap_of(v):
    leading = lax.broadcasted_iota(jnp.int32, v.shape, 1) % HEAD_SIZE < HALF
    return jnp.where(leading, -pltpu.roll(v, v.shape[1] - HALF, 1), pltpu.roll(v, HALF, 1))


def attend(h_one, wqkv, freqs, spans, cot, wd_own):
    rows = h_one.shape[0]
    count = N_CTX * rows

    def kernel(
        h, w, fr, so, u, wd, out, kept, us, wds, stage, seq, heads, attn, send, recv, osend, orecv, ksem, *sems
    ):
        here = Here()
        c = here.c
        greet(here.ctx_peers() + here.exp_peers())
        cots = PairGather(here, u, us, *sems[0:4])
        downs = AxisGather(here, wd, wds, *sems[4:6])
        cots.start()
        cos, sin = tables(place_column(so, 2 * c, rows), fr[...])

        def block_rows(ref, j):
            return ref.at[pl.ds(pl.multiple_of(j * rows, rows), rows)]

        def column(j):
            return out.at[:, pl.ds(pl.multiple_of(j * 128, 128), 128)]

        def arrive(j):
            return remote(stage.at[j], block_rows(seq, c), send.at[j], recv.at[c], {"ctx": j})

        def arrive_own():
            return pltpu.make_async_copy(stage.at[c], block_rows(seq, c), send.at[c])

        def project(b, carry):
            j = lax.rem(c + 1 + b, N_CTX)
            p = dot(h[...], w[:, pl.ds(pl.multiple_of(j * 256, 256), 256)])
            stage[j] = (p * cos + swap_of(p) * sin).astype(bf16)

            @pl.when(b < N_CTX - 1)
            def _():
                arrive(j).start()

            return carry

        lax.fori_loop(0, N_CTX, project, 0)
        arrive_own().start()
        downs.start()
        pr = place_row(so)
        arrive_own().wait()
        for k in range(1, N_CTX):
            j = here.ctx(k)
            arrive(j).wait_send()
            remote(stage.at[j], block_rows(seq, j), send.at[j], recv.at[j], {"ctx": j}).wait_recv()
        keep = pltpu.make_async_copy(seq, kept, ksem)
        keep.start()
        cots.cross()
        downs.cross()
        for i, part in enumerate(split_heads(seq[:, 128:])):
            heads[i] = part

        def leave(j):
            return remote(block_rows(attn, j), column(c), osend.at[j], orecv.at[c], {"ctx": j})

        def local():
            return pltpu.make_async_copy(block_rows(attn, c), column(c), osend.at[c])

        def step(b, carry):
            block = lax.rem(b + c // 2, count // QROWS)
            at = pl.ds(pl.multiple_of(block * QROWS, QROWS), QROWS)
            visible = pr <= place_column(so, block * (QROWS // SPAN), QROWS)
            q = seq[at, :128]
            total = jnp.zeros((QROWS, 128), f32)
            for i in range(2):
                total += dot(probs_of(q, heads[i], visible).astype(bf16), heads[2 + i])
            attn[at] = total.astype(bf16)
            for i in range(QROWS // rows):
                j = block * (QROWS // rows) + i

                @pl.when(j != c)
                def _():
                    leave(j).start()

                @pl.when(j == c)
                def _():
                    local().start()

            return carry

        lax.fori_loop(0, count // QROWS, step, 0)
        cots.pass_on()
        for k in range(1, N_CTX):
            j = here.ctx(k)
            leave(j).wait_send()
            remote(block_rows(attn, c), column(j), osend.at[j], orecv.at[j], {"ctx": j}).wait_recv()
        local().wait()
        keep.wait()
        cots.wait()
        downs.wait()

    return pl.pallas_call(
        kernel,
        out_shape=[
            shape((rows, N_CTX * 128), bf16),
            shape((count, 256), bf16),
            shape((16,) + cot.shape, bf16),
            shape((8,) + wd_own.shape, bf16),
        ],
        in_specs=[VMEM] * 3 + [SMEM] + [ANY] * 2,
        out_specs=[ANY] * 4,
        scratch_shapes=[
            pltpu.VMEM((N_CTX, rows, 256), bf16),
            pltpu.VMEM((count, 256), bf16),
            pltpu.VMEM((4, count, 128), bf16),
            pltpu.VMEM((count, 128), bf16),
        ]
        + [DMA((8,))] * 4
        + [DMA]
        + sem_shapes(PairGather, AxisGather),
        compiler_params=params(2),
    )(h_one, wqkv, freqs, spans, cot, wd_own)


def attend_back(
    grad_routed, gate_back, gates, routed, pack, x_mid, gain, cot, attn_low, wo_full, seq_qkv, freqs, spans, h_all, out_part
):
    rows, width = grad_routed.shape
    count = N_CTX * rows
    own = width // N_EXP
    scatters = [
        out_part,
        jax.ShapeDtypeStruct((16, own, width), bf16),
        jax.ShapeDtypeStruct((16, own, 384), bf16),
    ]

    def kernel(
        gr, gb, gt, ri, pk, xm, gn, u, al, wof, seq, fr, so, h, op, mid, back, moe, wos, alls,
        low_w, low, wo_total, total, payload, wp, ga, grads, heads, acc, dqkv, cos, sin, *rest,
    ):
        here = Here()
        greet(here.ctx_peers() + here.exp_peers())
        bufs, sems = rest[:12], rest[12:]
        arrive = Columns(here, ga, grads, *sems[0:2])
        outs = PairScatter(here, op, moe, *bufs[0:4], *sems[2:7])
        wo = PairScatter(here, wp, wo_total, *bufs[4:8], *sems[7:12])
        proj = PairScatter(here, payload, total, *bufs[8:12], *sems[12:17])
        turn = Turn(here, dqkv, back, *sems[17:19])
        wo_rows = Gather(here, low_w, wos, *sems[19:21])
        all_rows = Gather(here, low, alls, *sems[21:23])
        outs.start()
        spot = lax.broadcasted_iota(jnp.int32, (16 * 8, 128), 0)
        lane = lax.broadcasted_iota(jnp.int32, (16 * 8, 128), 1)
        picks = jnp.where(jnp.logical_and(spot % 8 < 2, spot // 8 * 2 + spot % 8 == lane), 1.0, 0.0)
        exact = functools.partial(
            lax.dot_general, dimension_numbers=(TN, ((), ())), precision=lax.Precision.HIGHEST, preferred_element_type=f32
        )
        grad_gates = exact(gb[...].reshape(16 * 8, rows), picks)
        weighted = gt[...] * grad_gates
        grad_logits = (weighted - gt[...] * jnp.sum(weighted, axis=-1, keepdims=True)).astype(bf16)
        routed_grad = gr[...] + dot(grad_logits, pk[...], NT)
        values = xm[...]
        factor = factor_of(values)
        grad_mid = u[...].astype(f32) + normalize_back(values, factor, gn[...], routed_grad)
        mid[...] = grad_mid
        branch = grad_mid.astype(bf16)
        ga[...] = dot(branch, wof[...], NT).astype(bf16)
        arrive.start()
        wp[...] = dot(al[...], branch, TN).astype(bf16).reshape(16, own, width)
        wo.start()
        column = (lax.broadcasted_iota(jnp.int32, (rows, 128), 1) == 32).astype(f32)
        small = dot(ri[...], grad_logits, TN) + exact(routed_grad * values * factor, column)
        payload[:, :, 256:] = small.astype(bf16).reshape(16, own, 128)
        pr = place_row(so)
        cos[...], sin[...] = tables(place_column(so, 0, count), fr[...])
        for i, part in enumerate(split_heads(seq[:, 128:])):
            heads[i] = part
        acc[...] = jnp.zeros_like(acc)
        arrive.wait()
        wo.pass_on()
        outs.pass_on()

        def step(b, carry):
            at = pl.ds(pl.multiple_of(b * QROWS, QROWS), QROWS)
            visible = pr <= place_column(so, b * (QROWS // SPAN), QROWS)
            q, g = seq[at, :128], grads[at]
            dq = jnp.zeros((QROWS, 128), f32)
            for i in range(2):
                probs = probs_of(q, heads[i], visible)
                grad_probs = dot(g, heads[2 + i], NT)
                inner = jnp.sum(probs * grad_probs, axis=-1, keepdims=True)
                grad_scores = (probs * (grad_probs - inner)).astype(bf16)
                dq += dot(grad_scores, heads[i])
                acc[i] += dot(grad_scores, q, TN)
                acc[2 + i] += dot(probs.astype(bf16), g, TN)
            dq = dq * SCALE
            dqkv[at, :128] = (dq * cos[at] - swap_of(dq * sin[at])).astype(bf16)
            return carry

        lax.fori_loop(0, count // QROWS, step, 0)
        left = left_lanes((count, 128))
        dk = (acc[0] + pltpu.roll(acc[1], HEAD_SIZE, 1)) * SCALE
        dv = pltpu.roll(acc[2], HEAD_SIZE, 1) + acc[3]
        dk = dk * cos[...] - swap_of(dk * sin[...])
        dqkv[:, 128:] = jnp.where(left, dk, dv).astype(bf16)
        turn.start()
        wo.cross()
        outs.cross()
        payload[:, :, :256] = dot(h[...], dqkv[...], TN).astype(bf16).reshape(16, own, 256)
        proj.start()
        wo.wait()
        low_w[...] = wo_total[...].astype(bf16)
        wo_rows.start()
        proj.pass_on()
        proj.cross()
        proj.wait()
        low[...] = total[...].astype(bf16)
        all_rows.start()
        outs.wait()
        turn.wait()
        wo_rows.wait()
        all_rows.wait()

    return pl.pallas_call(
        kernel,
        out_shape=[
            shape((rows, width), f32),
            shape((rows, N_CTX * 256), bf16),
            shape((rows, width), f32),
            shape((8, own, width), bf16),
            shape((8, own, 384), bf16),
        ],
        in_specs=[VMEM] * 12 + [SMEM, VMEM, ANY],
        out_specs=[VMEM, ANY, VMEM, ANY, ANY],
        scratch_shapes=[
            pltpu.VMEM((own, width), bf16),
            pltpu.VMEM((own, 384), bf16),
            pltpu.VMEM((own, width), f32),
            pltpu.VMEM((own, 384), f32),
            pltpu.VMEM((16, own, 384), bf16),
            pltpu.VMEM((16, own, width), bf16),
            pltpu.VMEM((rows, width), bf16),
            pltpu.VMEM((count, 128), bf16),
            pltpu.VMEM((4, count, 128), bf16),
            pltpu.VMEM((4, count, 128), f32),
            pltpu.VMEM((count, 256), bf16),
            pltpu.VMEM((count, 128), f32),
            pltpu.VMEM((count, 128), f32),
        ]
        + [b for x in scatters for b in PairScatter.scratch(x)]
        + sem_shapes(Columns, PairScatter, PairScatter, PairScatter, Turn, Gather, Gather),
        compiler_params=pltpu.CompilerParams(collective_id=4, has_side_effects=True, vmem_limit_bytes=54 * 2**20),
    )(
        grad_routed, gate_back, gates, routed, pack, x_mid, gain, cot, attn_low, wo_full, seq_qkv, freqs, spans, h_all,
        out_part,
    )


def finish_tokens(
    back, wqkv, tokens, gain, grad_mid, x_mid, moe_out, owned, wo_sums, w_query, key_matrix, value_matrix, norm_attn
):
    rows, width = tokens.shape
    own = w_query.shape[0]

    def kernel(
        back, wqkv, x, gain, mid, xm, moe, owned, wos, wq, wk, wv, norm,
        result, grad, gq, gk, gv, go, tail, ga,
    ):
        result[...] = (xm[...] + moe[...]).astype(bf16)
        values = x[...].astype(f32)
        factor = factor_of(values)
        grad[...] = mid[...] + normalize_back(values, factor, gain[...], dot(back[...], wqkv[...], NT))
        left = left_lanes((own, 128))
        rest = jnp.zeros((own, 128), f32)
        sums = jnp.zeros((own, 128), f32)
        for i in range(N_CTX):
            block = owned[i, :, :128].astype(f32)
            at = slice(128 * i, 128 * (i + 1))
            gq[:, at] = block
            sums += block * wq[:, at].astype(f32)
            rest += owned[i, :, 256:].astype(f32)
        for i in range(N_CTX // 2):
            one, two = owned[2 * i, :, 128:256].astype(f32), owned[2 * i + 1, :, 128:256].astype(f32)
            at = slice(128 * i, 128 * (i + 1))
            keys = jnp.where(left, one, pltpu.roll(two, HEAD_SIZE, 1))
            vals = jnp.where(left, pltpu.roll(one, HEAD_SIZE, 1), two)
            gk[:, at] = keys
            gv[:, at] = vals
            sums += keys * wk[:, at].astype(f32) + vals * wv[:, at].astype(f32)
        tail[...] = rest
        ga[...] = jnp.broadcast_to(jnp.sum(sums, axis=1, keepdims=True) / norm[...].astype(f32), (own, 128))
        total = wos[0].astype(f32)
        for i in range(1, N_CTX):
            total += wos[i].astype(f32)
        go[...] = total

    args = (
        back, wqkv, tokens, gain, grad_mid, x_mid, moe_out, owned, wo_sums, w_query, key_matrix, value_matrix,
        norm_attn[:, None],
    )
    return pl.pallas_call(
        kernel,
        out_shape=[
            shape((rows, width), bf16),
            shape((rows, width), f32),
            shape((own, width), f32),
            shape((own, width // 2), f32),
            shape((own, width // 2), f32),
            shape((own, width), f32),
            shape((own, 128), f32),
            shape((own, 128), f32),
        ],
        in_specs=[VMEM] * len(args),
        out_specs=[VMEM] * 8,
        compiler_params=pltpu.CompilerParams(vmem_limit_bytes=40 * 2**20),
    )(*args)


def finish_experts(shares):
    rows = shares.shape[0] * 2 // 3
    f = shares.shape[1] // 4

    def kernel(x, gg, gu, gd):
        for i in range(2):
            gg[i] = x[:rows, f * i : f * (i + 1)].astype(f32)
            gu[i] = x[:rows, f * (2 + i) : f * (3 + i)].astype(f32)
            gd[i] = x[rows:, 2 * f * i : 2 * f * (i + 1)].astype(f32)

    return pl.pallas_call(
        kernel,
        out_shape=[shape((2, rows, f), f32), shape((2, rows, f), f32), shape((2, rows // 2, 2 * f), f32)],
        in_specs=[VMEM],
        out_specs=[VMEM] * 3,
        compiler_params=pltpu.CompilerParams(vmem_limit_bytes=20 * 2**20),
    )(shares)


def body(
    tokens, cotangent, span_order, expert_choice, norm_attn, w_query, key_matrix, value_matrix,
    w_out, norm_moe, w_router, w_gate, w_up, w_down,
):
    c = lax.axis_index("ctx")
    tokens, cotangent, choice = tokens[0], cotangent[0], expert_choice[0]
    rows, width = tokens.shape
    own_rows = w_query.shape[0]
    wgu_own = jnp.concatenate([w_gate[0], w_gate[1], w_up[0], w_up[1]], axis=1)
    wd_own = jnp.concatenate([w_down[0], w_down[1]], axis=1)
    wqkv_own = jnp.concatenate(
        [
            w_query.reshape(own_rows, N_CTX, 128),
            key_matrix.reshape(own_rows, N_CTX, 64),
            value_matrix.reshape(own_rows, N_CTX, 64),
        ],
        axis=2,
    ).reshape(own_rows, N_CTX * 256)
    pack = jnp.pad(w_router, ((0, 0), (0, 128 - 32)))
    gains = jnp.stack([norm_attn, norm_moe])
    odd = lax.axis_index("exp") % 2
    gains = jnp.concatenate([jnp.where(odd == 0, gains, 0.0), jnp.where(odd == 1, gains, 0.0)], axis=1)
    gains = jnp.pad(gains, ((0, 14), (0, 0)))
    wgu_all, wqkv, pack_all, gains, wo = start_exchange(wgu_own, wqkv_own, pack, gains, w_out)
    wgu_all = wgu_all.reshape(width, 4 * w_gate.shape[2])
    wqkv = wqkv.reshape(width, N_CTX * 256)
    pack_all = pack_all.reshape(width, 128)
    wo = wo.reshape(width, width)
    gains = jnp.sum(gains[:, :2].astype(f32).reshape(8, 2, 2, 128), axis=1).transpose(1, 0, 2).reshape(2, width)
    gain_a, gain_m = gains[0:1], gains[1:2]
    lanes = jnp.arange(256, dtype=jnp.int32)
    freqs = rope_base ** (-((lanes % HALF).astype(f32) * 2.0 / HEAD_SIZE))
    freqs = jnp.where(lanes < 192, freqs, 0.0)[None, :]
    inputs = tokens.astype(f32)
    h_one = (inputs * factor_of(inputs) * gain_a).astype(bf16)
    attn_low, seq_qkv, up_all, wd_all = attend(h_one, wqkv, freqs, span_order, cotangent, wd_own)
    x_mid = inputs + dot(attn_low, wo)
    routed_in = (x_mid * factor_of(x_mid) * gain_m).astype(bf16)
    logits = dot(routed_in, pack_all)
    expert_ids = jnp.arange(128, dtype=jnp.int32)
    chosen = jnp.any(choice[:, :, None] == expert_ids[None, None, :], axis=1)
    masked = jnp.where(chosen, logits, neg_big)
    lifted = jnp.where(chosen, jnp.exp(masked - jnp.max(masked, axis=-1, keepdims=True)), 0.0)
    gates = lifted / jnp.sum(lifted, axis=-1, keepdims=True)
    out_part, grad_routed, gate_back, grad_weights = experts(routed_in, gates[:, :32].T, up_all, wgu_all, wd_all)
    h_late, _ = lax.optimization_barrier((h_one, attn_low))
    h_all = lax.all_gather(h_late, "ctx", axis=0, tiled=True)
    shares = lax.psum_scatter(grad_weights, "ctx", scatter_dimension=0, tiled=True)[0]
    grad_mid, back, moe_out, wo_sums, owned = attend_back(
        grad_routed, gate_back, gates, routed_in, pack_all, x_mid, gain_m, cotangent, attn_low, wo, seq_qkv,
        freqs[:, :128], span_order, h_all, out_part,
    )
    result, grad_tokens, out_wq, out_wk, out_wv, out_wo, tail, out_gain_a = finish_tokens(
        back, wqkv, tokens, gain_a, grad_mid, x_mid, moe_out, owned, wo_sums, w_query, key_matrix, value_matrix, norm_attn
    )
    out_wg, out_wu, out_wd = finish_experts(shares)
    return (
        result[None],
        grad_tokens[None],
        out_gain_a[:, 0],
        out_wq,
        out_wk,
        out_wv,
        out_wo,
        tail[:, 32],
        tail[:, :32],
        out_wg,
        out_wu,
        out_wd,
    )


def solution(mesh):
    return jax.shard_map(
        body,
        mesh=mesh,
        in_specs=(
            P("exp", "ctx", None),
            P("exp", "ctx", None),
            P(),
            P("exp", "ctx", None),
            P("exp"),
            P("exp", None),
            P("exp", None),
            P("exp", None),
            P("exp", None),
            P("exp"),
            P("exp", None),
            P("exp", "ctx", None),
            P("exp", "ctx", None),
            P("exp", "ctx", None),
        ),
        out_specs=(
            P("exp", "ctx", None),
            P("exp", "ctx", None),
            P("exp"),
            P("exp", None),
            P("exp", None),
            P("exp", None),
            P("exp", None),
            P("exp"),
            P("exp", None),
            P("exp", "ctx", None),
            P("exp", "ctx", None),
            P("exp", "ctx", None),
        ),
        check_vma=False,
    )
```

```python
import functools

import jax
import jax.numpy as jnp
from jax import lax
from jax.experimental import pallas as pl
from jax.experimental.pallas import tpu as pltpu
from jax.sharding import PartitionSpec as P

HEAD_SIZE = 64
HALF = 32
N_CTX = 8
N_EXP = 16
eps_norm = 1e-06
rope_base = 10000.0
neg_big = -1e30
f32, bf16 = jnp.float32, jnp.bfloat16

MESH = pl.DeviceIdType.MESH
ANY = pl.BlockSpec(memory_space=pl.ANY)
HBM = pl.BlockSpec(memory_space=pltpu.HBM)
VMEM = pl.BlockSpec(memory_space=pltpu.VMEM)
DMA = pltpu.SemaphoreType.DMA
NEAR_LAST = (6, 5, 7, 2, 4, 1, 3)
NEAR_FIRST = (1, 3, 2, 4, 5, 7, 6)
CTX_ORDER = (2, 6, 4, 1, 3, 5, 7)


def remote(src, dst, send, recv, where):
    return pltpu.make_async_remote_copy(
        src_ref=src, dst_ref=dst, send_sem=send, recv_sem=recv, device_id=where, device_id_type=MESH
    )


def greet(places, amount=None):
    barrier = pltpu.get_barrier_semaphore()
    for where in places:
        pl.semaphore_signal(barrier, inc=1, device_id=where, device_id_type=MESH)
    pl.semaphore_wait(barrier, len(places) if amount is None else amount)


class Here:
    def __init__(self):
        self.c = lax.axis_index("ctx")
        self.e = lax.axis_index("exp")
        self.core = lax.rem(self.e, 2)
        self.chip = self.e // 2
        self.partner = {"exp": self.e + 1 - 2 * self.core}

    def ctx(self, k):
        return lax.rem(self.c + k, N_CTX)

    def chip_at(self, k):
        return 4 * lax.rem(self.chip // 4 + k // 4, 2) + lax.rem(lax.rem(self.chip, 4) + lax.rem(k, 4), 4)

    def chip_from(self, k):
        return 4 * lax.rem(self.chip // 4 + k // 4, 2) + lax.rem(lax.rem(self.chip, 4) + 4 - lax.rem(k, 4), 4)

    def turn(self, k):
        k = k + k // 3 - 2 * (k // 4) + k // 5 - k // 6
        m = lax.rem(k, 4)
        return k // 4, m + m // 2 - 2 * (m // 3)

    def turn_at(self, k):
        z, y = self.turn(k)
        return 4 * lax.rem(self.chip // 4 + z, 2) + lax.rem(lax.rem(self.chip, 4) + y, 4)

    def turn_from(self, k):
        z, y = self.turn(k)
        return 4 * lax.rem(self.chip // 4 + z, 2) + lax.rem(lax.rem(self.chip, 4) + 4 - y, 4)

    def ctx_peers(self):
        return [{"ctx": self.ctx(k)} for k in range(1, N_CTX)]

    def same_core(self, k):
        return {"exp": 2 * self.chip_at(k) + self.core}

    def exp_peers(self):
        return [self.partner] + [self.same_core(k) for k in range(1, 8)]

    def other_core_peers(self):
        return [{"exp": 2 * self.chip_at(k) + 1 - self.core} for k in range(1, 8)]


class Gather:
    sems = (8, 8)

    def __init__(self, here, x, out, send, recv):
        self.copies = [pltpu.make_async_copy(x, out.at[here.c], send.at[0])]
        for k in CTX_ORDER:
            self.copies.append(remote(x, out.at[here.c], send.at[k], recv.at[k], {"ctx": here.ctx(k)}))

    def start(self):
        for c in self.copies:
            c.start()

    def wait(self):
        for c in self.copies:
            c.wait()


class AxisGather:
    sems = (8, 8)

    def __init__(self, here, x, out, send, recv):
        c = here.c
        self.own = pltpu.make_async_copy(x, out.at[c], send.at[0])
        across = lax.rem(c + 4, 8)
        self.across = remote(x, out.at[c], send.at[4], recv.at[4], {"ctx": across})
        self.near, self.rest = [], []
        for k in (2, 1, 3):
            peer = {"ctx": c // 4 * 4 + lax.rem(lax.rem(c, 4) + k, 4)}
            self.near.append(remote(x, out.at[c], send.at[k], recv.at[k], peer))
            self.rest.append(remote(out.at[across], out.at[across], send.at[4 + k], recv.at[4 + k], peer))

    def start(self):
        self.across.start()
        for copy in self.near:
            copy.start()
        self.own.start()

    def cross(self):
        self.across.wait_recv()
        for copy in self.rest:
            copy.start()

    def wait(self):
        self.own.wait()
        self.across.wait_send()
        for copy in self.near + self.rest:
            copy.wait()


class AxisScatter:
    sems = (2, 8, 8)

    @staticmethod
    def scratch(x):
        one = x.shape[1:]
        return [pltpu.VMEM((2,) + one, x.dtype), pltpu.VMEM((8,) + one, x.dtype), pltpu.VMEM(one, x.dtype)]

    def __init__(self, here, x, total, mine, far, summed, load, send, recv):
        c = here.c
        across = lax.rem(c + 4, 8)
        self.mine, self.far, self.summed, self.total = mine, far, summed, total
        self.loads = [pltpu.make_async_copy(x.at[j], mine.at[i], load.at[i]) for i, j in enumerate((c, across))]
        self.copies = []
        for z in (1, 0):
            for k in (2, 1, 3):
                peer = c // 4 * 4 + lax.rem(lax.rem(c, 4) + k, 4)
                i = 4 * z + k
                block = lax.rem(peer + 4 * z, 8)
                self.copies.append(remote(x.at[block], far.at[i], send.at[i], recv.at[i], {"ctx": peer}))
        self.over = remote(summed, far.at[4], send.at[4], recv.at[4], {"ctx": across})

    def start(self):
        for copy in self.loads + self.copies:
            copy.start()

    def cross(self):
        for copy in self.loads:
            copy.wait()
        for copy in self.copies:
            copy.wait_recv()
        both = self.mine[1].astype(f32)
        for k in (5, 6, 7):
            both += self.far[k].astype(f32)
        self.summed[...] = both.astype(bf16)
        self.over.start()
        both = self.mine[0].astype(f32)
        for k in (1, 2, 3):
            both += self.far[k].astype(f32)
        self.total[...] = both

    def wait(self):
        self.over.wait_recv()
        self.total[...] += self.far[4].astype(f32)
        self.over.wait_send()
        for copy in self.copies:
            copy.wait_send()


class Turn:
    sems = (8, 8)

    def __init__(self, here, x, out, send, recv):
        rows, cols = out.shape[0], x.shape[1]
        into = out.at[:, pl.ds(pl.multiple_of(here.c * cols, cols), cols)]

        def part(j):
            return x.at[pl.ds(pl.multiple_of(j * rows, rows), rows)]

        self.copies = [pltpu.make_async_copy(part(here.c), into, send.at[0])]
        for k in CTX_ORDER:
            j = here.ctx(k)
            self.copies.append(remote(part(j), into, send.at[k], recv.at[k], {"ctx": j}))

    start = Gather.start
    wait = Gather.wait


class Columns:
    sems = (8, 8)

    def __init__(self, here, x, out, send, recv):
        rows, cols = x.shape[0], out.shape[1]
        into = out.at[pl.ds(pl.multiple_of(here.c * rows, rows), rows)]

        def part(j):
            return x.at[:, pl.ds(pl.multiple_of(j * cols, cols), cols)]

        self.copies = [pltpu.make_async_copy(part(here.c), into, send.at[0])]
        for k in CTX_ORDER:
            j = here.ctx(k)
            self.copies.append(remote(part(j), into, send.at[k], recv.at[k], {"ctx": j}))

    start = Gather.start
    wait = Gather.wait


class PairGather:
    sems = (8, 8, 8, 8)

    def __init__(self, here, x, out, send, recv, fsend, frecv):
        e = here.e
        self.own = pltpu.make_async_copy(x, out.at[e], fsend.at[0])
        self.first = remote(x, out.at[e], send.at[0], recv.at[0], here.partner)
        self.far, self.forward = {}, {}
        across = out.at[2 * here.chip_at(4) + here.core]
        for k in range(1, 8):
            if k <= 4:
                self.far[k] = remote(x, out.at[e], send.at[k], recv.at[k], here.same_core(k))
            else:
                self.far[k] = remote(across, across, send.at[k], recv.at[k], here.same_core(k - 4))
            slot = 2 * here.chip_from(k) + here.core
            self.forward[k] = remote(out.at[slot], out.at[slot], fsend.at[k], frecv.at[k], here.partner)

    def start(self):
        for k in (4, 2, 1, 3):
            self.far[k].start()
        self.first.start()
        self.own.start()

    def cross(self):
        self.far[4].wait_recv()
        for k in (6, 5, 7):
            self.far[k].start()
        self.forward[4].start()

    def pass_on(self):
        for k in (1, 3, 2, 5, 7, 6):
            self.far[k].wait_recv()
            self.forward[k].start()

    def wait(self):
        self.own.wait()
        self.first.wait()
        for k in range(1, 8):
            self.far[k].wait_send()
            self.forward[k].wait()


class PairScatter:
    sems = (8, 8, 8, 8, 8)

    @staticmethod
    def scratch(x):
        return [pltpu.VMEM((8,) + x.shape[1:], x.dtype)] * 4

    def __init__(self, here, x, total, mine, near, summed, far, load, nsend, nrecv, fsend, frecv):
        self.total, self.mine, self.near, self.summed, self.far = total, mine, near, summed, far
        self.loads, self.nears, self.fars = {}, {}, {}
        self.order = (6, 2, 5, 1, 7, 3, 4, 0)
        for k in self.order:
            there = here.chip_at(k)
            self.nears[k] = remote(x.at[2 * there + 1 - here.core], near.at[k], nsend.at[k], nrecv.at[k], here.partner)
            self.loads[k] = pltpu.make_async_copy(x.at[2 * there + here.core], mine.at[k], load.at[k])
            if k:
                where = here.same_core(k if k <= 4 else k - 4)
                self.fars[k] = remote(summed.at[k], far.at[k], fsend.at[k], frecv.at[k], where)

    def start(self):
        for k in self.order:
            self.nears[k].start()
            self.loads[k].start()

    def pass_on(self):
        for k in self.order:
            self.loads[k].wait()
            self.nears[k].wait_recv()
            both = self.mine[k].astype(f32) + self.near[k].astype(f32)
            if k == 0:
                self.total[...] = both
            else:
                self.summed[k] = both.astype(self.summed.dtype)
                if k != 4:
                    self.fars[k].start()

    def cross(self):
        for k in (5, 7, 6):
            self.fars[k].wait_recv()
        both = self.summed[4].astype(f32) + self.far[5].astype(f32)
        both += self.far[6].astype(f32) + self.far[7].astype(f32)
        self.summed[4] = both.astype(self.summed.dtype)
        self.fars[4].start()

    def wait(self):
        for k in (1, 3, 2, 4):
            self.fars[k].wait_recv()
            self.total[...] += self.far[k].astype(f32)
        for k in self.order:
            self.nears[k].wait_send()
            if k:
                self.fars[k].wait_send()


class Spread:
    sems = (16, 16)

    def __init__(self, here, x, out, send, recv):
        self.copies = [pltpu.make_async_copy(x.at[here.e], out.at[here.e], send.at[0])]
        for k in range(1, N_EXP):
            j = lax.rem(here.e + k, N_EXP)
            self.copies.append(remote(x.at[j], out.at[here.e], send.at[k], recv.at[k], {"exp": j}))

    start = Gather.start
    wait = Gather.wait


def sem_shapes(*kinds):
    return [DMA((n,)) for kind in kinds for n in kind.sems]


def params(cid):
    return pltpu.CompilerParams(collective_id=cid, has_side_effects=True, vmem_limit_bytes=60 * 2**20)


def call(kernel, outs, scratch, cid, *args, out_specs=None):
    return pl.pallas_call(
        kernel,
        out_shape=outs,
        in_specs=[ANY] * len(args),
        out_specs=out_specs or [HBM] * len(outs),
        scratch_shapes=scratch,
        compiler_params=params(cid),
    )(*args)


def shape(s, t):
    return jax.ShapeDtypeStruct(s, t)


def start_exchange(over_ctx, *shards):
    n = len(shards)

    def kernel(*refs):
        here = Here()
        greet(here.exp_peers() + here.ctx_peers())
        ins, outs, sems = refs[: n + 1], refs[n + 1 : 2 * n + 2], refs[2 * n + 2 :]
        items = [PairGather(here, ins[i + 1], outs[i + 1], *sems[4 * i + 2 : 4 * i + 6]) for i in range(n)]
        rows = AxisGather(here, ins[0], outs[0], *sems[0:2])
        for i in items:
            i.start()
        rows.start()
        for i in items:
            i.cross()
        rows.cross()
        for i in items:
            i.pass_on()
        for i in items:
            i.wait()
        rows.wait()

    return call(
        kernel,
        [shape((8,) + over_ctx.shape, over_ctx.dtype)] + [shape((16,) + a.shape, a.dtype) for a in shards],
        sem_shapes(AxisGather, *[PairGather] * n),
        1,
        over_ctx,
        *shards,
    )


def dot(a, b, dims=((1,), (0,))):
    return lax.dot_general(a, b, (dims, ((), ())), preferred_element_type=f32)


NT = ((1,), (1,))
TN = ((0,), (0,))


def factor_of(values):
    return lax.rsqrt(jnp.mean(values * values, axis=-1, keepdims=True) + eps_norm)


def normalize_back(values, factor, gain, upstream):
    scaled = upstream * gain
    inner = jnp.mean(scaled * values, axis=-1, keepdims=True)
    return factor * scaled - values * factor * factor * factor * inner


def experts(routed, gates, up_all, wgu_all, wd_all, h_one):
    rows, width = routed.shape
    both = 2 * rows
    f = wd_all.shape[2] // 2 * 8 * wd_all.shape[1] // width
    hid = 2 * f
    chunk = 256

    def kernel(
        x, g, u, wg, wdown, ho, out_part, total, gback, dwgu, dwd, hs,
        dparts, dmine, dfar, dsum, xs, gs, up, wgu, wd, usem, wsem, parts, near, summed, far, hg, dgu, gparts,
        xsend, xrecv, xfsend, xfrecv, gsend, grecv, gfsend, gfrecv,
        nsend, nrecv, rsend, rrecv, hsend, hrecv, dload, dsend, drecv, psend, precv,
    ):
        here = Here()
        core, e = here.core, here.e
        greet(here.exp_peers() + here.other_core_peers() + here.ctx_peers())
        rows_h = AxisGather(here, ho, hs, hsend, hrecv)
        down = AxisScatter(here, dparts, dwd, dmine, dfar, dsum, dload, dsend, drecv)
        own = [
            pltpu.make_async_copy(g, gs.at[e], gfsend.at[0]),
            pltpu.make_async_copy(x, xs.at[e], xfsend.at[0]),
            pltpu.make_async_copy(u, up, usem),
        ]
        own.append(pltpu.make_async_copy(wg, wgu, wsem.at[16]))
        for j in range(8):
            for i in range(2):
                own.append(
                    pltpu.make_async_copy(
                        wdown.at[j, :, pl.ds(width * i, width)],
                        wd.at[pl.ds(f * i + rows // 2 * j, rows // 2)],
                        wsem.at[2 * j + i],
                    )
                )
        first = [
            remote(g, gs.at[e], gsend.at[0], grecv.at[0], here.partner),
            remote(x, xs.at[e], xsend.at[0], xrecv.at[0], here.partner),
        ]
        for copy in own + first:
            copy.start()

        def away(k):
            return [
                remote(g, gs.at[e], gsend.at[k], grecv.at[k], {"exp": 2 * here.turn_at(k) + core}),
                remote(x, xs.at[e], xsend.at[k], xrecv.at[k], {"exp": 2 * here.turn_at(k) + core}),
            ]

        def pass_on(k):
            slot = 2 * here.turn_from(k) + core
            return [
                remote(gs.at[slot], gs.at[slot], gfsend.at[k], gfrecv.at[k], here.partner),
                remote(xs.at[slot], xs.at[slot], xfsend.at[k], xfrecv.at[k], here.partner),
            ]

        def to_partner(k):
            return remote(parts.at[k, 1 - core], near.at[k], nsend.at[k], nrecv.at[k], here.partner)

        def to_chip(k):
            where = {"exp": 2 * here.turn_from(k) + core}
            return remote(summed.at[k], far.at[k], rsend.at[k], rrecv.at[k], where)

        def gate_part(j):
            return remote(gparts.at[j], gback.at[e], psend.at[j], precv.at[e], {"exp": j})

        for k in range(1, 4):
            for copy in away(jnp.int32(k)):
                copy.start()
        rows_h.start()

        picks = lax.broadcasted_iota(jnp.int32, (32, 2 * 128), 0) == 2 * e + (
            lax.broadcasted_iota(jnp.int32, (32, 2 * 128), 1) // 128
        )
        picks = picks.astype(f32)

        def finish(k):
            to_partner(k).wait_recv()
            both_cores = parts[k, core].astype(f32) + near[k].astype(f32)

            @pl.when(k == 0)
            def _():
                total[...] = both_cores

            @pl.when(k > 0)
            def _():
                summed[k] = both_cores.astype(bf16)
                to_chip(k).start()

        def step(k, carry):
            @pl.when(k < 4)
            def _():
                for copy in away(k + 4):
                    copy.start()

            @pl.when(k == 0)
            def _():
                for copy in own:
                    copy.wait()
                for copy in first:
                    copy.wait_recv()

            @pl.when(k > 0)
            def _():
                for copy in pass_on(k):
                    copy.wait_recv()

            chip = here.turn_from(k)
            at = pl.ds(pl.multiple_of(chip * both, both), both)
            xb = xs[pl.ds(2 * chip, 2)].reshape(both, width)
            ub = up[pl.ds(2 * chip, 2)].reshape(both, width)
            gate_cols = jnp.concatenate(
                [
                    lax.dot_general(
                        gs[2 * chip + i], picks, (TN, ((), ())), precision=lax.Precision.HIGHEST,
                        preferred_element_type=f32,
                    )
                    for i in range(2)
                ],
                axis=0,
            )
            gate_sums = jnp.zeros((8, both), f32)
            for i in range(2):
                gate = jnp.concatenate([gate_cols[:, 128 * i : 128 * (i + 1)]] * (chunk // 128), axis=1)
                to_row = (lax.broadcasted_iota(jnp.int32, (8, chunk), 0) == i).astype(bf16)
                for j in range(i * f, (i + 1) * f, chunk):
                    cols, up_cols = pl.ds(j, chunk), pl.ds(hid + j, chunk)
                    gate_h = dot(xb, wgu[:, cols])
                    up_h = dot(xb, wgu[:, up_cols])
                    back = dot(ub, wd[cols], NT)
                    sig = 1.0 / (1.0 + jnp.exp(-gate_h))
                    silu = gate_h * sig
                    hidden = silu * up_h
                    hg[at, cols] = (hidden * gate).astype(bf16)
                    gate_sums += dot(to_row, (hidden * back).astype(bf16), NT)
                    grad_hidden = back * gate
                    dgu[at, cols] = (grad_hidden * up_h * (sig * (1.0 + gate_h * (1.0 - sig)))).astype(bf16)
                    dgu[at, up_cols] = (grad_hidden * silu).astype(bf16)
            for i in range(2):
                gparts[2 * chip + i] = gate_sums[:, rows * i : rows * (i + 1)]
            parts[k] = dot(dgu[at], wgu[...], NT).astype(bf16).reshape(2, rows, width)
            to_partner(k).start()
            gate_part(2 * chip + 1 - core).start()

            @pl.when(k < 7)
            def _():
                for copy in away(k + 1):
                    copy.wait_recv()
                for copy in pass_on(k + 1):
                    copy.start()

            @pl.when(k > 0)
            def _():
                gate_part(2 * chip + core).start()

            @pl.when(k > 0)
            def _():
                finish(k - 1)

            return carry

        lax.fori_loop(0, 8, step, 0)
        mine = pltpu.make_async_copy(gparts.at[e], gback.at[e], psend.at[e])
        mine.start()
        finish(jnp.int32(7))
        rows_h.cross()

        def down_rows(i, carry):
            at = pl.ds(pl.multiple_of(i * 256, 256), 256)
            grads = dot(hg[:, at], up[...].reshape(16 * rows, width), TN).astype(bf16)
            cols = pl.ds(pl.multiple_of((i // 2) * width, width), width)
            dparts[pl.ds(4 * lax.rem(i, 2), 4), :, cols] = grads.reshape(4, rows // 2, width)
            return carry

        lax.fori_loop(0, hid // 256, down_rows, 0)
        down.start()

        def weight_rows(i, carry):
            at = pl.ds(pl.multiple_of(i * 256, 256), 256)
            columns = xs[:, :, at].reshape(16 * rows, 256)
            grads = dot(columns, dgu[...], TN).astype(bf16)
            dwgu[pl.ds(2 * i, 2)] = grads.reshape(2, rows, 2 * hid)
            return carry

        lax.fori_loop(0, width // 256, weight_rows, 0)

        def outputs(i, carry):
            at = pl.ds(pl.multiple_of(i * 512, 512), 512)
            out_part[pl.ds(512 // rows * i, 512 // rows)] = dot(hg[at], wd[...]).astype(bf16).reshape(512 // rows, rows, width)
            return carry

        lax.fori_loop(0, 16 * rows // 512, outputs, 0)

        def collect(k, carry):
            to_chip(k).wait_recv()
            total[...] += far[k].astype(f32)
            return carry

        lax.fori_loop(1, 8, collect, 0)
        down.cross()
        for copy in first:
            copy.wait_send()
        mine.wait()
        rows_h.wait()

        def drain(k, carry):
            for copy in away(k) + pass_on(k) + [to_partner(k), to_chip(k)]:
                copy.wait_send()
            return carry

        lax.fori_loop(1, 8, drain, 0)
        to_partner(0).wait_send()

        def drain_gates(k, carry):
            j = lax.rem(e + k, N_EXP)
            gate_part(j).wait_send()
            remote(gparts.at[j], gback.at[j], psend.at[j], precv.at[j], {"exp": j}).wait_recv()
            return carry

        lax.fori_loop(1, N_EXP, drain_gates, 0)
        down.wait()

    block = (8, rows, width)
    return pl.pallas_call(
        kernel,
        out_shape=[
            shape((16, rows, width), bf16),
            shape((rows, width), f32),
            shape((16, 8, rows), f32),
            shape((8, rows, 2 * hid), bf16),
            shape((rows // 2, 2 * width), f32),
            shape((8,) + h_one.shape, bf16),
        ],
        in_specs=[ANY] * 6,
        out_specs=[VMEM, VMEM, ANY, VMEM, VMEM, HBM],
        scratch_shapes=[
            pltpu.VMEM((8, rows // 2, 2 * width), bf16),
            *AxisScatter.scratch(shape((8, rows // 2, 2 * width), bf16)),
            pltpu.VMEM((16, rows, width), bf16),
            pltpu.VMEM((16, 32, rows), f32),
            pltpu.VMEM((16, rows, width), bf16),
            pltpu.VMEM((width, 2 * hid), bf16),
            pltpu.VMEM((hid, width), bf16),
            DMA,
            DMA((17,)),
            pltpu.VMEM((8, 2, rows, width), bf16),
            pltpu.VMEM(block, bf16),
            pltpu.VMEM(block, bf16),
            pltpu.VMEM(block, bf16),
            pltpu.VMEM((16 * rows, hid), bf16),
            pltpu.VMEM((16 * rows, 2 * hid), bf16),
            pltpu.VMEM((16, 8, rows), f32),
        ]
        + [DMA((8,))] * 14
        + sem_shapes(AxisScatter)
        + [DMA((16,))] * 2,
        compiler_params=pltpu.CompilerParams(collective_id=3, has_side_effects=True, vmem_limit_bytes=60 * 2**20),
    )(routed, gates, up_all, wgu_all, wd_all, h_one)


SCALE = HEAD_SIZE ** (-0.5)
QROWS = 256
SPAN = 64
SMEM = pl.BlockSpec(memory_space=pltpu.SMEM)


def left_lanes(shape_):
    return lax.broadcasted_iota(jnp.int32, shape_, 1) % 128 < HEAD_SIZE


def split_heads(kv):
    wide = kv.astype(f32)
    turned = pltpu.roll(wide, HEAD_SIZE, 1)
    left = left_lanes(kv.shape)
    return [
        jnp.where(left, wide, 0.0).astype(bf16),
        jnp.where(left, 0.0, turned).astype(bf16),
        jnp.where(left, turned, 0.0).astype(bf16),
        jnp.where(left, 0.0, wide).astype(bf16),
    ]


def place_column(spans, first, count):
    row = lax.broadcasted_iota(jnp.int32, (count, 1), 0)
    base = jnp.zeros((count, 1), jnp.int32)
    for i in range(count // SPAN):
        base = jnp.where(row // SPAN == i, spans[first + i], base)
    return base * SPAN + row % SPAN


def place_row(spans):
    lane = lax.broadcasted_iota(jnp.int32, (1, 16 * SPAN), 1)
    base = jnp.zeros((1, 16 * SPAN), jnp.int32)
    for i in range(16):
        base = jnp.where(lane // SPAN == i, spans[i], base)
    return base * SPAN + lane % SPAN


def tables(places, freqs):
    turned = places.astype(f32) * freqs
    return jnp.cos(turned), jnp.sin(turned)


def probs_of(q, k, visible):
    scores = jnp.where(visible, dot(q, k, NT) * SCALE, neg_big)
    shifted = jnp.exp(scores - jnp.max(scores, axis=-1, keepdims=True))
    return shifted * (1.0 / jnp.sum(shifted, axis=-1, keepdims=True))


def swap_of(v):
    leading = lax.broadcasted_iota(jnp.int32, v.shape, 1) % HEAD_SIZE < HALF
    return jnp.where(leading, -pltpu.roll(v, v.shape[1] - HALF, 1), pltpu.roll(v, HALF, 1))


def attend(h_one, wqkv, freqs, spans, cot, wd_own):
    rows = h_one.shape[0]
    count = N_CTX * rows

    def kernel(
        h, wh, fr, so, u, wd, out, kept, us, wds, w, wsem, stage, seq, heads, attn, send, recv, osend, orecv, ksem, *sems
    ):
        here = Here()
        c = here.c
        load = pltpu.make_async_copy(wh, w, wsem)
        load.start()
        greet(here.ctx_peers() + here.exp_peers())
        cots = PairGather(here, u, us, *sems[0:4])
        downs = AxisGather(here, wd, wds, *sems[4:6])
        cots.start()
        cos, sin = tables(place_column(so, 2 * c, rows), fr[...])

        def block_rows(ref, j):
            return ref.at[pl.ds(pl.multiple_of(j * rows, rows), rows)]

        def column(j):
            return out.at[:, pl.ds(pl.multiple_of(j * 128, 128), 128)]

        def arrive(j):
            return remote(stage.at[j], block_rows(seq, c), send.at[j], recv.at[c], {"ctx": j})

        def arrive_own():
            return pltpu.make_async_copy(stage.at[c], block_rows(seq, c), send.at[c])

        def project(b, carry):
            j = lax.rem(c + 1 + b, N_CTX)
            p = dot(h[...], w[:, pl.ds(pl.multiple_of(j * 256, 256), 256)])
            stage[j] = (p * cos + swap_of(p) * sin).astype(bf16)

            @pl.when(b < N_CTX - 1)
            def _():
                arrive(j).start()

            return carry

        load.wait()
        lax.fori_loop(0, N_CTX, project, 0)
        arrive_own().start()
        downs.start()
        pr = place_row(so)
        arrive_own().wait()
        for k in range(1, N_CTX):
            j = here.ctx(k)
            arrive(j).wait_send()
            remote(stage.at[j], block_rows(seq, j), send.at[j], recv.at[j], {"ctx": j}).wait_recv()
        keep = pltpu.make_async_copy(seq, kept, ksem)
        keep.start()
        cots.cross()
        downs.cross()
        for i, part in enumerate(split_heads(seq[:, 128:])):
            heads[i] = part

        def leave(j):
            return remote(block_rows(attn, j), column(c), osend.at[j], orecv.at[c], {"ctx": j})

        def local():
            return pltpu.make_async_copy(block_rows(attn, c), column(c), osend.at[c])

        def step(b, carry):
            block = lax.rem(b + c // 2, count // QROWS)
            at = pl.ds(pl.multiple_of(block * QROWS, QROWS), QROWS)
            visible = pr <= place_column(so, block * (QROWS // SPAN), QROWS)
            q = seq[at, :128]
            total = jnp.zeros((QROWS, 128), f32)
            for i in range(2):
                total += dot(probs_of(q, heads[i], visible).astype(bf16), heads[2 + i])
            attn[at] = total.astype(bf16)
            for i in range(QROWS // rows):
                j = block * (QROWS // rows) + i

                @pl.when(j != c)
                def _():
                    leave(j).start()

                @pl.when(j == c)
                def _():
                    local().start()

            return carry

        lax.fori_loop(0, count // QROWS, step, 0)
        cots.pass_on()
        for k in range(1, N_CTX):
            j = here.ctx(k)
            leave(j).wait_send()
            remote(block_rows(attn, c), column(j), osend.at[j], orecv.at[j], {"ctx": j}).wait_recv()
        local().wait()
        keep.wait()
        cots.wait()
        downs.wait()

    return pl.pallas_call(
        kernel,
        out_shape=[
            shape((rows, N_CTX * 128), bf16),
            shape((count, 256), bf16),
            shape((16,) + cot.shape, bf16),
            shape((8,) + wd_own.shape, bf16),
        ],
        in_specs=[VMEM, ANY, VMEM, SMEM] + [ANY] * 2,
        out_specs=[HBM] * 4,
        scratch_shapes=[
            pltpu.VMEM(wqkv.shape, bf16),
            DMA,
            pltpu.VMEM((N_CTX, rows, 256), bf16),
            pltpu.VMEM((count, 256), bf16),
            pltpu.VMEM((4, count, 128), bf16),
            pltpu.VMEM((count, 128), bf16),
        ]
        + [DMA((8,))] * 4
        + [DMA]
        + sem_shapes(PairGather, AxisGather),
        compiler_params=params(2),
    )(h_one, wqkv, freqs, spans, cot, wd_own)


def attend_back(
    grad_routed, gate_back, gates, routed, pack, x_mid, gain, cot, attn_low, wo_full, seq_qkv, freqs, spans, h_all, out_part,
    first_part,
):
    rows, width = grad_routed.shape
    count = N_CTX * rows
    own = width // N_EXP
    scatters = [
        out_part,
        jax.ShapeDtypeStruct((16, own, width), bf16),
        jax.ShapeDtypeStruct((16, own, 384), bf16),
    ]

    def kernel(
        gr, gb, gt, ri, pk, xm, gn, u, al, wof, seq, fr, so, hh, op, dp, mid, back, moe, wos, alls, dwgu, h, hsem,
        low_w, low, wo_total, total, payload, wp, ga, grads, heads, acc, dqkv, cos, sin, *rest,
    ):
        here = Here()
        load = pltpu.make_async_copy(hh, h, hsem)
        load.start()
        greet(here.ctx_peers() + here.exp_peers())
        bufs, sems = rest[:15], rest[15:]
        first = AxisScatter(here, dp, dwgu, *bufs[12:15], *sems[23:26])
        arrive = Columns(here, ga, grads, *sems[0:2])
        outs = PairScatter(here, op, moe, *bufs[0:4], *sems[2:7])
        wo = PairScatter(here, wp, wo_total, *bufs[4:8], *sems[7:12])
        proj = PairScatter(here, payload, total, *bufs[8:12], *sems[12:17])
        turn = Turn(here, dqkv, back, *sems[17:19])
        wo_rows = Gather(here, low_w, wos, *sems[19:21])
        all_rows = Gather(here, low, alls, *sems[21:23])
        outs.start()
        spot = lax.broadcasted_iota(jnp.int32, (16 * 8, 128), 0)
        lane = lax.broadcasted_iota(jnp.int32, (16 * 8, 128), 1)
        picks = jnp.where(jnp.logical_and(spot % 8 < 2, spot // 8 * 2 + spot % 8 == lane), 1.0, 0.0)
        exact = functools.partial(
            lax.dot_general, dimension_numbers=(TN, ((), ())), precision=lax.Precision.HIGHEST, preferred_element_type=f32
        )
        grad_gates = exact(gb[...].reshape(16 * 8, rows), picks)
        weighted = gt[...] * grad_gates
        grad_logits = (weighted - gt[...] * jnp.sum(weighted, axis=-1, keepdims=True)).astype(bf16)
        routed_grad = gr[...] + dot(grad_logits, pk[...], NT)
        values = xm[...]
        factor = factor_of(values)
        grad_mid = u[...].astype(f32) + normalize_back(values, factor, gn[...], routed_grad)
        mid[...] = grad_mid
        branch = grad_mid.astype(bf16)
        ga[...] = dot(branch, wof[...], NT).astype(bf16)
        arrive.start()
        first.start()
        wp[...] = dot(al[...], branch, TN).astype(bf16).reshape(16, own, width)
        wo.start()
        column = (lax.broadcasted_iota(jnp.int32, (rows, 128), 1) == 32).astype(f32)
        small = dot(ri[...], grad_logits, TN) + exact(routed_grad * values * factor, column)
        payload[:, :, 256:] = small.astype(bf16).reshape(16, own, 128)
        pr = place_row(so)
        cos[...], sin[...] = tables(place_column(so, 0, count), fr[...])
        for i, part in enumerate(split_heads(seq[:, 128:])):
            heads[i] = part
        acc[...] = jnp.zeros_like(acc)
        arrive.wait()
        wo.pass_on()
        outs.pass_on()

        def step(b, carry):
            at = pl.ds(pl.multiple_of(b * QROWS, QROWS), QROWS)
            visible = pr <= place_column(so, b * (QROWS // SPAN), QROWS)
            q, g = seq[at, :128], grads[at]
            dq = jnp.zeros((QROWS, 128), f32)
            for i in range(2):
                probs = probs_of(q, heads[i], visible)
                grad_probs = dot(g, heads[2 + i], NT)
                inner = jnp.sum(probs * grad_probs, axis=-1, keepdims=True)
                grad_scores = (probs * (grad_probs - inner)).astype(bf16)
                dq += dot(grad_scores, heads[i])
                acc[i] += dot(grad_scores, q, TN)
                acc[2 + i] += dot(probs.astype(bf16), g, TN)
            dq = dq * SCALE
            dqkv[at, :128] = (dq * cos[at] - swap_of(dq * sin[at])).astype(bf16)
            return carry

        lax.fori_loop(0, count // QROWS, step, 0)
        left = left_lanes((count, 128))
        dk = (acc[0] + pltpu.roll(acc[1], HEAD_SIZE, 1)) * SCALE
        dv = pltpu.roll(acc[2], HEAD_SIZE, 1) + acc[3]
        dk = dk * cos[...] - swap_of(dk * sin[...])
        dqkv[:, 128:] = jnp.where(left, dk, dv).astype(bf16)
        turn.start()
        load.wait()
        payload[:, :, :256] = dot(h[...], dqkv[...], TN).astype(bf16).reshape(16, own, 256)
        proj.start()
        wo.cross()
        proj.pass_on()
        wo.wait()
        low_w[...] = wo_total[...].astype(bf16)
        wo_rows.start()
        proj.cross()
        outs.cross()
        proj.wait()
        low[...] = total[...].astype(bf16)
        all_rows.start()
        outs.wait()
        first.cross()
        turn.wait()
        wo_rows.wait()
        all_rows.wait()
        first.wait()

    return pl.pallas_call(
        kernel,
        out_shape=[
            shape((rows, width), f32),
            shape((rows, N_CTX * 256), bf16),
            shape((rows, width), f32),
            shape((8, own, width), bf16),
            shape((8, own, 384), bf16),
            shape(first_part.shape[1:], f32),
        ],
        in_specs=[VMEM] * 12 + [SMEM, ANY, ANY, ANY],
        out_specs=[VMEM, HBM, VMEM, HBM, HBM, VMEM],
        scratch_shapes=[
            pltpu.VMEM(h_all.shape, bf16),
            DMA,
            pltpu.VMEM((own, width), bf16),
            pltpu.VMEM((own, 384), bf16),
            pltpu.VMEM((own, width), f32),
            pltpu.VMEM((own, 384), f32),
            pltpu.VMEM((16, own, 384), bf16),
            pltpu.VMEM((16, own, width), bf16),
            pltpu.VMEM((rows, width), bf16),
            pltpu.VMEM((count, 128), bf16),
            pltpu.VMEM((4, count, 128), bf16),
            pltpu.VMEM((4, count, 128), f32),
            pltpu.VMEM((count, 256), bf16),
            pltpu.VMEM((count, 128), f32),
            pltpu.VMEM((count, 128), f32),
        ]
        + [b for x in scatters for b in PairScatter.scratch(x)]
        + AxisScatter.scratch(first_part)
        + sem_shapes(Columns, PairScatter, PairScatter, PairScatter, Turn, Gather, Gather, AxisScatter),
        compiler_params=pltpu.CompilerParams(collective_id=4, has_side_effects=True, vmem_limit_bytes=60 * 2**20),
    )(
        grad_routed, gate_back, gates, routed, pack, x_mid, gain, cot, attn_low, wo_full, seq_qkv, freqs, spans, h_all,
        out_part, first_part,
    )


def finish_tokens(
    back, wqkv, tokens, gain, grad_mid, x_mid, moe_out, owned, wo_sums, w_query, key_matrix, value_matrix, norm_attn,
    grad_first, grad_down,
):
    rows, width = tokens.shape
    own = w_query.shape[0]
    f = grad_first.shape[1] // 4
    args = (
        back, wqkv, tokens, gain, grad_mid, x_mid, moe_out, owned, wo_sums, w_query, key_matrix, value_matrix,
        norm_attn[None, :], grad_first, grad_down,
    )

    def kernel(*refs):
        n = len(args)
        ins, (result, grad, gq, gk, gv, go, tail, gm, ga, gg, gu, gd) = refs[:n], refs[n : n + 12]
        held, sems = refs[n + 12 : -1], refs[-1]
        loads = [pltpu.make_async_copy(a, b, sems.at[i]) for i, (a, b) in enumerate(zip(ins, held))]
        for load in loads:
            load.start()
        for load in loads:
            load.wait()
        back, wqkv, x, gain, mid, xm, moe, owned, wos, wq, wk, wv, norm, first, down = held
        for i in range(2):
            gg[i] = first[:, f * i : f * (i + 1)]
            gu[i] = first[:, f * (2 + i) : f * (3 + i)]
            gd[i] = down[:, 2 * f * i : 2 * f * (i + 1)]
        result[...] = (xm[...] + moe[...]).astype(bf16)
        values = x[...].astype(f32)
        factor = factor_of(values)
        grad[...] = mid[...] + normalize_back(values, factor, gain[...], dot(back[...], wqkv[...], NT))
        left = left_lanes((own, 128))
        rest = jnp.zeros((own, 128), f32)
        sums = jnp.zeros((own, 128), f32)
        for i in range(N_CTX):
            block = owned[i, :, :128].astype(f32)
            at = slice(128 * i, 128 * (i + 1))
            gq[:, at] = block
            sums += block * wq[:, at].astype(f32)
            rest += owned[i, :, 256:].astype(f32)
        for i in range(N_CTX // 2):
            one, two = owned[2 * i, :, 128:256].astype(f32), owned[2 * i + 1, :, 128:256].astype(f32)
            at = slice(128 * i, 128 * (i + 1))
            keys = jnp.where(left, one, pltpu.roll(two, HEAD_SIZE, 1))
            vals = jnp.where(left, pltpu.roll(one, HEAD_SIZE, 1), two)
            gk[:, at] = keys
            gv[:, at] = vals
            sums += keys * wk[:, at].astype(f32) + vals * wv[:, at].astype(f32)
        turned = jnp.transpose(rest)
        tail[...] = turned[:32]
        gm[...] = turned[32:33]
        ga[...] = jnp.sum(jnp.transpose(sums), axis=0, keepdims=True) / norm[...].astype(f32)
        total = wos[0].astype(f32)
        for i in range(1, N_CTX):
            total += wos[i].astype(f32)
        go[...] = total

    return pl.pallas_call(
        kernel,
        out_shape=[
            shape((rows, width), bf16),
            shape((rows, width), f32),
            shape((own, width), f32),
            shape((own, width // 2), f32),
            shape((own, width // 2), f32),
            shape((own, width), f32),
            shape((32, own), f32),
            shape((1, own), f32),
            shape((1, own), f32),
            shape((2, rows, f), f32),
            shape((2, rows, f), f32),
            shape((2, rows // 2, 2 * f), f32),
        ],
        in_specs=[ANY] * len(args),
        out_specs=[VMEM] * 12,
        scratch_shapes=[pltpu.VMEM(a.shape, a.dtype) for a in args] + [DMA((len(args),))],
        compiler_params=pltpu.CompilerParams(vmem_limit_bytes=60 * 2**20),
    )(*args)


def body(
    tokens, cotangent, span_order, expert_choice, norm_attn, w_query, key_matrix, value_matrix,
    w_out, norm_moe, w_router, w_gate, w_up, w_down,
):
    c = lax.axis_index("ctx")
    tokens, cotangent, choice = tokens[0], cotangent[0], expert_choice[0]
    rows, width = tokens.shape
    own_rows = w_query.shape[0]
    wgu_own = jnp.concatenate([w_gate[0], w_gate[1], w_up[0], w_up[1]], axis=1)
    wd_own = jnp.concatenate([w_down[0], w_down[1]], axis=1)
    wqkv_own = jnp.concatenate(
        [
            w_query.reshape(own_rows, N_CTX, 128),
            key_matrix.reshape(own_rows, N_CTX, 64),
            value_matrix.reshape(own_rows, N_CTX, 64),
        ],
        axis=2,
    ).reshape(own_rows, N_CTX * 256)
    pack = jnp.pad(w_router, ((0, 0), (0, 128 - 32)))
    gains = jnp.stack([norm_attn, norm_moe])
    odd = lax.axis_index("exp") % 2
    gains = jnp.concatenate([jnp.where(odd == 0, gains, 0.0), jnp.where(odd == 1, gains, 0.0)], axis=1)
    gains = jnp.pad(gains, ((0, 14), (0, 0)))
    wgu_all, wqkv, pack_all, gains, wo = start_exchange(wgu_own, wqkv_own, pack, gains, w_out)
    wgu_all = wgu_all.reshape(width, 4 * w_gate.shape[2])
    wqkv = wqkv.reshape(width, N_CTX * 256)
    pack_all = pack_all.reshape(width, 128)
    wo = wo.reshape(width, width)
    gains = jnp.sum(gains[:, :2].astype(f32).reshape(8, 2, 2, 128), axis=1).transpose(1, 0, 2).reshape(2, width)
    gain_a, gain_m = gains[0:1], gains[1:2]
    lanes = jnp.arange(256, dtype=jnp.int32)
    freqs = rope_base ** (-((lanes % HALF).astype(f32) * 2.0 / HEAD_SIZE))
    freqs = jnp.where(lanes < 192, freqs, 0.0)[None, :]
    inputs = tokens.astype(f32)
    h_one = (inputs * factor_of(inputs) * gain_a).astype(bf16)
    attn_low, seq_qkv, up_all, wd_all = attend(h_one, wqkv, freqs, span_order, cotangent, wd_own)
    x_mid = inputs + dot(attn_low, wo)
    routed_in = (x_mid * factor_of(x_mid) * gain_m).astype(bf16)
    logits = dot(routed_in, pack_all)
    expert_ids = jnp.arange(128, dtype=jnp.int32)
    chosen = jnp.any(choice[:, :, None] == expert_ids[None, None, :], axis=1)
    masked = jnp.where(chosen, logits, neg_big)
    lifted = jnp.where(chosen, jnp.exp(masked - jnp.max(masked, axis=-1, keepdims=True)), 0.0)
    gates = lifted / jnp.sum(lifted, axis=-1, keepdims=True)
    out_part, grad_routed, gate_back, grad_wgu, grad_wd, h_all = experts(
        routed_in, gates[:, :32].T, up_all, wgu_all, wd_all, h_one
    )
    h_all = h_all.reshape(N_CTX * rows, width)
    grad_mid, back, moe_out, wo_sums, owned, grad_first = attend_back(
        grad_routed, gate_back, gates, routed_in, pack_all, x_mid, gain_m, cotangent, attn_low, wo, seq_qkv,
        freqs[:, :128], span_order, h_all, out_part, grad_wgu,
    )
    result, grad_tokens, out_wq, out_wk, out_wv, out_wo, tail, out_gain_m, out_gain_a, out_wg, out_wu, out_wd = finish_tokens(
        back, wqkv, tokens, gain_a, grad_mid, x_mid, moe_out, owned, wo_sums, w_query, key_matrix, value_matrix, norm_attn,
        grad_first, grad_wd,
    )
    return (
        result[None],
        grad_tokens[None],
        out_gain_a[0],
        out_wq,
        out_wk,
        out_wv,
        out_wo,
        out_gain_m[0],
        tail.T,
        out_wg,
        out_wu,
        out_wd,
    )


def solution(mesh):
    return jax.shard_map(
        body,
        mesh=mesh,
        in_specs=(
            P("exp", "ctx", None),
            P("exp", "ctx", None),
            P(),
            P("exp", "ctx", None),
            P("exp"),
            P("exp", None),
            P("exp", None),
            P("exp", None),
            P("exp", None),
            P("exp"),
            P("exp", None),
            P("exp", "ctx", None),
            P("exp", "ctx", None),
            P("exp", "ctx", None),
        ),
        out_specs=(
            P("exp", "ctx", None),
            P("exp", "ctx", None),
            P("exp"),
            P("exp", None),
            P("exp", None),
            P("exp", None),
            P("exp", None),
            P("exp"),
            P("exp", None),
            P("exp", "ctx", None),
            P("exp", "ctx", None),
            P("exp", "ctx", None),
        ),
        check_vma=False,
    )
```

```python
import functools

import jax
import jax.numpy as jnp
from jax import lax
from jax.experimental import pallas as pl
from jax.experimental.pallas import tpu as pltpu
from jax.sharding import PartitionSpec as P

HEAD_SIZE = 64
HALF = 32
N_CTX = 8
N_EXP = 16
eps_norm = 1e-06
rope_base = 10000.0
neg_big = -1e30
f32, bf16 = jnp.float32, jnp.bfloat16

MESH = pl.DeviceIdType.MESH
ANY = pl.BlockSpec(memory_space=pl.ANY)
HBM = pl.BlockSpec(memory_space=pltpu.HBM)
VMEM = pl.BlockSpec(memory_space=pltpu.VMEM)
DMA = pltpu.SemaphoreType.DMA
NEAR_LAST = (6, 5, 7, 2, 4, 1, 3)
NEAR_FIRST = (1, 3, 2, 4, 5, 7, 6)
CTX_ORDER = (2, 6, 4, 1, 3, 5, 7)


def remote(src, dst, send, recv, where):
    return pltpu.make_async_remote_copy(
        src_ref=src, dst_ref=dst, send_sem=send, recv_sem=recv, device_id=where, device_id_type=MESH
    )


def greet(places, amount=None):
    barrier = pltpu.get_barrier_semaphore()
    for where in places:
        pl.semaphore_signal(barrier, inc=1, device_id=where, device_id_type=MESH)
    pl.semaphore_wait(barrier, len(places) if amount is None else amount)


class Here:
    def __init__(self):
        self.c = lax.axis_index("ctx")
        self.e = lax.axis_index("exp")
        self.core = lax.rem(self.e, 2)
        self.chip = self.e // 2
        self.partner = {"exp": self.e + 1 - 2 * self.core}

    def ctx(self, k):
        return lax.rem(self.c + k, N_CTX)

    def chip_at(self, k):
        return 4 * lax.rem(self.chip // 4 + k // 4, 2) + lax.rem(lax.rem(self.chip, 4) + lax.rem(k, 4), 4)

    def chip_from(self, k):
        return 4 * lax.rem(self.chip // 4 + k // 4, 2) + lax.rem(lax.rem(self.chip, 4) + 4 - lax.rem(k, 4), 4)

    def turn(self, k):
        k = k + k // 3 - 2 * (k // 4) + k // 5 - k // 6
        m = lax.rem(k, 4)
        return k // 4, m + m // 2 - 2 * (m // 3)

    def turn_at(self, k):
        z, y = self.turn(k)
        return 4 * lax.rem(self.chip // 4 + z, 2) + lax.rem(lax.rem(self.chip, 4) + y, 4)

    def turn_from(self, k):
        z, y = self.turn(k)
        return 4 * lax.rem(self.chip // 4 + z, 2) + lax.rem(lax.rem(self.chip, 4) + 4 - y, 4)

    def ctx_peers(self):
        return [{"ctx": self.ctx(k)} for k in range(1, N_CTX)]

    def same_core(self, k):
        return {"exp": 2 * self.chip_at(k) + self.core}

    def exp_peers(self):
        return [self.partner] + [self.same_core(k) for k in range(1, 8)]

    def other_core_peers(self):
        return [{"exp": 2 * self.chip_at(k) + 1 - self.core} for k in range(1, 8)]


class Gather:
    sems = (8, 8)

    def __init__(self, here, x, out, send, recv):
        self.copies = [pltpu.make_async_copy(x, out.at[here.c], send.at[0])]
        for k in CTX_ORDER:
            self.copies.append(remote(x, out.at[here.c], send.at[k], recv.at[k], {"ctx": here.ctx(k)}))

    def start(self):
        for c in self.copies:
            c.start()

    def wait(self):
        for c in self.copies:
            c.wait()


class AxisGather:
    sems = (8, 8)

    def __init__(self, here, x, out, send, recv):
        c = here.c
        self.own = pltpu.make_async_copy(x, out.at[c], send.at[0])
        across = lax.rem(c + 4, 8)
        self.across = remote(x, out.at[c], send.at[4], recv.at[4], {"ctx": across})
        self.near, self.rest = [], []
        for k in (2, 1, 3):
            peer = {"ctx": c // 4 * 4 + lax.rem(lax.rem(c, 4) + k, 4)}
            self.near.append(remote(x, out.at[c], send.at[k], recv.at[k], peer))
            self.rest.append(remote(out.at[across], out.at[across], send.at[4 + k], recv.at[4 + k], peer))

    def start(self):
        self.across.start()
        for copy in self.near:
            copy.start()
        self.own.start()

    def cross(self):
        self.across.wait_recv()
        for copy in self.rest:
            copy.start()

    def wait(self):
        self.own.wait()
        self.across.wait_send()
        for copy in self.near + self.rest:
            copy.wait()


class AxisScatter:
    sems = (2, 8, 8)

    @staticmethod
    def scratch(x):
        one = x.shape[1:]
        return [pltpu.VMEM((2,) + one, x.dtype), pltpu.VMEM((8,) + one, x.dtype), pltpu.VMEM(one, x.dtype)]

    def __init__(self, here, x, total, mine, far, summed, load, send, recv):
        c = here.c
        across = lax.rem(c + 4, 8)
        self.mine, self.far, self.summed, self.total = mine, far, summed, total
        self.loads = [pltpu.make_async_copy(x.at[j], mine.at[i], load.at[i]) for i, j in enumerate((c, across))]
        self.copies = []
        for z in (1, 0):
            for k in (2, 1, 3):
                peer = c // 4 * 4 + lax.rem(lax.rem(c, 4) + k, 4)
                i = 4 * z + k
                block = lax.rem(peer + 4 * z, 8)
                self.copies.append(remote(x.at[block], far.at[i], send.at[i], recv.at[i], {"ctx": peer}))
        self.over = remote(summed, far.at[4], send.at[4], recv.at[4], {"ctx": across})

    def start(self):
        for copy in self.loads + self.copies:
            copy.start()

    def cross(self):
        for copy in self.loads:
            copy.wait()
        for copy in self.copies:
            copy.wait_recv()
        both = self.mine[1].astype(f32)
        for k in (5, 6, 7):
            both += self.far[k].astype(f32)
        self.summed[...] = both.astype(bf16)
        self.over.start()
        both = self.mine[0].astype(f32)
        for k in (1, 2, 3):
            both += self.far[k].astype(f32)
        self.total[...] = both

    def wait(self):
        self.over.wait_recv()
        self.total[...] += self.far[4].astype(f32)
        self.over.wait_send()
        for copy in self.copies:
            copy.wait_send()


class Turn:
    sems = (8, 8)

    def __init__(self, here, x, out, send, recv):
        rows, cols = out.shape[0], x.shape[1]
        into = out.at[:, pl.ds(pl.multiple_of(here.c * cols, cols), cols)]

        def part(j):
            return x.at[pl.ds(pl.multiple_of(j * rows, rows), rows)]

        self.copies = [pltpu.make_async_copy(part(here.c), into, send.at[0])]
        for k in CTX_ORDER:
            j = here.ctx(k)
            self.copies.append(remote(part(j), into, send.at[k], recv.at[k], {"ctx": j}))

    start = Gather.start
    wait = Gather.wait


class Columns:
    sems = (8, 8)

    def __init__(self, here, x, out, send, recv):
        rows, cols = x.shape[0], out.shape[1]
        into = out.at[pl.ds(pl.multiple_of(here.c * rows, rows), rows)]

        def part(j):
            return x.at[:, pl.ds(pl.multiple_of(j * cols, cols), cols)]

        self.copies = [pltpu.make_async_copy(part(here.c), into, send.at[0])]
        for k in CTX_ORDER:
            j = here.ctx(k)
            self.copies.append(remote(part(j), into, send.at[k], recv.at[k], {"ctx": j}))

    start = Gather.start
    wait = Gather.wait


class PairGather:
    sems = (8, 8, 8, 8)

    def __init__(self, here, x, out, send, recv, fsend, frecv):
        e = here.e
        self.own = pltpu.make_async_copy(x, out.at[e], fsend.at[0])
        self.first = remote(x, out.at[e], send.at[0], recv.at[0], here.partner)
        self.far, self.forward = {}, {}
        across = out.at[2 * here.chip_at(4) + here.core]
        for k in range(1, 8):
            if k <= 4:
                self.far[k] = remote(x, out.at[e], send.at[k], recv.at[k], here.same_core(k))
            else:
                self.far[k] = remote(across, across, send.at[k], recv.at[k], here.same_core(k - 4))
            slot = 2 * here.chip_from(k) + here.core
            self.forward[k] = remote(out.at[slot], out.at[slot], fsend.at[k], frecv.at[k], here.partner)

    def start(self):
        for k in (4, 2, 1, 3):
            self.far[k].start()
        self.first.start()
        self.own.start()

    def cross(self):
        self.far[4].wait_recv()
        for k in (6, 5, 7):
            self.far[k].start()
        self.forward[4].start()

    def pass_on(self):
        for k in (1, 3, 2, 5, 7, 6):
            self.far[k].wait_recv()
            self.forward[k].start()

    def wait(self):
        self.own.wait()
        self.first.wait()
        for k in range(1, 8):
            self.far[k].wait_send()
            self.forward[k].wait()


class PairScatter:
    sems = (8, 8, 8, 8, 8)

    @staticmethod
    def scratch(x):
        return [pltpu.VMEM((8,) + x.shape[1:], x.dtype)] * 4

    def __init__(self, here, x, total, mine, near, summed, far, load, nsend, nrecv, fsend, frecv):
        self.total, self.mine, self.near, self.summed, self.far = total, mine, near, summed, far
        self.loads, self.nears, self.fars = {}, {}, {}
        self.order = (6, 2, 5, 1, 7, 3, 4, 0)
        for k in self.order:
            there = here.chip_at(k)
            self.nears[k] = remote(x.at[2 * there + 1 - here.core], near.at[k], nsend.at[k], nrecv.at[k], here.partner)
            self.loads[k] = pltpu.make_async_copy(x.at[2 * there + here.core], mine.at[k], load.at[k])
            if k:
                where = here.same_core(k if k <= 4 else k - 4)
                self.fars[k] = remote(summed.at[k], far.at[k], fsend.at[k], frecv.at[k], where)

    def start(self):
        for k in self.order:
            self.nears[k].start()
            self.loads[k].start()

    def pass_on(self):
        for k in self.order:
            self.loads[k].wait()
            self.nears[k].wait_recv()
            both = self.mine[k].astype(f32) + self.near[k].astype(f32)
            if k == 0:
                self.total[...] = both
            else:
                self.summed[k] = both.astype(self.summed.dtype)
                if k != 4:
                    self.fars[k].start()

    def cross(self):
        for k in (5, 7, 6):
            self.fars[k].wait_recv()
        both = self.summed[4].astype(f32) + self.far[5].astype(f32)
        both += self.far[6].astype(f32) + self.far[7].astype(f32)
        self.summed[4] = both.astype(self.summed.dtype)
        self.fars[4].start()

    def wait(self):
        for k in (1, 3, 2, 4):
            self.fars[k].wait_recv()
            self.total[...] += self.far[k].astype(f32)
        for k in self.order:
            self.nears[k].wait_send()
            if k:
                self.fars[k].wait_send()


class Spread:
    sems = (16, 16)

    def __init__(self, here, x, out, send, recv):
        self.copies = [pltpu.make_async_copy(x.at[here.e], out.at[here.e], send.at[0])]
        for k in range(1, N_EXP):
            j = lax.rem(here.e + k, N_EXP)
            self.copies.append(remote(x.at[j], out.at[here.e], send.at[k], recv.at[k], {"exp": j}))

    start = Gather.start
    wait = Gather.wait


def sem_shapes(*kinds):
    return [DMA((n,)) for kind in kinds for n in kind.sems]


def params(cid):
    return pltpu.CompilerParams(collective_id=cid, has_side_effects=True, vmem_limit_bytes=60 * 2**20)


def call(kernel, outs, scratch, cid, *args, out_specs=None):
    return pl.pallas_call(
        kernel,
        out_shape=outs,
        in_specs=[ANY] * len(args),
        out_specs=out_specs or [HBM] * len(outs),
        scratch_shapes=scratch,
        compiler_params=params(cid),
    )(*args)


def shape(s, t):
    return jax.ShapeDtypeStruct(s, t)


def dot(a, b, dims=((1,), (0,))):
    return lax.dot_general(a, b, (dims, ((), ())), preferred_element_type=f32)


NT = ((1,), (1,))
TN = ((0,), (0,))


def factor_of(values):
    return lax.rsqrt(jnp.mean(values * values, axis=-1, keepdims=True) + eps_norm)


def normalize_back(values, factor, gain, upstream):
    scaled = upstream * gain
    inner = jnp.mean(scaled * values, axis=-1, keepdims=True)
    return factor * scaled - values * factor * factor * factor * inner


def experts(routed, gates, up_all, wgu_all, wd_all, h_one):
    rows, width = routed.shape
    both = 2 * rows
    f = wd_all.shape[2] // 2 * 8 * wd_all.shape[1] // width
    hid = 2 * f
    chunk = 256

    def kernel(
        x, g, u, wg, wdown, ho, out_part, total, gback, dwgu, dwd, hs,
        dparts, dmine, dfar, dsum, xs, gs, up, wgu, wd, usem, wsem, parts, near, summed, far, hg, dgu, gparts,
        xsend, xrecv, xfsend, xfrecv, gsend, grecv, gfsend, gfrecv,
        nsend, nrecv, rsend, rrecv, hsend, hrecv, dload, dsend, drecv, psend, precv,
    ):
        here = Here()
        core, e = here.core, here.e
        greet(here.exp_peers() + here.other_core_peers() + here.ctx_peers())
        rows_h = AxisGather(here, ho, hs, hsend, hrecv)
        down = AxisScatter(here, dparts, dwd, dmine, dfar, dsum, dload, dsend, drecv)
        own = [
            pltpu.make_async_copy(g, gs.at[e], gfsend.at[0]),
            pltpu.make_async_copy(x, xs.at[e], xfsend.at[0]),
            pltpu.make_async_copy(u, up, usem),
        ]
        own.append(pltpu.make_async_copy(wg, wgu, wsem.at[16]))
        for j in range(8):
            for i in range(2):
                own.append(
                    pltpu.make_async_copy(
                        wdown.at[j, :, pl.ds(width * i, width)],
                        wd.at[pl.ds(f * i + rows // 2 * j, rows // 2)],
                        wsem.at[2 * j + i],
                    )
                )
        first = [
            remote(g, gs.at[e], gsend.at[0], grecv.at[0], here.partner),
            remote(x, xs.at[e], xsend.at[0], xrecv.at[0], here.partner),
        ]
        for copy in own + first:
            copy.start()

        def away(k):
            return [
                remote(g, gs.at[e], gsend.at[k], grecv.at[k], {"exp": 2 * here.turn_at(k) + core}),
                remote(x, xs.at[e], xsend.at[k], xrecv.at[k], {"exp": 2 * here.turn_at(k) + core}),
            ]

        def pass_on(k):
            slot = 2 * here.turn_from(k) + core
            return [
                remote(gs.at[slot], gs.at[slot], gfsend.at[k], gfrecv.at[k], here.partner),
                remote(xs.at[slot], xs.at[slot], xfsend.at[k], xfrecv.at[k], here.partner),
            ]

        def to_partner(k):
            return remote(parts.at[k, 1 - core], near.at[k], nsend.at[k], nrecv.at[k], here.partner)

        def to_chip(k):
            where = {"exp": 2 * here.turn_from(k) + core}
            return remote(summed.at[k], far.at[k], rsend.at[k], rrecv.at[k], where)

        def gate_part(j):
            return remote(gparts.at[j], gback.at[e], psend.at[j], precv.at[e], {"exp": j})

        for k in range(1, 4):
            for copy in away(jnp.int32(k)):
                copy.start()
        rows_h.start()

        picks = lax.broadcasted_iota(jnp.int32, (32, 2 * 128), 0) == 2 * e + (
            lax.broadcasted_iota(jnp.int32, (32, 2 * 128), 1) // 128
        )
        picks = picks.astype(f32)

        def finish(k):
            to_partner(k).wait_recv()
            both_cores = parts[k, core].astype(f32) + near[k].astype(f32)

            @pl.when(k == 0)
            def _():
                total[...] = both_cores

            @pl.when(k > 0)
            def _():
                summed[k] = both_cores.astype(bf16)
                to_chip(k).start()

        def step(k, carry):
            @pl.when(k < 4)
            def _():
                for copy in away(k + 4):
                    copy.start()

            @pl.when(k == 0)
            def _():
                for copy in own:
                    copy.wait()
                for copy in first:
                    copy.wait_recv()

            @pl.when(k > 0)
            def _():
                for copy in pass_on(k):
                    copy.wait_recv()

            chip = here.turn_from(k)
            at = pl.ds(pl.multiple_of(chip * both, both), both)
            xb = xs[pl.ds(2 * chip, 2)].reshape(both, width)
            ub = up[pl.ds(2 * chip, 2)].reshape(both, width)
            gate_cols = jnp.concatenate(
                [
                    lax.dot_general(
                        gs[2 * chip + i], picks, (TN, ((), ())), precision=lax.Precision.HIGHEST,
                        preferred_element_type=f32,
                    )
                    for i in range(2)
                ],
                axis=0,
            )
            gate_sums = jnp.zeros((8, both), f32)
            for i in range(2):
                gate = jnp.concatenate([gate_cols[:, 128 * i : 128 * (i + 1)]] * (chunk // 128), axis=1)
                to_row = (lax.broadcasted_iota(jnp.int32, (8, chunk), 0) == i).astype(bf16)
                for j in range(i * f, (i + 1) * f, chunk):
                    cols, up_cols = pl.ds(j, chunk), pl.ds(hid + j, chunk)
                    gate_h = dot(xb, wgu[:, cols])
                    up_h = dot(xb, wgu[:, up_cols])
                    back = dot(ub, wd[cols], NT)
                    sig = 1.0 / (1.0 + jnp.exp(-gate_h))
                    silu = gate_h * sig
                    hidden = silu * up_h
                    hg[at, cols] = (hidden * gate).astype(bf16)
                    gate_sums += dot(to_row, (hidden * back).astype(bf16), NT)
                    grad_hidden = back * gate
                    dgu[at, cols] = (grad_hidden * up_h * (sig * (1.0 + gate_h * (1.0 - sig)))).astype(bf16)
                    dgu[at, up_cols] = (grad_hidden * silu).astype(bf16)
            for i in range(2):
                gparts[2 * chip + i] = gate_sums[:, rows * i : rows * (i + 1)]
            gate_part(2 * chip + 1 - core).start()

            @pl.when(k < 7)
            def _():
                for copy in away(k + 1):
                    copy.wait_recv()
                for copy in pass_on(k + 1):
                    copy.start()

            @pl.when(k > 0)
            def _():
                gate_part(2 * chip + core).start()

            return carry

        lax.fori_loop(0, 8, step, 0)
        mine = pltpu.make_async_copy(gparts.at[e], gback.at[e], psend.at[e])
        mine.start()
        rows_h.cross()

        def down_rows(i, carry):
            at = pl.ds(pl.multiple_of(i * 256, 256), 256)
            grads = dot(hg[:, at], up[...].reshape(16 * rows, width), TN).astype(bf16)
            cols = pl.ds(pl.multiple_of((i // 2) * width, width), width)
            dparts[pl.ds(4 * lax.rem(i, 2), 4), :, cols] = grads.reshape(4, rows // 2, width)
            return carry

        lax.fori_loop(0, hid // 256, down_rows, 0)
        down.start()

        def input_rows(k, carry):
            at = pl.ds(pl.multiple_of(here.turn_from(k) * both, both), both)
            parts[k] = dot(dgu[at], wgu[...], NT).astype(bf16).reshape(2, rows, width)
            to_partner(k).start()

            @pl.when(k > 0)
            def _():
                finish(k - 1)

            return carry

        lax.fori_loop(0, 8, input_rows, 0)
        finish(jnp.int32(7))

        def weight_rows(i, carry):
            at = pl.ds(pl.multiple_of(i * 256, 256), 256)
            columns = xs[:, :, at].reshape(16 * rows, 256)
            grads = dot(columns, dgu[...], TN).astype(bf16)
            dwgu[pl.ds(2 * i, 2)] = grads.reshape(2, rows, 2 * hid)
            return carry

        lax.fori_loop(0, width // 256, weight_rows, 0)

        def outputs(i, carry):
            at = pl.ds(pl.multiple_of(i * 512, 512), 512)
            out_part[pl.ds(512 // rows * i, 512 // rows)] = dot(hg[at], wd[...]).astype(bf16).reshape(512 // rows, rows, width)
            return carry

        lax.fori_loop(0, 16 * rows // 512, outputs, 0)

        def collect(k, carry):
            to_chip(k).wait_recv()
            total[...] += far[k].astype(f32)
            return carry

        lax.fori_loop(1, 8, collect, 0)
        down.cross()
        for copy in first:
            copy.wait_send()
        mine.wait()
        rows_h.wait()

        def drain(k, carry):
            for copy in away(k) + pass_on(k) + [to_partner(k), to_chip(k)]:
                copy.wait_send()
            return carry

        lax.fori_loop(1, 8, drain, 0)
        to_partner(0).wait_send()

        def drain_gates(k, carry):
            j = lax.rem(e + k, N_EXP)
            gate_part(j).wait_send()
            remote(gparts.at[j], gback.at[j], psend.at[j], precv.at[j], {"exp": j}).wait_recv()
            return carry

        lax.fori_loop(1, N_EXP, drain_gates, 0)
        down.wait()

    block = (8, rows, width)
    return pl.pallas_call(
        kernel,
        out_shape=[
            shape((16, rows, width), bf16),
            shape((rows, width), f32),
            shape((16, 8, rows), f32),
            shape((8, rows, 2 * hid), bf16),
            shape((rows // 2, 2 * width), f32),
            shape((8,) + h_one.shape, bf16),
        ],
        in_specs=[ANY] * 6,
        out_specs=[VMEM, VMEM, ANY, VMEM, VMEM, HBM],
        scratch_shapes=[
            pltpu.VMEM((8, rows // 2, 2 * width), bf16),
            *AxisScatter.scratch(shape((8, rows // 2, 2 * width), bf16)),
            pltpu.VMEM((16, rows, width), bf16),
            pltpu.VMEM((16, 32, rows), f32),
            pltpu.VMEM((16, rows, width), bf16),
            pltpu.VMEM((width, 2 * hid), bf16),
            pltpu.VMEM((hid, width), bf16),
            DMA,
            DMA((17,)),
            pltpu.VMEM((8, 2, rows, width), bf16),
            pltpu.VMEM(block, bf16),
            pltpu.VMEM(block, bf16),
            pltpu.VMEM(block, bf16),
            pltpu.VMEM((16 * rows, hid), bf16),
            pltpu.VMEM((16 * rows, 2 * hid), bf16),
            pltpu.VMEM((16, 8, rows), f32),
        ]
        + [DMA((8,))] * 14
        + sem_shapes(AxisScatter)
        + [DMA((16,))] * 2,
        compiler_params=pltpu.CompilerParams(collective_id=3, has_side_effects=True, vmem_limit_bytes=60 * 2**20),
    )(routed, gates, up_all, wgu_all, wd_all, h_one)


SCALE = HEAD_SIZE ** (-0.5)
QROWS = 256
SPAN = 64
SMEM = pl.BlockSpec(memory_space=pltpu.SMEM)


def left_lanes(shape_):
    return lax.broadcasted_iota(jnp.int32, shape_, 1) % 128 < HEAD_SIZE


def split_heads(kv):
    wide = kv.astype(f32)
    turned = pltpu.roll(wide, HEAD_SIZE, 1)
    left = left_lanes(kv.shape)
    return [
        jnp.where(left, wide, 0.0).astype(bf16),
        jnp.where(left, 0.0, turned).astype(bf16),
        jnp.where(left, turned, 0.0).astype(bf16),
        jnp.where(left, 0.0, wide).astype(bf16),
    ]


def place_column(spans, first, count):
    row = lax.broadcasted_iota(jnp.int32, (count, 1), 0)
    base = jnp.zeros((count, 1), jnp.int32)
    for i in range(count // SPAN):
        base = jnp.where(row // SPAN == i, spans[first + i], base)
    return base * SPAN + row % SPAN


def place_row(spans):
    lane = lax.broadcasted_iota(jnp.int32, (1, 16 * SPAN), 1)
    base = jnp.zeros((1, 16 * SPAN), jnp.int32)
    for i in range(16):
        base = jnp.where(lane // SPAN == i, spans[i], base)
    return base * SPAN + lane % SPAN


def tables(places, freqs):
    turned = places.astype(f32) * freqs
    return jnp.cos(turned), jnp.sin(turned)


def probs_of(q, k, visible):
    scores = jnp.where(visible, dot(q, k, NT) * SCALE, neg_big)
    shifted = jnp.exp(scores - jnp.max(scores, axis=-1, keepdims=True))
    return shifted * (1.0 / jnp.sum(shifted, axis=-1, keepdims=True))


def swap_of(v):
    leading = lax.broadcasted_iota(jnp.int32, v.shape, 1) % HEAD_SIZE < HALF
    return jnp.where(leading, -pltpu.roll(v, v.shape[1] - HALF, 1), pltpu.roll(v, HALF, 1))


def front(tokens, w_query, key_matrix, value_matrix, gains, router, w_out, cot, w_gate, w_up, w_down, freqs, spans):
    rows, width = tokens.shape
    own = w_query.shape[0]
    f = w_gate.shape[2]
    count = N_CTX * rows

    def kernel(
        x, wq, wk, wv, gn, ro, wo, u, wg, wup, wdn, fr, so,
        out, kept, h_out, gain_out, w_out_, ros, wos, us, wgus, wds,
        own_w, own_wgu, own_wd, own_gain, w, gs, h, stage, seq, heads, attn, lsem,
        send, recv, osend, orecv, ksem, *sems,
    ):
        here = Here()
        c = here.c
        loads = []
        for i in range(2):
            loads.append(pltpu.make_async_copy(wg.at[i], own_wgu.at[:, pl.ds(f * i, f)], lsem.at[3 * i]))
            loads.append(pltpu.make_async_copy(wup.at[i], own_wgu.at[:, pl.ds(f * (2 + i), f)], lsem.at[3 * i + 1]))
            loads.append(pltpu.make_async_copy(wdn.at[i], own_wd.at[:, pl.ds(width * i, width)], lsem.at[3 * i + 2]))
        for load in loads:
            load.start()
        left = left_lanes((own, 128))
        for i in range(N_CTX // 2):
            at = slice(128 * i, 128 * (i + 1))
            keys, vals = wk[:, at].astype(f32), wv[:, at].astype(f32)
            one = jnp.where(left, keys, pltpu.roll(vals, HEAD_SIZE, 1))
            two = jnp.where(left, pltpu.roll(keys, HEAD_SIZE, 1), vals)
            for j, kv in ((2 * i, one), (2 * i + 1, two)):
                own_w[:, 256 * j : 256 * j + 128] = wq[:, 128 * j : 128 * (j + 1)]
                own_w[:, 256 * j + 128 : 256 * (j + 1)] = kv.astype(bf16)
        half = gn[...].astype(f32)
        odd = here.core == 1
        lane = lax.broadcasted_iota(jnp.int32, half.shape, 1)
        own_gain[...] = jnp.where(odd, jnp.where(lane < 64, 0.0, pltpu.roll(half, 64, 1)), jnp.where(lane < 64, half, 0.0))
        greet(here.ctx_peers() + here.exp_peers())
        gain_all = PairGather(here, own_gain, gs, *sems[0:4])
        w_all = PairGather(here, own_w, w, *sems[4:8])
        ro_all = PairGather(here, ro, ros, *sems[8:12])
        wo_all = PairGather(here, wo, wos, *sems[12:16])
        cots = PairGather(here, u, us, *sems[16:20])
        firsts = AxisGather(here, own_wgu, wgus, *sems[20:22])
        downs = AxisGather(here, own_wd, wds, *sems[22:24])
        gain_all.start()
        w_all.start()
        for load in loads:
            load.wait()
        firsts.start()
        cos, sin = tables(place_column(so, 2 * c, rows), fr[...])
        pr = place_row(so)
        gain_all.cross()
        w_all.cross()
        for item in (wo_all, ro_all, cots):
            item.start()
        firsts.cross()
        gain_all.pass_on()
        gain_all.wait()
        for i in range(8):
            pair = gs[2 * i] + gs[2 * i + 1]
            gain_out[:, 128 * i : 128 * (i + 1)] = pair
        values = x[...].astype(f32)
        h[...] = (values * factor_of(values) * gain_out[0:1, :]).astype(bf16)
        keep_h = pltpu.make_async_copy(h, h_out, ksem.at[1])
        keep_h.start()
        w_all.pass_on()
        w_all.wait()
        keep_w = pltpu.make_async_copy(w, w_out_, ksem.at[2])
        keep_w.start()

        def block_rows(ref, j):
            return ref.at[pl.ds(pl.multiple_of(j * rows, rows), rows)]

        def column(j):
            return out.at[:, pl.ds(pl.multiple_of(j * 128, 128), 128)]

        def arrive(j):
            return remote(stage.at[j], block_rows(seq, c), send.at[j], recv.at[c], {"ctx": j})

        def arrive_own():
            return pltpu.make_async_copy(stage.at[c], block_rows(seq, c), send.at[c])

        def project(b, carry):
            j = lax.rem(c + 1 + b, N_CTX)
            at = pl.ds(pl.multiple_of(j * 256, 256), 256)
            p = dot(h[...], w[:, :, at].reshape(width, 256))
            stage[j] = (p * cos + swap_of(p) * sin).astype(bf16)

            @pl.when(b < N_CTX - 1)
            def _():
                arrive(j).start()

            return carry

        lax.fori_loop(0, N_CTX, project, 0)
        arrive_own().start()
        for item in (wo_all, ro_all, cots):
            item.cross()
        arrive_own().wait()
        for k in range(1, N_CTX):
            j = here.ctx(k)
            arrive(j).wait_send()
            remote(stage.at[j], block_rows(seq, j), send.at[j], recv.at[j], {"ctx": j}).wait_recv()
        downs.start()
        keep = pltpu.make_async_copy(seq, kept, ksem.at[0])
        keep.start()
        for i, part in enumerate(split_heads(seq[:, 128:])):
            heads[i] = part

        def leave(j):
            return remote(block_rows(attn, j), column(c), osend.at[j], orecv.at[c], {"ctx": j})

        def local():
            return pltpu.make_async_copy(block_rows(attn, c), column(c), osend.at[c])

        def step(b, carry):
            block = lax.rem(b + c // 2, count // QROWS)
            at = pl.ds(pl.multiple_of(block * QROWS, QROWS), QROWS)
            visible = pr <= place_column(so, block * (QROWS // SPAN), QROWS)
            q = seq[at, :128]
            total = jnp.zeros((QROWS, 128), f32)
            for i in range(2):
                total += dot(probs_of(q, heads[i], visible).astype(bf16), heads[2 + i])
            attn[at] = total.astype(bf16)
            for i in range(QROWS // rows):
                j = block * (QROWS // rows) + i

                @pl.when(j != c)
                def _():
                    leave(j).start()

                @pl.when(j == c)
                def _():
                    local().start()

            return carry

        lax.fori_loop(0, count // QROWS, step, 0)
        downs.cross()
        for item in (wo_all, ro_all, cots):
            item.pass_on()
        for k in range(1, N_CTX):
            j = here.ctx(k)
            leave(j).wait_send()
            remote(block_rows(attn, c), column(j), osend.at[j], orecv.at[j], {"ctx": j}).wait_recv()
        local().wait()
        for item in (keep, keep_h, keep_w, wo_all, ro_all, cots, firsts, downs):
            item.wait()

    return pl.pallas_call(
        kernel,
        out_shape=[
            shape((rows, N_CTX * 128), bf16),
            shape((count, 256), bf16),
            shape((rows, width), bf16),
            shape((8, width), f32),
            shape((16, own, N_CTX * 256), bf16),
            shape((16,) + router.shape, bf16),
            shape((16,) + w_out.shape, bf16),
            shape((16,) + cot.shape, bf16),
            shape((8, rows, 4 * f), bf16),
            shape((8, w_down.shape[1], 2 * width), bf16),
        ],
        in_specs=[VMEM] * 5 + [ANY] * 6 + [VMEM, SMEM],
        out_specs=[HBM] * 3 + [VMEM] + [HBM] * 6,
        scratch_shapes=[
            pltpu.VMEM((own, N_CTX * 256), bf16),
            pltpu.VMEM((rows, 4 * f), bf16),
            pltpu.VMEM((w_down.shape[1], 2 * width), bf16),
            pltpu.VMEM((8, 128), f32),
            pltpu.VMEM((16, own, N_CTX * 256), bf16),
            pltpu.VMEM((16, 8, 128), f32),
            pltpu.VMEM((rows, width), bf16),
            pltpu.VMEM((N_CTX, rows, 256), bf16),
            pltpu.VMEM((count, 256), bf16),
            pltpu.VMEM((4, count, 128), bf16),
            pltpu.VMEM((count, 128), bf16),
            DMA((6,)),
        ]
        + [DMA((8,))] * 4
        + [DMA((3,))]
        + sem_shapes(*[PairGather] * 5, AxisGather, AxisGather),
        compiler_params=params(2),
    )(tokens, w_query, key_matrix, value_matrix, gains, router, w_out, cot, w_gate, w_up, w_down, freqs, spans)


def attend_back(
    grad_routed, gate_back, gates, routed, pack, x_mid, gain, cot, attn_low, wo_full, seq_qkv, freqs, spans, h_all, out_part,
    first_part,
):
    rows, width = grad_routed.shape
    count = N_CTX * rows
    own = width // N_EXP
    scatters = [
        out_part,
        jax.ShapeDtypeStruct((16, own, width), bf16),
        jax.ShapeDtypeStruct((16, own, 384), bf16),
    ]

    def kernel(
        gr, gb, gt, ri, pk, xm, gn, u, al, wof, seq, fr, so, hh, op, dp, mid, back, moe, wos, alls, dwgu, h, hsem,
        low_w, low, wo_total, total, payload, wp, ga, grads, heads, acc, dqkv, cos, sin, *rest,
    ):
        here = Here()
        load = pltpu.make_async_copy(hh, h, hsem)
        load.start()
        greet(here.ctx_peers() + here.exp_peers())
        bufs, sems = rest[:15], rest[15:]
        first = AxisScatter(here, dp, dwgu, *bufs[12:15], *sems[23:26])
        arrive = Columns(here, ga, grads, *sems[0:2])
        outs = PairScatter(here, op, moe, *bufs[0:4], *sems[2:7])
        wo = PairScatter(here, wp, wo_total, *bufs[4:8], *sems[7:12])
        proj = PairScatter(here, payload, total, *bufs[8:12], *sems[12:17])
        turn = Turn(here, dqkv, back, *sems[17:19])
        wo_rows = Gather(here, low_w, wos, *sems[19:21])
        all_rows = Gather(here, low, alls, *sems[21:23])
        outs.start()
        spot = lax.broadcasted_iota(jnp.int32, (16 * 8, 128), 0)
        lane = lax.broadcasted_iota(jnp.int32, (16 * 8, 128), 1)
        picks = jnp.where(jnp.logical_and(spot % 8 < 2, spot // 8 * 2 + spot % 8 == lane), 1.0, 0.0)
        exact = functools.partial(
            lax.dot_general, dimension_numbers=(TN, ((), ())), precision=lax.Precision.HIGHEST, preferred_element_type=f32
        )
        grad_gates = exact(gb[...].reshape(16 * 8, rows), picks)
        weighted = gt[...] * grad_gates
        grad_logits = (weighted - gt[...] * jnp.sum(weighted, axis=-1, keepdims=True)).astype(bf16)
        routed_grad = gr[...] + dot(grad_logits, pk[...], NT)
        values = xm[...]
        factor = factor_of(values)
        grad_mid = u[...].astype(f32) + normalize_back(values, factor, gn[...], routed_grad)
        mid[...] = grad_mid
        branch = grad_mid.astype(bf16)
        ga[...] = dot(branch, wof[...], NT).astype(bf16)
        arrive.start()
        first.start()
        wp[...] = dot(al[...], branch, TN).astype(bf16).reshape(16, own, width)
        wo.start()
        column = (lax.broadcasted_iota(jnp.int32, (rows, 128), 1) == 32).astype(f32)
        small = dot(ri[...], grad_logits, TN) + exact(routed_grad * values * factor, column)
        payload[:, :, 256:] = small.astype(bf16).reshape(16, own, 128)
        pr = place_row(so)
        cos[...], sin[...] = tables(place_column(so, 0, count), fr[...])
        for i, part in enumerate(split_heads(seq[:, 128:])):
            heads[i] = part
        acc[...] = jnp.zeros_like(acc)
        arrive.wait()
        wo.pass_on()
        outs.pass_on()

        def step(b, carry):
            at = pl.ds(pl.multiple_of(b * QROWS, QROWS), QROWS)
            visible = pr <= place_column(so, b * (QROWS // SPAN), QROWS)
            q, g = seq[at, :128], grads[at]
            dq = jnp.zeros((QROWS, 128), f32)
            for i in range(2):
                probs = probs_of(q, heads[i], visible)
                grad_probs = dot(g, heads[2 + i], NT)
                inner = jnp.sum(probs * grad_probs, axis=-1, keepdims=True)
                grad_scores = (probs * (grad_probs - inner)).astype(bf16)
                dq += dot(grad_scores, heads[i])
                acc[i] += dot(grad_scores, q, TN)
                acc[2 + i] += dot(probs.astype(bf16), g, TN)
            dq = dq * SCALE
            dqkv[at, :128] = (dq * cos[at] - swap_of(dq * sin[at])).astype(bf16)
            return carry

        lax.fori_loop(0, count // QROWS, step, 0)
        left = left_lanes((count, 128))
        dk = (acc[0] + pltpu.roll(acc[1], HEAD_SIZE, 1)) * SCALE
        dv = pltpu.roll(acc[2], HEAD_SIZE, 1) + acc[3]
        dk = dk * cos[...] - swap_of(dk * sin[...])
        dqkv[:, 128:] = jnp.where(left, dk, dv).astype(bf16)
        turn.start()
        load.wait()
        payload[:, :, :256] = dot(h[...], dqkv[...], TN).astype(bf16).reshape(16, own, 256)
        proj.start()
        wo.cross()
        proj.pass_on()
        wo.wait()
        low_w[...] = wo_total[...].astype(bf16)
        wo_rows.start()
        proj.cross()
        outs.cross()
        proj.wait()
        low[...] = total[...].astype(bf16)
        all_rows.start()
        first.cross()
        outs.wait()
        turn.wait()
        wo_rows.wait()
        all_rows.wait()
        first.wait()

    return pl.pallas_call(
        kernel,
        out_shape=[
            shape((rows, width), f32),
            shape((rows, N_CTX * 256), bf16),
            shape((rows, width), f32),
            shape((8, own, width), bf16),
            shape((8, own, 384), bf16),
            shape(first_part.shape[1:], f32),
        ],
        in_specs=[VMEM] * 12 + [SMEM, ANY, ANY, ANY],
        out_specs=[VMEM, HBM, VMEM, HBM, HBM, VMEM],
        scratch_shapes=[
            pltpu.VMEM(h_all.shape, bf16),
            DMA,
            pltpu.VMEM((own, width), bf16),
            pltpu.VMEM((own, 384), bf16),
            pltpu.VMEM((own, width), f32),
            pltpu.VMEM((own, 384), f32),
            pltpu.VMEM((16, own, 384), bf16),
            pltpu.VMEM((16, own, width), bf16),
            pltpu.VMEM((rows, width), bf16),
            pltpu.VMEM((count, 128), bf16),
            pltpu.VMEM((4, count, 128), bf16),
            pltpu.VMEM((4, count, 128), f32),
            pltpu.VMEM((count, 256), bf16),
            pltpu.VMEM((count, 128), f32),
            pltpu.VMEM((count, 128), f32),
        ]
        + [b for x in scatters for b in PairScatter.scratch(x)]
        + AxisScatter.scratch(first_part)
        + sem_shapes(Columns, PairScatter, PairScatter, PairScatter, Turn, Gather, Gather, AxisScatter),
        compiler_params=pltpu.CompilerParams(collective_id=4, has_side_effects=True, vmem_limit_bytes=60 * 2**20),
    )(
        grad_routed, gate_back, gates, routed, pack, x_mid, gain, cot, attn_low, wo_full, seq_qkv, freqs, spans, h_all,
        out_part, first_part,
    )


def finish_tokens(
    back, wqkv, tokens, gain, grad_mid, x_mid, moe_out, owned, wo_sums, w_query, key_matrix, value_matrix, norm_attn,
    grad_first, grad_down,
):
    rows, width = tokens.shape
    own = w_query.shape[0]
    f = grad_first.shape[1] // 4
    args = (
        back, wqkv, tokens, gain, grad_mid, x_mid, moe_out, owned, wo_sums, w_query, key_matrix, value_matrix,
        norm_attn[None, :], grad_first, grad_down,
    )

    def kernel(*refs):
        n = len(args)
        ins, (result, grad, gq, gk, gv, go, tail, gm, ga, gg, gu, gd) = refs[:n], refs[n : n + 12]
        held, sems = refs[n + 12 : -1], refs[-1]
        loads = [pltpu.make_async_copy(a, b, sems.at[i]) for i, (a, b) in enumerate(zip(ins, held))]
        for load in loads:
            load.start()
        for load in loads:
            load.wait()
        back, wqkv, x, gain, mid, xm, moe, owned, wos, wq, wk, wv, norm, first, down = held
        for i in range(2):
            gg[i] = first[:, f * i : f * (i + 1)]
            gu[i] = first[:, f * (2 + i) : f * (3 + i)]
            gd[i] = down[:, 2 * f * i : 2 * f * (i + 1)]
        result[...] = (xm[...] + moe[...]).astype(bf16)
        values = x[...].astype(f32)
        factor = factor_of(values)
        grad[...] = mid[...] + normalize_back(values, factor, gain[...], dot(back[...], wqkv[...], NT))
        left = left_lanes((own, 128))
        rest = jnp.zeros((own, 128), f32)
        sums = jnp.zeros((own, 128), f32)
        for i in range(N_CTX):
            block = owned[i, :, :128].astype(f32)
            at = slice(128 * i, 128 * (i + 1))
            gq[:, at] = block
            sums += block * wq[:, at].astype(f32)
            rest += owned[i, :, 256:].astype(f32)
        for i in range(N_CTX // 2):
            one, two = owned[2 * i, :, 128:256].astype(f32), owned[2 * i + 1, :, 128:256].astype(f32)
            at = slice(128 * i, 128 * (i + 1))
            keys = jnp.where(left, one, pltpu.roll(two, HEAD_SIZE, 1))
            vals = jnp.where(left, pltpu.roll(one, HEAD_SIZE, 1), two)
            gk[:, at] = keys
            gv[:, at] = vals
            sums += keys * wk[:, at].astype(f32) + vals * wv[:, at].astype(f32)
        turned = jnp.transpose(rest)
        tail[...] = turned[:32]
        gm[...] = turned[32:33]
        ga[...] = jnp.sum(jnp.transpose(sums), axis=0, keepdims=True) / norm[...].astype(f32)
        total = wos[0].astype(f32)
        for i in range(1, N_CTX):
            total += wos[i].astype(f32)
        go[...] = total

    return pl.pallas_call(
        kernel,
        out_shape=[
            shape((rows, width), bf16),
            shape((rows, width), f32),
            shape((own, width), f32),
            shape((own, width // 2), f32),
            shape((own, width // 2), f32),
            shape((own, width), f32),
            shape((32, own), f32),
            shape((1, own), f32),
            shape((1, own), f32),
            shape((2, rows, f), f32),
            shape((2, rows, f), f32),
            shape((2, rows // 2, 2 * f), f32),
        ],
        in_specs=[ANY] * len(args),
        out_specs=[VMEM] * 12,
        scratch_shapes=[pltpu.VMEM(a.shape, a.dtype) for a in args] + [DMA((len(args),))],
        compiler_params=pltpu.CompilerParams(vmem_limit_bytes=60 * 2**20),
    )(*args)


def body(
    tokens, cotangent, span_order, expert_choice, norm_attn, w_query, key_matrix, value_matrix,
    w_out, norm_moe, w_router, w_gate, w_up, w_down,
):
    tokens, cotangent, choice = tokens[0], cotangent[0], expert_choice[0]
    rows, width = tokens.shape
    pack = jnp.pad(w_router, ((0, 0), (0, 128 - 32)))
    gains = jnp.pad(jnp.stack([norm_attn, norm_moe]), ((0, 6), (0, 64)))
    lanes = jnp.arange(256, dtype=jnp.int32)
    freqs = rope_base ** (-((lanes % HALF).astype(f32) * 2.0 / HEAD_SIZE))
    freqs = jnp.where(lanes < 192, freqs, 0.0)[None, :]
    attn_low, seq_qkv, h_one, gains, wqkv, pack_all, wo, up_all, wgu_all, wd_all = front(
        tokens, w_query, key_matrix, value_matrix, gains, pack, w_out, cotangent, w_gate, w_up, w_down, freqs, span_order
    )
    gain_a, gain_m = gains[0:1], gains[1:2]
    wgu_all = wgu_all.reshape(width, 4 * w_gate.shape[2])
    wqkv = wqkv.reshape(width, N_CTX * 256)
    pack_all = pack_all.reshape(width, 128)
    wo = wo.reshape(width, width)
    inputs = tokens.astype(f32)
    x_mid = inputs + dot(attn_low, wo)
    routed_in = (x_mid * factor_of(x_mid) * gain_m).astype(bf16)
    logits = dot(routed_in, pack_all)
    expert_ids = jnp.arange(128, dtype=jnp.int32)
    chosen = jnp.any(choice[:, :, None] == expert_ids[None, None, :], axis=1)
    masked = jnp.where(chosen, logits, neg_big)
    lifted = jnp.where(chosen, jnp.exp(masked - jnp.max(masked, axis=-1, keepdims=True)), 0.0)
    gates = lifted / jnp.sum(lifted, axis=-1, keepdims=True)
    out_part, grad_routed, gate_back, grad_wgu, grad_wd, h_all = experts(
        routed_in, gates[:, :32].T, up_all, wgu_all, wd_all, h_one
    )
    h_all = h_all.reshape(N_CTX * rows, width)
    grad_mid, back, moe_out, wo_sums, owned, grad_first = attend_back(
        grad_routed, gate_back, gates, routed_in, pack_all, x_mid, gain_m, cotangent, attn_low, wo, seq_qkv,
        freqs[:, :128], span_order, h_all, out_part, grad_wgu,
    )
    result, grad_tokens, out_wq, out_wk, out_wv, out_wo, tail, out_gain_m, out_gain_a, out_wg, out_wu, out_wd = finish_tokens(
        back, wqkv, tokens, gain_a, grad_mid, x_mid, moe_out, owned, wo_sums, w_query, key_matrix, value_matrix, norm_attn,
        grad_first, grad_wd,
    )
    return (
        result[None],
        grad_tokens[None],
        out_gain_a[0],
        out_wq,
        out_wk,
        out_wv,
        out_wo,
        out_gain_m[0],
        tail.T,
        out_wg,
        out_wu,
        out_wd,
    )


def solution(mesh):
    return jax.shard_map(
        body,
        mesh=mesh,
        in_specs=(
            P("exp", "ctx", None),
            P("exp", "ctx", None),
            P(),
            P("exp", "ctx", None),
            P("exp"),
            P("exp", None),
            P("exp", None),
            P("exp", None),
            P("exp", None),
            P("exp"),
            P("exp", None),
            P("exp", "ctx", None),
            P("exp", "ctx", None),
            P("exp", "ctx", None),
        ),
        out_specs=(
            P("exp", "ctx", None),
            P("exp", "ctx", None),
            P("exp"),
            P("exp", None),
            P("exp", None),
            P("exp", None),
            P("exp", None),
            P("exp"),
            P("exp", None),
            P("exp", "ctx", None),
            P("exp", "ctx", None),
            P("exp", "ctx", None),
        ),
        check_vma=False,
    )
```

```python
import functools

import jax
import jax.numpy as jnp
from jax import lax
from jax.experimental import pallas as pl
from jax.experimental.pallas import tpu as pltpu
from jax.sharding import PartitionSpec as P

HEAD_SIZE = 64
HALF = 32
N_CTX = 8
N_EXP = 16
eps_norm = 1e-06
rope_base = 10000.0
neg_big = -1e30
f32, bf16 = jnp.float32, jnp.bfloat16

MESH = pl.DeviceIdType.MESH
ANY = pl.BlockSpec(memory_space=pl.ANY)
HBM = pl.BlockSpec(memory_space=pltpu.HBM)
VMEM = pl.BlockSpec(memory_space=pltpu.VMEM)
DMA = pltpu.SemaphoreType.DMA
NEAR_LAST = (6, 5, 7, 2, 4, 1, 3)
NEAR_FIRST = (1, 3, 2, 4, 5, 7, 6)
CTX_ORDER = (2, 6, 4, 1, 3, 5, 7)


def remote(src, dst, send, recv, where):
    return pltpu.make_async_remote_copy(
        src_ref=src, dst_ref=dst, send_sem=send, recv_sem=recv, device_id=where, device_id_type=MESH
    )


def greet(places, amount=None):
    barrier = pltpu.get_barrier_semaphore()
    for where in places:
        pl.semaphore_signal(barrier, inc=1, device_id=where, device_id_type=MESH)
    pl.semaphore_wait(barrier, len(places) if amount is None else amount)


class Here:
    def __init__(self):
        self.c = lax.axis_index("ctx")
        self.e = lax.axis_index("exp")
        self.core = lax.rem(self.e, 2)
        self.chip = self.e // 2
        self.partner = {"exp": self.e + 1 - 2 * self.core}

    def ctx(self, k):
        return lax.rem(self.c + k, N_CTX)

    def chip_at(self, k):
        return 4 * lax.rem(self.chip // 4 + k // 4, 2) + lax.rem(lax.rem(self.chip, 4) + lax.rem(k, 4), 4)

    def chip_from(self, k):
        return 4 * lax.rem(self.chip // 4 + k // 4, 2) + lax.rem(lax.rem(self.chip, 4) + 4 - lax.rem(k, 4), 4)

    def turn(self, k):
        k = k + k // 3 - 2 * (k // 4) + k // 5 - k // 6
        m = lax.rem(k, 4)
        return k // 4, m + m // 2 - 2 * (m // 3)

    def turn_at(self, k):
        z, y = self.turn(k)
        return 4 * lax.rem(self.chip // 4 + z, 2) + lax.rem(lax.rem(self.chip, 4) + y, 4)

    def turn_from(self, k):
        z, y = self.turn(k)
        return 4 * lax.rem(self.chip // 4 + z, 2) + lax.rem(lax.rem(self.chip, 4) + 4 - y, 4)

    def ctx_peers(self):
        return [{"ctx": self.ctx(k)} for k in range(1, N_CTX)]

    def same_core(self, k):
        return {"exp": 2 * self.chip_at(k) + self.core}

    def exp_peers(self):
        return [self.partner] + [self.same_core(k) for k in range(1, 8)]

    def other_core_peers(self):
        return [{"exp": 2 * self.chip_at(k) + 1 - self.core} for k in range(1, 8)]


class Gather:
    sems = (8, 8)

    def __init__(self, here, x, out, send, recv):
        self.copies = [pltpu.make_async_copy(x, out.at[here.c], send.at[0])]
        for k in CTX_ORDER:
            self.copies.append(remote(x, out.at[here.c], send.at[k], recv.at[k], {"ctx": here.ctx(k)}))

    def start(self):
        for c in self.copies:
            c.start()

    def wait(self):
        for c in self.copies:
            c.wait()


class AxisGather:
    sems = (8, 8)

    def __init__(self, here, x, out, send, recv):
        c = here.c
        self.own = pltpu.make_async_copy(x, out.at[c], send.at[0])
        across = lax.rem(c + 4, 8)
        self.across = remote(x, out.at[c], send.at[4], recv.at[4], {"ctx": across})
        self.near, self.rest = [], []
        for k in (2, 1, 3):
            peer = {"ctx": c // 4 * 4 + lax.rem(lax.rem(c, 4) + k, 4)}
            self.near.append(remote(x, out.at[c], send.at[k], recv.at[k], peer))
            self.rest.append(remote(out.at[across], out.at[across], send.at[4 + k], recv.at[4 + k], peer))

    def start(self):
        self.across.start()
        for copy in self.near:
            copy.start()
        self.own.start()

    def cross(self):
        self.across.wait_recv()
        for copy in self.rest:
            copy.start()

    def wait(self):
        self.own.wait()
        self.across.wait_send()
        for copy in self.near + self.rest:
            copy.wait()


class AxisScatter:
    sems = (2, 8, 8)

    @staticmethod
    def scratch(x):
        one = x.shape[1:]
        return [pltpu.VMEM((2,) + one, x.dtype), pltpu.VMEM((8,) + one, x.dtype), pltpu.VMEM(one, x.dtype)]

    def __init__(self, here, x, total, mine, far, summed, load, send, recv):
        c = here.c
        across = lax.rem(c + 4, 8)
        self.mine, self.far, self.summed, self.total = mine, far, summed, total
        self.loads = [pltpu.make_async_copy(x.at[j], mine.at[i], load.at[i]) for i, j in enumerate((c, across))]
        self.copies = []
        for z in (1, 0):
            for k in (2, 1, 3):
                peer = c // 4 * 4 + lax.rem(lax.rem(c, 4) + k, 4)
                i = 4 * z + k
                block = lax.rem(peer + 4 * z, 8)
                self.copies.append(remote(x.at[block], far.at[i], send.at[i], recv.at[i], {"ctx": peer}))
        self.over = remote(summed, far.at[4], send.at[4], recv.at[4], {"ctx": across})

    def start(self):
        for copy in self.loads + self.copies:
            copy.start()

    def cross(self):
        for copy in self.loads:
            copy.wait()
        for copy in self.copies:
            copy.wait_recv()
        both = self.mine[1].astype(f32)
        for k in (5, 6, 7):
            both += self.far[k].astype(f32)
        self.summed[...] = both.astype(bf16)
        self.over.start()
        both = self.mine[0].astype(f32)
        for k in (1, 2, 3):
            both += self.far[k].astype(f32)
        self.total[...] = both

    def wait(self):
        self.over.wait_recv()
        self.total[...] += self.far[4].astype(f32)
        self.over.wait_send()
        for copy in self.copies:
            copy.wait_send()


class Turn:
    sems = (8, 8)

    def __init__(self, here, x, out, send, recv):
        rows, cols = out.shape[0], x.shape[1]
        into = out.at[:, pl.ds(pl.multiple_of(here.c * cols, cols), cols)]

        def part(j):
            return x.at[pl.ds(pl.multiple_of(j * rows, rows), rows)]

        self.copies = [pltpu.make_async_copy(part(here.c), into, send.at[0])]
        for k in CTX_ORDER:
            j = here.ctx(k)
            self.copies.append(remote(part(j), into, send.at[k], recv.at[k], {"ctx": j}))

    start = Gather.start
    wait = Gather.wait


class Columns:
    sems = (8, 8)

    def __init__(self, here, x, out, send, recv):
        rows, cols = x.shape[0], out.shape[1]
        into = out.at[pl.ds(pl.multiple_of(here.c * rows, rows), rows)]

        def part(j):
            return x.at[:, pl.ds(pl.multiple_of(j * cols, cols), cols)]

        self.copies = [pltpu.make_async_copy(part(here.c), into, send.at[0])]
        for k in CTX_ORDER:
            j = here.ctx(k)
            self.copies.append(remote(part(j), into, send.at[k], recv.at[k], {"ctx": j}))

    start = Gather.start
    wait = Gather.wait


class PairGather:
    sems = (8, 8, 8, 8)

    def __init__(self, here, x, out, send, recv, fsend, frecv):
        e = here.e
        self.own = pltpu.make_async_copy(x, out.at[e], fsend.at[0])
        self.first = remote(x, out.at[e], send.at[0], recv.at[0], here.partner)
        self.far, self.forward = {}, {}
        across = out.at[2 * here.chip_at(4) + here.core]
        for k in range(1, 8):
            if k <= 4:
                self.far[k] = remote(x, out.at[e], send.at[k], recv.at[k], here.same_core(k))
            else:
                self.far[k] = remote(across, across, send.at[k], recv.at[k], here.same_core(k - 4))
            slot = 2 * here.chip_from(k) + here.core
            self.forward[k] = remote(out.at[slot], out.at[slot], fsend.at[k], frecv.at[k], here.partner)

    def start(self):
        for k in (4, 2, 1, 3):
            self.far[k].start()
        self.first.start()
        self.own.start()

    def cross(self):
        self.far[4].wait_recv()
        for k in (6, 5, 7):
            self.far[k].start()
        self.forward[4].start()

    def pass_on(self):
        for k in (1, 3, 2, 5, 7, 6):
            self.far[k].wait_recv()
            self.forward[k].start()

    def wait(self):
        self.own.wait()
        self.first.wait()
        for k in range(1, 8):
            self.far[k].wait_send()
            self.forward[k].wait()


class PairScatter:
    sems = (8, 8, 8, 8, 8)

    @staticmethod
    def scratch(x):
        return [pltpu.VMEM((8,) + x.shape[1:], x.dtype)] * 4

    def __init__(self, here, x, total, mine, near, summed, far, load, nsend, nrecv, fsend, frecv):
        self.total, self.mine, self.near, self.summed, self.far = total, mine, near, summed, far
        self.loads, self.nears, self.fars = {}, {}, {}
        self.order = (6, 2, 5, 1, 7, 3, 4, 0)
        for k in self.order:
            there = here.chip_at(k)
            self.nears[k] = remote(x.at[2 * there + 1 - here.core], near.at[k], nsend.at[k], nrecv.at[k], here.partner)
            self.loads[k] = pltpu.make_async_copy(x.at[2 * there + here.core], mine.at[k], load.at[k])
            if k:
                where = here.same_core(k if k <= 4 else k - 4)
                self.fars[k] = remote(summed.at[k], far.at[k], fsend.at[k], frecv.at[k], where)

    def start(self):
        for k in self.order:
            self.nears[k].start()
            self.loads[k].start()

    def pass_on(self):
        for k in self.order:
            self.loads[k].wait()
            self.nears[k].wait_recv()
            both = self.mine[k].astype(f32) + self.near[k].astype(f32)
            if k == 0:
                self.total[...] = both
            else:
                self.summed[k] = both.astype(self.summed.dtype)
                if k != 4:
                    self.fars[k].start()

    def cross(self):
        for k in (5, 7, 6):
            self.fars[k].wait_recv()
        both = self.summed[4].astype(f32) + self.far[5].astype(f32)
        both += self.far[6].astype(f32) + self.far[7].astype(f32)
        self.summed[4] = both.astype(self.summed.dtype)
        self.fars[4].start()

    def wait(self):
        for k in (1, 3, 2, 4):
            self.fars[k].wait_recv()
            self.total[...] += self.far[k].astype(f32)
        for k in self.order:
            self.nears[k].wait_send()
            if k:
                self.fars[k].wait_send()


class Spread:
    sems = (16, 16)

    def __init__(self, here, x, out, send, recv):
        self.copies = [pltpu.make_async_copy(x.at[here.e], out.at[here.e], send.at[0])]
        for k in range(1, N_EXP):
            j = lax.rem(here.e + k, N_EXP)
            self.copies.append(remote(x.at[j], out.at[here.e], send.at[k], recv.at[k], {"exp": j}))

    start = Gather.start
    wait = Gather.wait


def sem_shapes(*kinds):
    return [DMA((n,)) for kind in kinds for n in kind.sems]


def params(cid):
    return pltpu.CompilerParams(collective_id=cid, has_side_effects=True, vmem_limit_bytes=60 * 2**20)


def call(kernel, outs, scratch, cid, *args, out_specs=None):
    return pl.pallas_call(
        kernel,
        out_shape=outs,
        in_specs=[ANY] * len(args),
        out_specs=out_specs or [HBM] * len(outs),
        scratch_shapes=scratch,
        compiler_params=params(cid),
    )(*args)


def shape(s, t):
    return jax.ShapeDtypeStruct(s, t)


def dot(a, b, dims=((1,), (0,))):
    return lax.dot_general(a, b, (dims, ((), ())), preferred_element_type=f32)


NT = ((1,), (1,))
TN = ((0,), (0,))


def factor_of(values):
    return lax.rsqrt(jnp.mean(values * values, axis=-1, keepdims=True) + eps_norm)


def normalize_back(values, factor, gain, upstream):
    scaled = upstream * gain
    inner = jnp.mean(scaled * values, axis=-1, keepdims=True)
    return factor * scaled - values * factor * factor * factor * inner


def experts(routed, gates, up_all, wgu_all, wd_all, h_one):
    rows, width = routed.shape
    both = 2 * rows
    f = wd_all.shape[2] // 2 * 8 * wd_all.shape[1] // width
    hid = 2 * f
    chunk = 256

    def kernel(
        x, g, u, wg, wdown, ho, out_part, total, gback, dwgu, dwd, hs,
        dparts, dmine, dfar, dsum, xs, gs, up, wgu, wd, usem, wsem, parts, near, summed, far, hg, dgu, gparts,
        xsend, xrecv, xfsend, xfrecv, gsend, grecv, gfsend, gfrecv,
        nsend, nrecv, rsend, rrecv, hsend, hrecv, dload, dsend, drecv, psend, precv,
    ):
        here = Here()
        core, e = here.core, here.e
        greet(here.exp_peers() + here.other_core_peers() + here.ctx_peers())
        rows_h = AxisGather(here, ho, hs, hsend, hrecv)
        down = AxisScatter(here, dparts, dwd, dmine, dfar, dsum, dload, dsend, drecv)
        own = [
            pltpu.make_async_copy(g, gs.at[e], gfsend.at[0]),
            pltpu.make_async_copy(x, xs.at[e], xfsend.at[0]),
            pltpu.make_async_copy(u, up, usem),
        ]
        own.append(pltpu.make_async_copy(wg, wgu, wsem.at[16]))
        for j in range(8):
            for i in range(2):
                own.append(
                    pltpu.make_async_copy(
                        wdown.at[j, :, pl.ds(width * i, width)],
                        wd.at[pl.ds(f * i + rows // 2 * j, rows // 2)],
                        wsem.at[2 * j + i],
                    )
                )
        first = [
            remote(g, gs.at[e], gsend.at[0], grecv.at[0], here.partner),
            remote(x, xs.at[e], xsend.at[0], xrecv.at[0], here.partner),
        ]
        for copy in own + first:
            copy.start()

        def away(k):
            return [
                remote(g, gs.at[e], gsend.at[k], grecv.at[k], {"exp": 2 * here.turn_at(k) + core}),
                remote(x, xs.at[e], xsend.at[k], xrecv.at[k], {"exp": 2 * here.turn_at(k) + core}),
            ]

        def pass_on(k):
            slot = 2 * here.turn_from(k) + core
            return [
                remote(gs.at[slot], gs.at[slot], gfsend.at[k], gfrecv.at[k], here.partner),
                remote(xs.at[slot], xs.at[slot], xfsend.at[k], xfrecv.at[k], here.partner),
            ]

        def to_partner(k):
            return remote(parts.at[k, 1 - core], near.at[k], nsend.at[k], nrecv.at[k], here.partner)

        def to_chip(k):
            where = {"exp": 2 * here.turn_from(k) + core}
            return remote(summed.at[k], far.at[k], rsend.at[k], rrecv.at[k], where)

        def gate_part(j):
            return remote(gparts.at[j], gback.at[e], psend.at[j], precv.at[e], {"exp": j})

        for k in range(1, 4):
            for copy in away(jnp.int32(k)):
                copy.start()
        rows_h.start()

        picks = lax.broadcasted_iota(jnp.int32, (32, 2 * 128), 0) == 2 * e + (
            lax.broadcasted_iota(jnp.int32, (32, 2 * 128), 1) // 128
        )
        picks = picks.astype(f32)

        def finish(k):
            to_partner(k).wait_recv()
            both_cores = parts[k, core].astype(f32) + near[k].astype(f32)

            @pl.when(k == 0)
            def _():
                total[...] = both_cores

            @pl.when(k > 0)
            def _():
                summed[k] = both_cores.astype(bf16)
                to_chip(k).start()

        def step(k, carry):
            @pl.when(k < 4)
            def _():
                for copy in away(k + 4):
                    copy.start()

            @pl.when(k == 0)
            def _():
                for copy in own:
                    copy.wait()
                for copy in first:
                    copy.wait_recv()

            @pl.when(k > 0)
            def _():
                for copy in pass_on(k):
                    copy.wait_recv()

            chip = here.turn_from(k)
            at = pl.ds(pl.multiple_of(chip * both, both), both)
            xb = xs[pl.ds(2 * chip, 2)].reshape(both, width)
            ub = up[pl.ds(2 * chip, 2)].reshape(both, width)
            gate_cols = jnp.concatenate(
                [
                    lax.dot_general(
                        gs[2 * chip + i], picks, (TN, ((), ())), precision=lax.Precision.HIGHEST,
                        preferred_element_type=f32,
                    )
                    for i in range(2)
                ],
                axis=0,
            )
            gate_sums = jnp.zeros((8, both), f32)
            for i in range(2):
                gate = jnp.concatenate([gate_cols[:, 128 * i : 128 * (i + 1)]] * (chunk // 128), axis=1)
                to_row = (lax.broadcasted_iota(jnp.int32, (8, chunk), 0) == i).astype(bf16)
                for j in range(i * f, (i + 1) * f, chunk):
                    cols, up_cols = pl.ds(j, chunk), pl.ds(hid + j, chunk)
                    gate_h = dot(xb, wgu[:, cols])
                    up_h = dot(xb, wgu[:, up_cols])
                    back = dot(ub, wd[cols], NT)
                    sig = 1.0 / (1.0 + jnp.exp(-gate_h))
                    silu = gate_h * sig
                    hidden = silu * up_h
                    hg[at, cols] = (hidden * gate).astype(bf16)
                    gate_sums += dot(to_row, (hidden * back).astype(bf16), NT)
                    grad_hidden = back * gate
                    dgu[at, cols] = (grad_hidden * up_h * (sig * (1.0 + gate_h * (1.0 - sig)))).astype(bf16)
                    dgu[at, up_cols] = (grad_hidden * silu).astype(bf16)
            for i in range(2):
                gparts[2 * chip + i] = gate_sums[:, rows * i : rows * (i + 1)]
            gate_part(2 * chip + 1 - core).start()

            @pl.when(k < 7)
            def _():
                for copy in away(k + 1):
                    copy.wait_recv()
                for copy in pass_on(k + 1):
                    copy.start()

            @pl.when(k > 0)
            def _():
                gate_part(2 * chip + core).start()

            out_part[pl.ds(2 * chip, 2)] = dot(hg[at], wd[...]).astype(bf16).reshape(2, rows, width)
            return carry

        lax.fori_loop(0, 8, step, 0)
        mine = pltpu.make_async_copy(gparts.at[e], gback.at[e], psend.at[e])
        mine.start()
        rows_h.cross()

        def down_rows(i, carry):
            at = pl.ds(pl.multiple_of(i * 256, 256), 256)
            grads = dot(hg[:, at], up[...].reshape(16 * rows, width), TN).astype(bf16)
            cols = pl.ds(pl.multiple_of((i // 2) * width, width), width)
            dparts[pl.ds(4 * lax.rem(i, 2), 4), :, cols] = grads.reshape(4, rows // 2, width)
            return carry

        lax.fori_loop(0, hid // 256, down_rows, 0)
        down.start()

        def input_rows(k, carry):
            at = pl.ds(pl.multiple_of(here.turn_from(k) * both, both), both)
            parts[k] = dot(dgu[at], wgu[...], NT).astype(bf16).reshape(2, rows, width)
            to_partner(k).start()

            @pl.when(k > 0)
            def _():
                finish(k - 1)

            return carry

        lax.fori_loop(0, 8, input_rows, 0)
        finish(jnp.int32(7))

        def weight_rows(i, carry):
            at = pl.ds(pl.multiple_of(i * 256, 256), 256)
            columns = xs[:, :, at].reshape(16 * rows, 256)
            grads = dot(columns, dgu[...], TN).astype(bf16)
            dwgu[pl.ds(2 * i, 2)] = grads.reshape(2, rows, 2 * hid)
            return carry

        lax.fori_loop(0, width // 256, weight_rows, 0)

        def collect(k, carry):
            to_chip(k).wait_recv()
            total[...] += far[k].astype(f32)
            return carry

        lax.fori_loop(1, 8, collect, 0)
        down.cross()
        for copy in first:
            copy.wait_send()
        mine.wait()
        rows_h.wait()

        def drain(k, carry):
            for copy in away(k) + pass_on(k) + [to_partner(k), to_chip(k)]:
                copy.wait_send()
            return carry

        lax.fori_loop(1, 8, drain, 0)
        to_partner(0).wait_send()

        def drain_gates(k, carry):
            j = lax.rem(e + k, N_EXP)
            gate_part(j).wait_send()
            remote(gparts.at[j], gback.at[j], psend.at[j], precv.at[j], {"exp": j}).wait_recv()
            return carry

        lax.fori_loop(1, N_EXP, drain_gates, 0)
        down.wait()

    block = (8, rows, width)
    return pl.pallas_call(
        kernel,
        out_shape=[
            shape((16, rows, width), bf16),
            shape((rows, width), f32),
            shape((16, 8, rows), f32),
            shape((8, rows, 2 * hid), bf16),
            shape((rows // 2, 2 * width), f32),
            shape((8,) + h_one.shape, bf16),
        ],
        in_specs=[ANY] * 6,
        out_specs=[VMEM, VMEM, ANY, VMEM, VMEM, HBM],
        scratch_shapes=[
            pltpu.VMEM((8, rows // 2, 2 * width), bf16),
            *AxisScatter.scratch(shape((8, rows // 2, 2 * width), bf16)),
            pltpu.VMEM((16, rows, width), bf16),
            pltpu.VMEM((16, 32, rows), f32),
            pltpu.VMEM((16, rows, width), bf16),
            pltpu.VMEM((width, 2 * hid), bf16),
            pltpu.VMEM((hid, width), bf16),
            DMA,
            DMA((17,)),
            pltpu.VMEM((8, 2, rows, width), bf16),
            pltpu.VMEM(block, bf16),
            pltpu.VMEM(block, bf16),
            pltpu.VMEM(block, bf16),
            pltpu.VMEM((16 * rows, hid), bf16),
            pltpu.VMEM((16 * rows, 2 * hid), bf16),
            pltpu.VMEM((16, 8, rows), f32),
        ]
        + [DMA((8,))] * 14
        + sem_shapes(AxisScatter)
        + [DMA((16,))] * 2,
        compiler_params=pltpu.CompilerParams(collective_id=3, has_side_effects=True, vmem_limit_bytes=60 * 2**20),
    )(routed, gates, up_all, wgu_all, wd_all, h_one)


SCALE = HEAD_SIZE ** (-0.5)
QROWS = 256
SPAN = 64
SMEM = pl.BlockSpec(memory_space=pltpu.SMEM)


def left_lanes(shape_):
    return lax.broadcasted_iota(jnp.int32, shape_, 1) % 128 < HEAD_SIZE


def split_heads(kv):
    wide = kv.astype(f32)
    turned = pltpu.roll(wide, HEAD_SIZE, 1)
    left = left_lanes(kv.shape)
    return [
        jnp.where(left, wide, 0.0).astype(bf16),
        jnp.where(left, 0.0, turned).astype(bf16),
        jnp.where(left, turned, 0.0).astype(bf16),
        jnp.where(left, 0.0, wide).astype(bf16),
    ]


def place_column(spans, first, count):
    row = lax.broadcasted_iota(jnp.int32, (count, 1), 0)
    base = jnp.zeros((count, 1), jnp.int32)
    for i in range(count // SPAN):
        base = jnp.where(row // SPAN == i, spans[first + i], base)
    return base * SPAN + row % SPAN


def place_row(spans):
    lane = lax.broadcasted_iota(jnp.int32, (1, 16 * SPAN), 1)
    base = jnp.zeros((1, 16 * SPAN), jnp.int32)
    for i in range(16):
        base = jnp.where(lane // SPAN == i, spans[i], base)
    return base * SPAN + lane % SPAN


def tables(places, freqs):
    turned = places.astype(f32) * freqs
    return jnp.cos(turned), jnp.sin(turned)


def probs_of(q, k, visible):
    scores = jnp.where(visible, dot(q, k, NT) * SCALE, neg_big)
    shifted = jnp.exp(scores - jnp.max(scores, axis=-1, keepdims=True))
    return shifted * (1.0 / jnp.sum(shifted, axis=-1, keepdims=True))


def swap_of(v):
    leading = lax.broadcasted_iota(jnp.int32, v.shape, 1) % HEAD_SIZE < HALF
    return jnp.where(leading, -pltpu.roll(v, v.shape[1] - HALF, 1), pltpu.roll(v, HALF, 1))


def front(tokens, w_query, key_matrix, value_matrix, gains, router, w_out, cot, w_gate, w_up, w_down, freqs, spans):
    rows, width = tokens.shape
    own = w_query.shape[0]
    f = w_gate.shape[2]
    count = N_CTX * rows

    def kernel(
        x, wq, wk, wv, gn, ro, wo, u, wg, wup, wdn, fr, so,
        out, kept, h_out, gain_out, w_out_, ros, wos, us, wgus, wds,
        own_w, own_wgu, own_wd, own_gain, w, gs, h, stage, seq, heads, attn, lsem,
        send, recv, osend, orecv, ksem, *sems,
    ):
        here = Here()
        c = here.c
        loads = []
        for i in range(2):
            loads.append(pltpu.make_async_copy(wg.at[i], own_wgu.at[:, pl.ds(f * i, f)], lsem.at[3 * i]))
            loads.append(pltpu.make_async_copy(wup.at[i], own_wgu.at[:, pl.ds(f * (2 + i), f)], lsem.at[3 * i + 1]))
            loads.append(pltpu.make_async_copy(wdn.at[i], own_wd.at[:, pl.ds(width * i, width)], lsem.at[3 * i + 2]))
        for load in loads:
            load.start()
        left = left_lanes((own, 128))
        for i in range(N_CTX // 2):
            at = slice(128 * i, 128 * (i + 1))
            keys, vals = wk[:, at].astype(f32), wv[:, at].astype(f32)
            one = jnp.where(left, keys, pltpu.roll(vals, HEAD_SIZE, 1))
            two = jnp.where(left, pltpu.roll(keys, HEAD_SIZE, 1), vals)
            for j, kv in ((2 * i, one), (2 * i + 1, two)):
                own_w[:, 256 * j : 256 * j + 128] = wq[:, 128 * j : 128 * (j + 1)]
                own_w[:, 256 * j + 128 : 256 * (j + 1)] = kv.astype(bf16)
        half = gn[...].astype(f32)
        odd = here.core == 1
        lane = lax.broadcasted_iota(jnp.int32, half.shape, 1)
        own_gain[...] = jnp.where(odd, jnp.where(lane < 64, 0.0, pltpu.roll(half, 64, 1)), jnp.where(lane < 64, half, 0.0))
        greet(here.ctx_peers() + here.exp_peers())
        gain_all = PairGather(here, own_gain, gs, *sems[0:4])
        w_all = PairGather(here, own_w, w, *sems[4:8])
        ro_all = PairGather(here, ro, ros, *sems[8:12])
        wo_all = PairGather(here, wo, wos, *sems[12:16])
        cots = PairGather(here, u, us, *sems[16:20])
        firsts = AxisGather(here, own_wgu, wgus, *sems[20:22])
        downs = AxisGather(here, own_wd, wds, *sems[22:24])
        gain_all.start()
        w_all.start()
        for load in loads:
            load.wait()
        firsts.start()
        cos, sin = tables(place_column(so, 2 * c, rows), fr[...])
        pr = place_row(so)
        gain_all.cross()
        w_all.cross()
        for item in (wo_all, ro_all, cots):
            item.start()
        firsts.cross()
        downs.start()
        gain_all.pass_on()
        gain_all.wait()
        for i in range(8):
            pair = gs[2 * i] + gs[2 * i + 1]
            gain_out[:, 128 * i : 128 * (i + 1)] = pair
        values = x[...].astype(f32)
        h[...] = (values * factor_of(values) * gain_out[0:1, :]).astype(bf16)
        keep_h = pltpu.make_async_copy(h, h_out, ksem.at[1])
        keep_h.start()
        w_all.pass_on()
        w_all.wait()
        keep_w = pltpu.make_async_copy(w, w_out_, ksem.at[2])
        keep_w.start()

        def block_rows(ref, j):
            return ref.at[pl.ds(pl.multiple_of(j * rows, rows), rows)]

        def column(j):
            return out.at[:, pl.ds(pl.multiple_of(j * 128, 128), 128)]

        def arrive(j):
            return remote(stage.at[j], block_rows(seq, c), send.at[j], recv.at[c], {"ctx": j})

        def arrive_own():
            return pltpu.make_async_copy(stage.at[c], block_rows(seq, c), send.at[c])

        def project(b, carry):
            j = lax.rem(c + 1 + b, N_CTX)
            at = pl.ds(pl.multiple_of(j * 256, 256), 256)
            p = dot(h[...], w[:, :, at].reshape(width, 256))
            stage[j] = (p * cos + swap_of(p) * sin).astype(bf16)

            @pl.when(b < N_CTX - 1)
            def _():
                arrive(j).start()

            return carry

        lax.fori_loop(0, N_CTX, project, 0)
        arrive_own().start()
        for item in (wo_all, ro_all, cots):
            item.cross()
        arrive_own().wait()
        for k in range(1, N_CTX):
            j = here.ctx(k)
            arrive(j).wait_send()
            remote(stage.at[j], block_rows(seq, j), send.at[j], recv.at[j], {"ctx": j}).wait_recv()
        downs.cross()
        keep = pltpu.make_async_copy(seq, kept, ksem.at[0])
        keep.start()
        for i, part in enumerate(split_heads(seq[:, 128:])):
            heads[i] = part

        def leave(j):
            return remote(block_rows(attn, j), column(c), osend.at[j], orecv.at[c], {"ctx": j})

        def local():
            return pltpu.make_async_copy(block_rows(attn, c), column(c), osend.at[c])

        def step(b, carry):
            block = lax.rem(b + c // 2, count // QROWS)
            at = pl.ds(pl.multiple_of(block * QROWS, QROWS), QROWS)
            visible = pr <= place_column(so, block * (QROWS // SPAN), QROWS)
            q = seq[at, :128]
            total = jnp.zeros((QROWS, 128), f32)
            for i in range(2):
                total += dot(probs_of(q, heads[i], visible).astype(bf16), heads[2 + i])
            attn[at] = total.astype(bf16)
            for i in range(QROWS // rows):
                j = block * (QROWS // rows) + i

                @pl.when(j != c)
                def _():
                    leave(j).start()

                @pl.when(j == c)
                def _():
                    local().start()

            return carry

        lax.fori_loop(0, count // QROWS, step, 0)
        for item in (wo_all, ro_all, cots):
            item.pass_on()
        for k in range(1, N_CTX):
            j = here.ctx(k)
            leave(j).wait_send()
            remote(block_rows(attn, c), column(j), osend.at[j], orecv.at[j], {"ctx": j}).wait_recv()
        local().wait()
        for item in (keep, keep_h, keep_w, wo_all, ro_all, cots, firsts, downs):
            item.wait()

    return pl.pallas_call(
        kernel,
        out_shape=[
            shape((rows, N_CTX * 128), bf16),
            shape((count, 256), bf16),
            shape((rows, width), bf16),
            shape((8, width), f32),
            shape((16, own, N_CTX * 256), bf16),
            shape((16,) + router.shape, bf16),
            shape((16,) + w_out.shape, bf16),
            shape((16,) + cot.shape, bf16),
            shape((8, rows, 4 * f), bf16),
            shape((8, w_down.shape[1], 2 * width), bf16),
        ],
        in_specs=[VMEM] * 5 + [ANY] * 6 + [VMEM, SMEM],
        out_specs=[HBM] * 3 + [VMEM] + [HBM] * 6,
        scratch_shapes=[
            pltpu.VMEM((own, N_CTX * 256), bf16),
            pltpu.VMEM((rows, 4 * f), bf16),
            pltpu.VMEM((w_down.shape[1], 2 * width), bf16),
            pltpu.VMEM((8, 128), f32),
            pltpu.VMEM((16, own, N_CTX * 256), bf16),
            pltpu.VMEM((16, 8, 128), f32),
            pltpu.VMEM((rows, width), bf16),
            pltpu.VMEM((N_CTX, rows, 256), bf16),
            pltpu.VMEM((count, 256), bf16),
            pltpu.VMEM((4, count, 128), bf16),
            pltpu.VMEM((count, 128), bf16),
            DMA((6,)),
        ]
        + [DMA((8,))] * 4
        + [DMA((3,))]
        + sem_shapes(*[PairGather] * 5, AxisGather, AxisGather),
        compiler_params=params(2),
    )(tokens, w_query, key_matrix, value_matrix, gains, router, w_out, cot, w_gate, w_up, w_down, freqs, spans)


def attend_back(
    grad_routed, gate_back, gates, routed, pack, x_mid, gain, cot, attn_low, wo_full, seq_qkv, freqs, spans, h_all, out_part,
    first_part,
):
    rows, width = grad_routed.shape
    count = N_CTX * rows
    own = width // N_EXP
    scatters = [
        out_part,
        jax.ShapeDtypeStruct((16, own, width), bf16),
        jax.ShapeDtypeStruct((16, own, 384), bf16),
    ]

    def kernel(
        gr, gb, gt, ri, pk, xm, gn, u, al, wof, seq, fr, so, hh, op, dp, mid, back, moe, wos, alls, dwgu, h, hsem,
        low_w, low, wo_total, total, payload, wp, ga, grads, heads, acc, dqkv, cos, sin, *rest,
    ):
        here = Here()
        load = pltpu.make_async_copy(hh, h, hsem)
        load.start()
        greet(here.ctx_peers() + here.exp_peers())
        bufs, sems = rest[:15], rest[15:]
        first = AxisScatter(here, dp, dwgu, *bufs[12:15], *sems[23:26])
        arrive = Columns(here, ga, grads, *sems[0:2])
        outs = PairScatter(here, op, moe, *bufs[0:4], *sems[2:7])
        wo = PairScatter(here, wp, wo_total, *bufs[4:8], *sems[7:12])
        proj = PairScatter(here, payload, total, *bufs[8:12], *sems[12:17])
        turn = Turn(here, dqkv, back, *sems[17:19])
        wo_rows = Gather(here, low_w, wos, *sems[19:21])
        all_rows = Gather(here, low, alls, *sems[21:23])
        outs.start()
        spot = lax.broadcasted_iota(jnp.int32, (16 * 8, 128), 0)
        lane = lax.broadcasted_iota(jnp.int32, (16 * 8, 128), 1)
        picks = jnp.where(jnp.logical_and(spot % 8 < 2, spot // 8 * 2 + spot % 8 == lane), 1.0, 0.0)
        exact = functools.partial(
            lax.dot_general, dimension_numbers=(TN, ((), ())), precision=lax.Precision.HIGHEST, preferred_element_type=f32
        )
        grad_gates = exact(gb[...].reshape(16 * 8, rows), picks)
        weighted = gt[...] * grad_gates
        grad_logits = (weighted - gt[...] * jnp.sum(weighted, axis=-1, keepdims=True)).astype(bf16)
        routed_grad = gr[...] + dot(grad_logits, pk[...], NT)
        values = xm[...]
        factor = factor_of(values)
        grad_mid = u[...].astype(f32) + normalize_back(values, factor, gn[...], routed_grad)
        mid[...] = grad_mid
        branch = grad_mid.astype(bf16)
        ga[...] = dot(branch, wof[...], NT).astype(bf16)
        arrive.start()
        first.start()
        wp[...] = dot(al[...], branch, TN).astype(bf16).reshape(16, own, width)
        wo.start()
        column = (lax.broadcasted_iota(jnp.int32, (rows, 128), 1) == 32).astype(f32)
        small = dot(ri[...], grad_logits, TN) + exact(routed_grad * values * factor, column)
        payload[:, :, 256:] = small.astype(bf16).reshape(16, own, 128)
        pr = place_row(so)
        cos[...], sin[...] = tables(place_column(so, 0, count), fr[...])
        for i, part in enumerate(split_heads(seq[:, 128:])):
            heads[i] = part
        acc[...] = jnp.zeros_like(acc)
        arrive.wait()
        wo.pass_on()
        outs.pass_on()

        def step(b, carry):
            at = pl.ds(pl.multiple_of(b * QROWS, QROWS), QROWS)
            visible = pr <= place_column(so, b * (QROWS // SPAN), QROWS)
            q, g = seq[at, :128], grads[at]
            dq = jnp.zeros((QROWS, 128), f32)
            for i in range(2):
                probs = probs_of(q, heads[i], visible)
                grad_probs = dot(g, heads[2 + i], NT)
                inner = jnp.sum(probs * grad_probs, axis=-1, keepdims=True)
                grad_scores = (probs * (grad_probs - inner)).astype(bf16)
                dq += dot(grad_scores, heads[i])
                acc[i] += dot(grad_scores, q, TN)
                acc[2 + i] += dot(probs.astype(bf16), g, TN)
            dq = dq * SCALE
            dqkv[at, :128] = (dq * cos[at] - swap_of(dq * sin[at])).astype(bf16)
            return carry

        lax.fori_loop(0, count // QROWS, step, 0)
        left = left_lanes((count, 128))
        dk = (acc[0] + pltpu.roll(acc[1], HEAD_SIZE, 1)) * SCALE
        dv = pltpu.roll(acc[2], HEAD_SIZE, 1) + acc[3]
        dk = dk * cos[...] - swap_of(dk * sin[...])
        dqkv[:, 128:] = jnp.where(left, dk, dv).astype(bf16)
        turn.start()
        load.wait()
        payload[:, :, :256] = dot(h[...], dqkv[...], TN).astype(bf16).reshape(16, own, 256)
        proj.start()
        wo.cross()
        proj.pass_on()
        wo.wait()
        low_w[...] = wo_total[...].astype(bf16)
        wo_rows.start()
        proj.cross()
        outs.cross()
        proj.wait()
        low[...] = total[...].astype(bf16)
        all_rows.start()
        first.cross()
        outs.wait()
        turn.wait()
        wo_rows.wait()
        all_rows.wait()
        first.wait()

    return pl.pallas_call(
        kernel,
        out_shape=[
            shape((rows, width), f32),
            shape((rows, N_CTX * 256), bf16),
            shape((rows, width), f32),
            shape((8, own, width), bf16),
            shape((8, own, 384), bf16),
            shape(first_part.shape[1:], f32),
        ],
        in_specs=[VMEM] * 12 + [SMEM, ANY, ANY, ANY],
        out_specs=[VMEM, HBM, VMEM, HBM, HBM, VMEM],
        scratch_shapes=[
            pltpu.VMEM(h_all.shape, bf16),
            DMA,
            pltpu.VMEM((own, width), bf16),
            pltpu.VMEM((own, 384), bf16),
            pltpu.VMEM((own, width), f32),
            pltpu.VMEM((own, 384), f32),
            pltpu.VMEM((16, own, 384), bf16),
            pltpu.VMEM((16, own, width), bf16),
            pltpu.VMEM((rows, width), bf16),
            pltpu.VMEM((count, 128), bf16),
            pltpu.VMEM((4, count, 128), bf16),
            pltpu.VMEM((4, count, 128), f32),
            pltpu.VMEM((count, 256), bf16),
            pltpu.VMEM((count, 128), f32),
            pltpu.VMEM((count, 128), f32),
        ]
        + [b for x in scatters for b in PairScatter.scratch(x)]
        + AxisScatter.scratch(first_part)
        + sem_shapes(Columns, PairScatter, PairScatter, PairScatter, Turn, Gather, Gather, AxisScatter),
        compiler_params=pltpu.CompilerParams(collective_id=4, has_side_effects=True, vmem_limit_bytes=60 * 2**20),
    )(
        grad_routed, gate_back, gates, routed, pack, x_mid, gain, cot, attn_low, wo_full, seq_qkv, freqs, spans, h_all,
        out_part, first_part,
    )


def finish_tokens(
    back, wqkv, tokens, gain, grad_mid, x_mid, moe_out, owned, wo_sums, w_query, key_matrix, value_matrix, norm_attn,
    grad_first, grad_down,
):
    rows, width = tokens.shape
    own = w_query.shape[0]
    f = grad_first.shape[1] // 4
    args = (
        back, wqkv, tokens, gain, grad_mid, x_mid, moe_out, owned, wo_sums, w_query, key_matrix, value_matrix,
        norm_attn[None, :], grad_first, grad_down,
    )

    def kernel(*refs):
        n = len(args)
        ins, (result, grad, gq, gk, gv, go, tail, gm, ga, gg, gu, gd) = refs[:n], refs[n : n + 12]
        held, sems = refs[n + 12 : -1], refs[-1]
        loads = [pltpu.make_async_copy(a, b, sems.at[i]) for i, (a, b) in enumerate(zip(ins, held))]
        for load in loads:
            load.start()
        for load in loads:
            load.wait()
        back, wqkv, x, gain, mid, xm, moe, owned, wos, wq, wk, wv, norm, first, down = held
        for i in range(2):
            gg[i] = first[:, f * i : f * (i + 1)]
            gu[i] = first[:, f * (2 + i) : f * (3 + i)]
            gd[i] = down[:, 2 * f * i : 2 * f * (i + 1)]
        result[...] = (xm[...] + moe[...]).astype(bf16)
        values = x[...].astype(f32)
        factor = factor_of(values)
        grad[...] = mid[...] + normalize_back(values, factor, gain[...], dot(back[...], wqkv[...], NT))
        left = left_lanes((own, 128))
        rest = jnp.zeros((own, 128), f32)
        sums = jnp.zeros((own, 128), f32)
        for i in range(N_CTX):
            block = owned[i, :, :128].astype(f32)
            at = slice(128 * i, 128 * (i + 1))
            gq[:, at] = block
            sums += block * wq[:, at].astype(f32)
            rest += owned[i, :, 256:].astype(f32)
        for i in range(N_CTX // 2):
            one, two = owned[2 * i, :, 128:256].astype(f32), owned[2 * i + 1, :, 128:256].astype(f32)
            at = slice(128 * i, 128 * (i + 1))
            keys = jnp.where(left, one, pltpu.roll(two, HEAD_SIZE, 1))
            vals = jnp.where(left, pltpu.roll(one, HEAD_SIZE, 1), two)
            gk[:, at] = keys
            gv[:, at] = vals
            sums += keys * wk[:, at].astype(f32) + vals * wv[:, at].astype(f32)
        turned = jnp.transpose(rest)
        tail[...] = turned[:32]
        gm[...] = turned[32:33]
        ga[...] = jnp.sum(jnp.transpose(sums), axis=0, keepdims=True) / norm[...].astype(f32)
        total = wos[0].astype(f32)
        for i in range(1, N_CTX):
            total += wos[i].astype(f32)
        go[...] = total

    return pl.pallas_call(
        kernel,
        out_shape=[
            shape((rows, width), bf16),
            shape((rows, width), f32),
            shape((own, width), f32),
            shape((own, width // 2), f32),
            shape((own, width // 2), f32),
            shape((own, width), f32),
            shape((32, own), f32),
            shape((1, own), f32),
            shape((1, own), f32),
            shape((2, rows, f), f32),
            shape((2, rows, f), f32),
            shape((2, rows // 2, 2 * f), f32),
        ],
        in_specs=[ANY] * len(args),
        out_specs=[VMEM] * 12,
        scratch_shapes=[pltpu.VMEM(a.shape, a.dtype) for a in args] + [DMA((len(args),))],
        compiler_params=pltpu.CompilerParams(vmem_limit_bytes=60 * 2**20),
    )(*args)


def body(
    tokens, cotangent, span_order, expert_choice, norm_attn, w_query, key_matrix, value_matrix,
    w_out, norm_moe, w_router, w_gate, w_up, w_down,
):
    tokens, cotangent, choice = tokens[0], cotangent[0], expert_choice[0]
    rows, width = tokens.shape
    pack = jnp.pad(w_router, ((0, 0), (0, 128 - 32)))
    gains = jnp.pad(jnp.stack([norm_attn, norm_moe]), ((0, 6), (0, 64)))
    lanes = jnp.arange(256, dtype=jnp.int32)
    freqs = rope_base ** (-((lanes % HALF).astype(f32) * 2.0 / HEAD_SIZE))
    freqs = jnp.where(lanes < 192, freqs, 0.0)[None, :]
    attn_low, seq_qkv, h_one, gains, wqkv, pack_all, wo, up_all, wgu_all, wd_all = front(
        tokens, w_query, key_matrix, value_matrix, gains, pack, w_out, cotangent, w_gate, w_up, w_down, freqs, span_order
    )
    gain_a, gain_m = gains[0:1], gains[1:2]
    wgu_all = wgu_all.reshape(width, 4 * w_gate.shape[2])
    wqkv = wqkv.reshape(width, N_CTX * 256)
    pack_all = pack_all.reshape(width, 128)
    wo = wo.reshape(width, width)
    inputs = tokens.astype(f32)
    x_mid = inputs + dot(attn_low, wo)
    routed_in = (x_mid * factor_of(x_mid) * gain_m).astype(bf16)
    logits = dot(routed_in, pack_all)
    expert_ids = jnp.arange(128, dtype=jnp.int32)
    chosen = jnp.any(choice[:, :, None] == expert_ids[None, None, :], axis=1)
    masked = jnp.where(chosen, logits, neg_big)
    lifted = jnp.where(chosen, jnp.exp(masked - jnp.max(masked, axis=-1, keepdims=True)), 0.0)
    gates = lifted / jnp.sum(lifted, axis=-1, keepdims=True)
    out_part, grad_routed, gate_back, grad_wgu, grad_wd, h_all = experts(
        routed_in, gates[:, :32].T, up_all, wgu_all, wd_all, h_one
    )
    h_all = h_all.reshape(N_CTX * rows, width)
    grad_mid, back, moe_out, wo_sums, owned, grad_first = attend_back(
        grad_routed, gate_back, gates, routed_in, pack_all, x_mid, gain_m, cotangent, attn_low, wo, seq_qkv,
        freqs[:, :128], span_order, h_all, out_part, grad_wgu,
    )
    result, grad_tokens, out_wq, out_wk, out_wv, out_wo, tail, out_gain_m, out_gain_a, out_wg, out_wu, out_wd = finish_tokens(
        back, wqkv, tokens, gain_a, grad_mid, x_mid, moe_out, owned, wo_sums, w_query, key_matrix, value_matrix, norm_attn,
        grad_first, grad_wd,
    )
    return (
        result[None],
        grad_tokens[None],
        out_gain_a[0],
        out_wq,
        out_wk,
        out_wv,
        out_wo,
        out_gain_m[0],
        tail.T,
        out_wg,
        out_wu,
        out_wd,
    )


def solution(mesh):
    return jax.shard_map(
        body,
        mesh=mesh,
        in_specs=(
            P("exp", "ctx", None),
            P("exp", "ctx", None),
            P(),
            P("exp", "ctx", None),
            P("exp"),
            P("exp", None),
            P("exp", None),
            P("exp", None),
            P("exp", None),
            P("exp"),
            P("exp", None),
            P("exp", "ctx", None),
            P("exp", "ctx", None),
            P("exp", "ctx", None),
        ),
        out_specs=(
            P("exp", "ctx", None),
            P("exp", "ctx", None),
            P("exp"),
            P("exp", None),
            P("exp", None),
            P("exp", None),
            P("exp", None),
            P("exp"),
            P("exp", None),
            P("exp", "ctx", None),
            P("exp", "ctx", None),
            P("exp", "ctx", None),
        ),
        check_vma=False,
    )
```
